128 devices in a mesh: tile: 32 (over y, z_hi, x), band: 4 (over z_lo, core).
Axes of the slice: x: 4, y: 4, z: 4 (z_hi: 2, z_lo: 2; z = z_hi * 2 + z_lo), core: 2. Of those that a mesh axis runs over, the one named last changes fastest.
Arguments:
- source_cells: bfloat16 [131072, 256], P(('tile', 'band')), may hold values from -6 to 6
- regrid_weights: bfloat16 [16384, 16, 64], P(('tile', 'band')), may hold values from -0.5 to 0.5
- pair_target: int32 [16384, 1], P(('tile', 'band')), may hold values from 0 to 127; in each aligned block of 128 rows (0 to 127, 128 to 255, ...) at most 2 rows name the same one
- pair_block: int32 [16384], P(('tile', 'band')), may hold values from 0 to 63
- pair_source: int32 [16384], P(('tile', 'band')), may hold values from 0 to 15
- flip_codes: int32 [32], replicated, may hold values from 0 to 1
- kernel_one: bfloat16 [3, 3, 256, 256], replicated, may hold values from -0.125 to 0.125
- kernel_two: bfloat16 [3, 3, 256, 256], replicated, may hold values from -0.125 to 0.125
- out_grad: bfloat16 [32, 32, 128, 256], P('tile', 'band'), may hold values from -6 to 6
Outputs:
- mixed_out: bfloat16 [32, 32, 128, 256], P('tile', 'band')
- kernel_one_grad: float32 [3, 3, 256, 256], replicated
- kernel_two_grad: float32 [3, 3, 256, 256], replicated
- source_grad: bfloat16 [131072, 256], P(('tile', 'band'))
The draws below stay inside these ranges and needn't reach their ends.
Inputs may be any that keep to these rules, and one draw needn't show every extreme that they name: `pair_target`: within the 128 pairs of one device no target device is named more than 2 times, and some target device exactly 2 times.
All inputs are finite; a program needn't handle non-finite values.
Results may differ from the reference program's by a relative error of at most 0.0065.
Values may be sent and summed in bfloat16 or wider, within the bound.
A program may use at most 128 MiB of HBM per device.

```python
import math
import jax
import jax.numpy as jnp
import numpy as np
from jax import lax

C = 256
TW = 128
BT = 16
BL = 64
SB = 16
MAXP = 128
CAP = 2
TB = 64
H = 32
SRC = 131072
PAIRS = 16384
N_TILE = 32
DEVICES = 128


def set_ends(entries, stream_key, low, largest):
    longest = entries.shape.index(max(entries.shape))
    spots = []
    for shift in (0, 1):
        where = [jax.random.randint(jax.random.fold_in(stream_key, axis), (), 0, length) for axis, length in enumerate(entries.shape)]
        where[longest] = (where[longest] + shift) % entries.shape[longest]
        spots.append(tuple(where))
    return entries.at[spots[0]].set(low).at[spots[1]].set(largest)


def block_levels(rng, shape, split, least, top_value):
    factor_of = 1.0
    for axis_at, blocks in split:
        draws = jax.random.uniform(jax.random.fold_in(jax.random.fold_in(rng, 6), axis_at), (blocks,), jnp.float32, least / len(split), top_value / len(split))
        factor_of = factor_of * jnp.repeat(jnp.exp(draws), shape[axis_at] // blocks).reshape((-1,) + (1,) * (len(shape) - 1 - axis_at))
    return factor_of


def assign_block(own_key, own, number, rows, number_of, top, limit, lean):
    order = jax.random.permutation(own_key, number_of)
    crowded, usual = shares(number_of, rows * top, limit, lean, True), shares(number_of, rows * top, limit, lean, False)
    places = jnp.arange(number_of)

    def named(lengths, offset_by):
        used = int((lengths > 0).sum())
        fixed = max(1, used // 4)
        shifted = fixed + (places - fixed + offset_by * (used - fixed)) % max(1, number_of - fixed)
        return jnp.zeros((number_of,), jnp.int32).at[order[jnp.where(places < fixed, places, shifted)]].set(jnp.asarray(lengths, jnp.int32))

    lengths = jnp.where(number % 4 == 0, named(crowded, number // 4), named(usual, number - number // 4 - 1))
    mixed = jax.random.permutation(jax.random.fold_in(own, 3), number_of)
    donor, sink = mixed[0:number_of // 2 * 2:2], mixed[1:number_of // 2 * 2:2]
    margin = jnp.minimum(lengths[donor] - 1, limit - lengths[sink]) // 2
    margin = jnp.where((donor == order[0]) | (sink == order[0]) | (lengths[sink] == 0), 0, jnp.maximum(margin, 0))
    shifted = jax.random.randint(jax.random.fold_in(own, 4), (number_of // 2,), 0, 1 << 20) % (margin + 1)
    lengths = lengths.at[donor].add(-shifted).at[sink].add(shifted)
    items = jnp.searchsorted(jnp.cumsum(lengths), jnp.arange(rows * top), side="right").astype(jnp.int32)
    grid = items.reshape(top, rows).T
    grid = grid[jax.random.permutation(jax.random.fold_in(own, 1), rows)]
    offset_by = jax.random.randint(jax.random.fold_in(own, 2), (rows, 1), 0, top)
    return jnp.take_along_axis(grid, (jnp.arange(top)[None, :] + offset_by) % top, axis=1)


def shares(amount, total, bound, lean, full):
    weights = [(1 << 20) // math.isqrt(rank ** lean) + 1 for rank in range(1, amount + 1)]
    largest = bound if full else min(bound, max(-(-total // amount), total * weights[0] // sum(weights)))
    least = 1 if total - largest >= amount - 1 else 0
    counts, spare = [largest] + [least] * (amount - 1), total - largest - least * (amount - 1)
    while spare > 0:
        movable = [i for i in range(1, amount) if counts[i] < largest] or [i for i in range(1, amount) if counts[i] < bound]
        whole, remaining = sum([weights[i] for i in movable]), spare
        for i in movable:
            addition = min(bound - counts[i], max(1, remaining * weights[i] // whole), spare)
            counts[i] = counts[i] + addition
            spare = spare - addition
    return np.array(counts)


def bell_draw(rng, shape, spread, reach, cuts=(), held_as=jnp.bfloat16):
    result = jax.random.normal(rng, shape, jnp.float32) * spread
    if len(cuts) > 0:
        result = block_levels(rng, shape, cuts, -0.22, 0.18) * result
    return jnp.clip(result, min=-reach, max=reach).astype(held_as)


def setup_inputs(seed: int = 0) -> dict:
    streams_of = jax.random.split(jax.random.key(seed), 10)
    source_cells = bell_draw(streams_of[0], (SRC, C), 1.0, 6.0, ((0, 128),))
    regrid_weights = bell_draw(streams_of[1], (PAIRS, BT, BL), (2 * BL) ** -0.5, 0.5, ((0, 128),))
    pair_target_keys = jax.random.split(jax.random.fold_in(streams_of[2], 1), PAIRS // MAXP)
    pair_target_turns = jax.random.permutation(jax.random.fold_in(streams_of[2], 3), PAIRS // MAXP)
    pair_target = jax.vmap(lambda own, number: assign_block(jax.random.fold_in(streams_of[2], 2), own, number, MAXP, DEVICES, 1, CAP, 2))(pair_target_keys, pair_target_turns).reshape((PAIRS, 1))
    pair_block = set_ends(jax.random.randint(streams_of[3], (PAIRS,), 0, TB), jax.random.fold_in(streams_of[3], 1), 0, TB - 1).astype(jnp.int32)
    pair_source = set_ends(jax.random.randint(streams_of[4], (PAIRS,), 0, SB), jax.random.fold_in(streams_of[4], 1), 0, SB - 1).astype(jnp.int32)
    flip_codes = set_ends(jax.random.randint(streams_of[5], (N_TILE,), 0, 2), jax.random.fold_in(streams_of[5], 1), 0, 1).astype(jnp.int32)
    kernel_one = bell_draw(streams_of[6], (3, 3, C, C), (9 * C) ** -0.5, 0.125)
    kernel_two = bell_draw(streams_of[7], (3, 3, C, C), (9 * C) ** -0.5, 0.125)
    out_grad = bell_draw(streams_of[8], (N_TILE, H, TW, C), 1.0, 6.0, ((0, 32), (1, 4)))
    return {"source_cells": source_cells, "regrid_weights": regrid_weights, "pair_target": pair_target, "pair_block": pair_block, "pair_source": pair_source, "flip_codes": flip_codes, "kernel_one": kernel_one, "kernel_two": kernel_two, "out_grad": out_grad}


HIGHEST_PREC = lax.Precision.HIGHEST

def sides_all(grid_in, flip_codes, rim_width):
    column_count = grid_in.shape[2]
    left_part = grid_in[:, :, :rim_width]
    right_part = grid_in[:, :, column_count - rim_width:][:, :, ::-1]
    flip_mask = (flip_codes == 1)[:, None, None, None]
    return (jnp.where(flip_mask, left_part, right_part), jnp.where(flip_mask, right_part, left_part))

def extend_all(grid_in, flip_codes, rim_width):
    to_next, to_prev = sides_all(grid_in, flip_codes, rim_width)
    from_prev = jnp.roll(to_next, 1, axis=0)
    from_next = jnp.roll(to_prev, -1, axis=0)
    keep_mask = (flip_codes == 0)[:, None, None, None]
    left_src = jnp.where(keep_mask, from_prev, from_next)
    right_src = jnp.where(keep_mask, from_next, from_prev)
    widened = jnp.concatenate([left_src[:, :, ::-1], grid_in, right_src], axis=2)
    return jnp.pad(widened, ((0, 0), (rim_width, rim_width), (0, 0), (0, 0)))

def conv_all(extended, kernel, dilation):
    rows_out = extended.shape[1] - 2 * dilation
    cols_out = extended.shape[2] - 2 * dilation
    summed = jnp.zeros((extended.shape[0] * rows_out * cols_out, kernel.shape[3]), jnp.float32)
    for row_tap in range(3):
        for col_tap in range(3):
            window = extended[:, dilation * row_tap:dilation * row_tap + rows_out, dilation * col_tap:dilation * col_tap + cols_out]
            summed = summed + jnp.dot(window.reshape(-1, extended.shape[3]), kernel[row_tap, col_tap], preferred_element_type=jnp.float32, precision=HIGHEST_PREC)
    return summed.reshape(extended.shape[0], rows_out, cols_out, kernel.shape[3])

def kernel_grad_all(extended, grad_in, dilation):
    rows_out = grad_in.shape[1]
    cols_out = grad_in.shape[2]
    flat_grads = grad_in.reshape(-1, grad_in.shape[3])
    pieces = []
    for row_tap in range(3):
        for col_tap in range(3):
            window = extended[:, dilation * row_tap:dilation * row_tap + rows_out, dilation * col_tap:dilation * col_tap + cols_out]
            pieces.append(lax.dot_general(window.reshape(-1, extended.shape[3]), flat_grads, (((0,), (0,)), ((), ())), preferred_element_type=jnp.float32, precision=HIGHEST_PREC))
    return jnp.stack(pieces).reshape(3, 3, extended.shape[3], grad_in.shape[3])

def input_adjoint(kernel, flip_codes, dilation, cotangent):

    def linear_part(grid_in):
        return conv_all(extend_all(grid_in, flip_codes, dilation), kernel.astype(jnp.float32), dilation)
    unused, pullback = jax.vjp(linear_part, jnp.zeros_like(cotangent))
    return pullback(cotangent)[0]

def reference(source_cells, regrid_weights, pair_target, pair_block, pair_source, flip_codes, kernel_one, kernel_two, out_grad):
    slabs = source_cells.reshape(DEVICES, SB, BL, C)
    weights_dev = regrid_weights.reshape(DEVICES, MAXP, BT, BL)
    target_dev = pair_target.reshape(DEVICES, MAXP)
    block_dev = pair_block.reshape(DEVICES, MAXP)
    source_dev = pair_source.reshape(DEVICES, MAXP)

    def add_device(carry, inputs):
        slab, weights, targets, blocks, sources = inputs
        picked = slab[sources].astype(jnp.float32)
        contrib = jnp.einsum('pbl,plc->pbc', weights.astype(jnp.float32), picked, precision=HIGHEST_PREC).astype(jnp.bfloat16)
        return (carry.at[targets * TB + blocks].add(contrib.astype(jnp.float32)), None)
    regrid_sum, unused = lax.scan(add_device, jnp.zeros((DEVICES * TB, BT, C), jnp.float32), (slabs, weights_dev, target_dev, block_dev, source_dev))
    regridded = regrid_sum.astype(jnp.bfloat16).reshape(N_TILE, H, TW, C)
    ext_one = extend_all(regridded, flip_codes, 1)
    pre_act = conv_all(ext_one, kernel_one, 1)
    hidden = jax.nn.silu(pre_act).astype(jnp.bfloat16)
    ext_two = extend_all(hidden, flip_codes, 2)
    mixed_out = (regridded.astype(jnp.float32) + conv_all(ext_two, kernel_two, 2)).astype(jnp.bfloat16)
    kernel_two_grad = kernel_grad_all(ext_two, out_grad, 2)
    hidden_grad = input_adjoint(kernel_two, flip_codes, 2, out_grad.astype(jnp.float32))
    sigmoid_act = jax.nn.sigmoid(pre_act)
    pre_grad = (hidden_grad * sigmoid_act * (1.0 + pre_act * (1.0 - sigmoid_act))).astype(jnp.bfloat16)
    kernel_one_grad = kernel_grad_all(ext_one, pre_grad, 1)
    input_grad = (out_grad.astype(jnp.float32) + input_adjoint(kernel_one, flip_codes, 1, pre_grad.astype(jnp.float32))).astype(jnp.bfloat16)
    grad_blocks = input_grad.reshape(DEVICES * TB, BT, C)

    def device_grad(inputs):
        weights, targets, blocks, sources = inputs
        pair_grad = grad_blocks[targets * TB + blocks].astype(jnp.float32)
        backed = jnp.einsum('pbl,pbc->plc', weights.astype(jnp.float32), pair_grad, precision=HIGHEST_PREC)
        return jax.ops.segment_sum(backed, sources, num_segments=SB).astype(jnp.bfloat16)
    source_grad = lax.map(device_grad, (weights_dev, target_dev, block_dev, source_dev)).reshape(DEVICES * SB * BL, C)
    return (mixed_out, kernel_one_grad, kernel_two_grad, source_grad)
```

```python
import jax
import jax.numpy as jnp
from jax import lax
from jax.experimental import pallas as pl
from jax.experimental.pallas import tpu as pltpu
from jax.sharding import PartitionSpec as P

F32 = jnp.float32
BF16 = jnp.bfloat16
MESH = pl.DeviceIdType.MESH
VM = pl.BlockSpec(memory_space=pltpu.VMEM)
SM = pl.BlockSpec(memory_space=pltpu.SMEM)
LIMIT = 48 * 2**20
ROWS, COLS, CH = 8, 128, 256
PAIRS, BT, BL, SB, BLOCKS = 128, 16, 64, 16, 64
CELLS = ROWS * COLS


def params(**more):
    return pltpu.CompilerParams(vmem_limit_bytes=LIMIT, **more)


def regrid_kernel(tgt, psrc, w_ref, src_ref, out_ref, slot_ref, cnt, masks, wexp):
    lane = lax.broadcasted_iota(jnp.int32, (BT, 128), 1)
    masks[0] = (lane < BL).astype(F32).astype(BF16)
    masks[1] = (lane >= BL).astype(F32).astype(BF16)
    wexp[...] = jnp.zeros_like(wexp)

    def clear(i, c):
        cnt[i] = 0
        return c

    lax.fori_loop(0, PAIRS, clear, 0)

    def rank(p, c):
        t = tgt[p]
        r = cnt[t]
        cnt[t] = r + 1
        slot_ref[p] = jnp.minimum(2 * t + r, 2 * PAIRS - 1)
        return c

    lax.fori_loop(0, PAIRS, rank, 0)

    def place(p, c):
        s = psrc[p]
        w = w_ref[p]
        ww = jnp.concatenate([w, w], axis=1) * masks[lax.rem(s, 2)]
        row = pl.multiple_of(p * BT, BT)
        col = pl.multiple_of((s // 2) * 128, 128)
        wexp[pl.ds(row, BT), pl.ds(col, 128)] = ww
        return c

    lax.fori_loop(0, PAIRS, place, 0, unroll=4)
    out_ref[...] = jnp.zeros_like(out_ref)
    for m in range(4):
        part = jnp.dot(wexp[m * 512 : (m + 1) * 512, :], src_ref[...], preferred_element_type=F32).astype(BF16)
        for q in range(32):
            out_ref[slot_ref[m * 32 + q]] = part[q * BT : (q + 1) * BT]


def regrid(tgt, psrc, weights, source):
    return pl.pallas_call(
        regrid_kernel,
        name="regrid",
        out_shape=(
            jax.ShapeDtypeStruct((2 * PAIRS, BT, CH), BF16),
            jax.ShapeDtypeStruct((PAIRS,), jnp.int32),
        ),
        in_specs=[SM, SM, VM, VM],
        out_specs=(VM, SM),
        scratch_shapes=[
            pltpu.SMEM((PAIRS,), jnp.int32),
            pltpu.VMEM((2, BT, 128), BF16),
            pltpu.VMEM((PAIRS * BT, SB * BL), BF16),
        ],
        compiler_params=params(),
        cost_estimate=pl.CostEstimate(flops=2 * 2048 * 1024 * 256, bytes_accessed=6 * 2**20, transcendentals=0),
    )(tgt, psrc, weights, source)


def gather_sum_kernel(ids, got_ref, out_ref, acc):
    acc[...] = jnp.zeros_like(acc)

    def add(q, c):
        k = ids[q]
        acc[k] += got_ref[q].astype(F32)
        return c

    lax.fori_loop(0, 2 * PAIRS, add, 0, unroll=8)
    out_ref[...] = acc[0:BLOCKS].astype(BF16)


def gather_sum(ids, arrived):
    return pl.pallas_call(
        gather_sum_kernel,
        name="gather_sum",
        out_shape=jax.ShapeDtypeStruct((BLOCKS, BT, CH), BF16),
        in_specs=[SM, VM],
        out_specs=VM,
        scratch_shapes=[pltpu.VMEM((BLOCKS + 1, BT, CH), F32)],
        compiler_params=params(),
        cost_estimate=pl.CostEstimate(flops=2**21, bytes_accessed=3 * 2**20, transcendentals=0),
    )(ids, arrived)


def place_in_mesh():
    return lax.axis_index("tile"), lax.axis_index("band"), lax.axis_size("tile"), lax.axis_size("band")


def greet(others=0):
    t, b, tiles, bands = place_in_mesh()
    barrier = pltpu.get_barrier_semaphore()
    for dt in (1, -1, 0):
        for db in (-1, 0, 1):
            if dt == 0 and db == 0:
                continue

            def say(dt=dt, db=db):
                pl.semaphore_signal(
                    barrier, inc=1, device_id=(lax.rem(t + dt + tiles, tiles), b + db), device_id_type=MESH
                )

            near_band(b, bands, db, say)
    near = 2 + jnp.where(b > 0, 3, 0) + jnp.where(b < bands - 1, 3, 0)
    pl.semaphore_wait(barrier, near + others)


def near_band(b, bands, db, action):
    if db == 0:
        action()
    elif db < 0:
        pl.when(b > 0)(action)
    else:
        pl.when(b < bands - 1)(action)


def side_copy(send, recv, ss, rs, way, db, group):
    t, b, tiles, bands = place_in_mesh()
    to = lax.rem(t + (1 if way == 0 else tiles - 1), tiles)
    return pltpu.make_async_remote_copy(
        src_ref=send.at[way],
        dst_ref=recv.at[way, group],
        send_sem=ss.at[way, 1 + db],
        recv_sem=rs.at[way, group],
        device_id=(to, b + db),
        device_id_type=MESH,
    )


def row_copy(ext, d, ss, rs, db):
    t, b, tiles, bands = place_in_mesh()
    if db < 0:
        src, dst, k = ext.at[pl.ds(d, d)], ext.at[pl.ds(ROWS + d, d)], 0
    else:
        src, dst, k = ext.at[pl.ds(ROWS, d)], ext.at[pl.ds(0, d)], 1
    return pltpu.make_async_remote_copy(
        src_ref=src, dst_ref=dst, send_sem=ss.at[k], recv_sem=rs.at[k], device_id=(t, b + db), device_id_type=MESH
    )


def start_sides(send, recv, ss, rs):
    b, bands = lax.axis_index("band"), lax.axis_size("band")
    for way in (0, 1):
        for db in (0, -1, 1):
            near_band(b, bands, db, lambda way=way, db=db: side_copy(send, recv, ss, rs, way, db, 1 - db).start())


def start_rows(ext, d, ss, rs):
    b, bands = lax.axis_index("band"), lax.axis_size("band")
    for db in (-1, 1):
        near_band(b, bands, db, lambda db=db: row_copy(ext, d, ss, rs, db).start())


def wait_sides_recv(send, recv, ss, rs):
    b, bands = lax.axis_index("band"), lax.axis_size("band")
    for way in (0, 1):
        for db in (0, -1, 1):
            near_band(b, bands, db, lambda way=way, db=db: side_copy(send, recv, ss, rs, way, 0, 1 + db).wait_recv())


def wait_sides_send(send, recv, ss, rs):
    b, bands = lax.axis_index("band"), lax.axis_size("band")
    for way in (0, 1):
        for db in (0, -1, 1):
            near_band(b, bands, db, lambda way=way, db=db: side_copy(send, recv, ss, rs, way, db, 1 - db).wait_send())


def wait_rows_recv(ext, d, ss, rs):
    b, bands = lax.axis_index("band"), lax.axis_size("band")
    near_band(b, bands, -1, lambda: row_copy(ext, d, ss, rs, 1).wait_recv())
    near_band(b, bands, 1, lambda: row_copy(ext, d, ss, rs, -1).wait_recv())


def wait_rows_send(ext, d, ss, rs):
    b, bands = lax.axis_index("band"), lax.axis_size("band")
    for db in (-1, 1):
        near_band(b, bands, db, lambda db=db: row_copy(ext, d, ss, rs, db).wait_send())


def clear_edges(ext, d):
    b, bands = lax.axis_index("band"), lax.axis_size("band")

    @pl.when(b == 0)
    def _():
        ext[0:d] = jnp.zeros((d, COLS, CH), BF16)

    @pl.when(b == bands - 1)
    def _():
        ext[ROWS + d : ROWS + 2 * d] = jnp.zeros((d, COLS, CH), BF16)


def clear_groups(recv):
    b, bands = lax.axis_index("band"), lax.axis_size("band")
    for way in (0, 1):

        @pl.when(b == 0)
        def _():
            recv[way, 0] = jnp.zeros(recv.shape[2:], BF16)

        @pl.when(b == bands - 1)
        def _():
            recv[way, 2] = jnp.zeros(recv.shape[2:], BF16)


def flags(flip):
    t, b, tiles, bands = place_in_mesh()
    me = flip[t]
    before = flip[lax.rem(t + tiles - 1, tiles)]
    after = flip[lax.rem(t + 1, tiles)]
    return me, before, after


def make_slab(ext, d, send, base, flip_me, tmp):
    if d == 1:
        tmp[...] = jnp.zeros_like(tmp)
    for r in range(ROWS):
        first = ext[d + r, 0:16, :].astype(F32)
        last = ext[d + r, COLS - 16 : COLS, :].astype(F32)
        for k in range(d):
            tmp[0, k * 8 + r : k * 8 + r + 1, :] = first[k : k + 1]
            tmp[1, k * 8 + r : k * 8 + r + 1, :] = last[15 - k : 16 - k]
    turned = jnp.full((16, CH), flip_me, jnp.int32) == 1
    left, right = tmp[0], tmp[1]
    send[0, base : base + 16] = jnp.where(turned, left, right).astype(BF16)
    send[1, base : base + 16] = jnp.where(turned, right, left).astype(BF16)


def open_slab(recv, d, base, flip_me, rim):
    turned = jnp.full((16, CH), flip_me, jnp.int32) == 1
    for g in range(3):
        before = recv[0, g, base : base + 16].astype(F32)
        after = recv[1, g, base : base + 16].astype(F32)
        sides = (jnp.where(turned, after, before), jnp.where(turned, before, after))
        for side in (0, 1):
            for k in range(d):
                part = sides[side][k * 8 : k * 8 + 8]
                if g == 0:
                    rim[side, k, 0:d, :] = part[8 - d :]
                elif g == 1:
                    rim[side, k, d : d + 8, :] = part
                else:
                    rim[side, k, d + 8 : 2 * d + 8, :] = part[:d]


def split_rim(rim, d, flip_me, flip_before, flip_after, turned_rim):
    odd_before = (flip_before != flip_me).astype(jnp.int32)
    odd_after = (flip_after != flip_me).astype(jnp.int32)
    odd_left = jnp.where(flip_me == 0, odd_before, odd_after)
    odd_right = jnp.where(flip_me == 0, odd_after, odd_before)
    for side, odd in ((0, odd_left), (1, odd_right)):
        mask = jnp.full((16, CH), odd, jnp.int32) == 1
        for k in range(d):
            whole = rim[side, k]
            turned_rim[side, k] = jnp.where(mask, whole, 0.0)
            rim[side, k] = jnp.where(mask, 0.0, whole)


def widen(ext, d, rim, wide):
    col = lax.broadcasted_iota(jnp.int32, (COLS, CH), 0)

    def one(row, carry):
        mid = ext[row]
        x = mid.astype(F32)
        left = pltpu.roll(x, d, 0)
        right = pltpu.roll(x, COLS - d, 0)
        for k in range(d):
            near = jnp.broadcast_to(rim[0, k, pl.ds(row, 1), :], (COLS, CH))
            left = jnp.where(col == d - 1 - k, near, left)
            near = jnp.broadcast_to(rim[1, k, pl.ds(row, 1), :], (COLS, CH))
            right = jnp.where(col == COLS - d + k, near, right)
        at = pl.ds(pl.multiple_of(row * COLS, COLS), COLS)
        wide[at, 0:CH] = left.astype(BF16)
        wide[at, CH : 2 * CH] = mid
        wide[at, 2 * CH : 3 * CH] = right.astype(BF16)
        return carry

    lax.fori_loop(0, ROWS + 2 * d, one, 0)


def conv_block(wide, d, taps, m, rows):
    total = None
    for i in range(3):
        lhs = wide[pl.ds(pl.multiple_of(m + i * d * COLS, COLS), rows), :]
        part = jnp.dot(lhs, taps[i], preferred_element_type=F32)
        total = part if total is None else total + part
    return total


def turned_part(turned_rim, d, taps, out):
    left, right = None, None
    for i in range(3):
        lhs_left = jnp.concatenate([turned_rim[0, d - 1 - c, i * d : i * d + 8, :] for c in range(d)], axis=0)
        lhs_right = jnp.concatenate([turned_rim[1, c, i * d : i * d + 8, :] for c in range(d)], axis=0)
        a = jnp.dot(lhs_left.astype(BF16), taps[i, 2 * CH : 3 * CH, :], preferred_element_type=F32)
        z = jnp.dot(lhs_right.astype(BF16), taps[i, 0:CH, :], preferred_element_type=F32)
        left = a if left is None else left + a
        right = z if right is None else right + z
    for c in range(d):
        for r in range(ROWS):
            at = r * COLS + c
            out[at : at + 1, :] += left[c * 8 + r : c * 8 + r + 1]
            at = r * COLS + COLS - d + c
            out[at : at + 1, :] += right[c * 8 + r : c * 8 + r + 1]


STEP = 256


def spot(t, b):
    x = lax.rem(t, 4)
    y = lax.div(t, 8)
    z = lax.rem(lax.div(t, 4), 2) * 2 + lax.div(b, 2)
    return x, y, z, lax.rem(b, 2)


def device_at(x, y, z, core):
    return (y * 8 + lax.div(z, 2) * 4 + x, lax.rem(z, 2) * 2 + core)


def table_peer(stage, k):
    t, b, tiles, bands = place_in_mesh()
    x, y, z, core = spot(t, b)
    if stage == 0:
        return (t, lax.rem(b + k, 4))
    if stage == 1:
        return (t - x + lax.rem(x + k, 4), b)
    if stage == 2:
        return (t + 4 - 8 * lax.rem(lax.div(t, 4), 2), b)
    return (lax.rem(t + 8 * k, 32), b)


TABLE_PEERS = (3, 3, 1, 3)
TABLE_ROWS = (1, 4, 16, 32)


def table_copy(tab, ss, rs, stage, k):
    t, b, tiles, bands = place_in_mesh()
    n = TABLE_ROWS[stage]
    at = lax.div(t * 4 + b, n) * n
    rows = tab.at[pl.ds(at, n)]
    return pltpu.make_async_remote_copy(
        src_ref=rows, dst_ref=rows, send_sem=ss.at[stage, k - 1], recv_sem=rs.at[stage, k - 1],
        device_id=table_peer(stage, k), device_id_type=MESH,
    )


def table_start(tab, ss, rs, stage):
    for k in range(1, TABLE_PEERS[stage] + 1):
        table_copy(tab, ss, rs, stage, k).start()


def table_wait(tab, ss, rs, stage):
    for k in range(1, TABLE_PEERS[stage] + 1):
        table_copy(tab, ss, rs, stage, k).wait()


def greet_table():
    barrier = pltpu.get_barrier_semaphore()
    for stage in range(4):
        for k in range(1, TABLE_PEERS[stage] + 1):
            pl.semaphore_signal(barrier, inc=1, device_id=table_peer(stage, k), device_id_type=MESH)


def back_kernel(
    flip, own_ref, g_ref, k1_ref, k2_ref, hg_ref, k1t_ref, tab,
    ext, send, recv, tmp, rim, trim, wide, k2t, ss, rs, rss, rrs, tss, trs,
):
    d = 2
    t, b, tiles, bands = place_in_mesh()
    tab[t * 4 + b] = own_ref[...]
    me, before, after = flags(flip)
    ext[pl.ds(d, ROWS)] = g_ref[...]
    make_slab(ext, d, send, 0, me, tmp)
    clear_edges(ext, d)
    clear_groups(recv)
    greet_table()
    greet(sum(TABLE_PEERS))
    table_start(tab, tss, trs, 0)
    start_sides(send, recv, ss, rs)
    start_rows(ext, d, rss, rrs)
    for i in range(3):
        for j in range(3):
            k2t[i, j * CH : (j + 1) * CH, :] = k2_ref[2 - i, 2 - j].T
            k1t_ref[i, j * CH : (j + 1) * CH, :] = k1_ref[2 - i, 2 - j].T
    table_wait(tab, tss, trs, 0)
    table_start(tab, tss, trs, 1)
    wait_sides_recv(send, recv, ss, rs)
    wait_rows_recv(ext, d, rss, rrs)
    open_slab(recv, d, 0, me, rim)
    split_rim(rim, d, me, before, after, trim)
    widen(ext, d, rim, wide)
    table_wait(tab, tss, trs, 1)
    table_start(tab, tss, trs, 2)

    def block(n, carry):
        m = pl.multiple_of(n * STEP, STEP)
        hg_ref[pl.ds(m, STEP), :] = conv_block(wide, d, k2t, m, STEP)
        return carry

    lax.fori_loop(0, CELLS // STEP, block, 0)
    table_wait(tab, tss, trs, 2)
    table_start(tab, tss, trs, 3)
    turned_part(trim, d, k2t, hg_ref)
    table_wait(tab, tss, trs, 3)
    wait_sides_send(send, recv, ss, rs)
    wait_rows_send(ext, d, rss, rrs)


def back(flip, own, grad, k1, k2):
    d = 2
    return pl.pallas_call(
        back_kernel,
        name="hidden_adjoint",
        out_shape=(
            jax.ShapeDtypeStruct((CELLS, CH), F32),
            jax.ShapeDtypeStruct((3, 3 * CH, CH), BF16),
            jax.ShapeDtypeStruct((PAIRS, 1, PAIRS), jnp.int32),
        ),
        in_specs=[SM, VM, VM, VM, VM],
        out_specs=(VM, VM, VM),
        scratch_shapes=[
            pltpu.VMEM((ROWS + 2 * d, COLS, CH), BF16),
            pltpu.VMEM((2, 16, CH), BF16),
            pltpu.VMEM((2, 3, 16, CH), BF16),
            pltpu.VMEM((2, 16, CH), F32),
            pltpu.VMEM((2, d, 16, CH), F32),
            pltpu.VMEM((2, d, 16, CH), F32),
            pltpu.VMEM(((ROWS + 2 * d) * COLS, 3 * CH), BF16),
            pltpu.VMEM((3, 3 * CH, CH), BF16),
            pltpu.SemaphoreType.DMA((2, 3)),
            pltpu.SemaphoreType.DMA((2, 3)),
            pltpu.SemaphoreType.DMA((2,)),
            pltpu.SemaphoreType.DMA((2,)),
            pltpu.SemaphoreType.DMA((4, 3)),
            pltpu.SemaphoreType.DMA((4, 3)),
        ],
        compiler_params=params(collective_id=1, has_side_effects=True),
        cost_estimate=pl.CostEstimate(flops=6 * 2**30, bytes_accessed=8 * 2**20, transcendentals=0),
    )(flip, own, grad, k1, k2)


def mid_kernel(
    flip, ids, x_ref, hg_ref, g_ref, k1_ref, k1t_ref,
    back_ref, wide1_ref, wide2_ref, pg_ref,
    ext, exth, extp, send, recv, send2, recv2, tmp, rim, rim2, trim, widep, ing, rounded,
    ss, rs, rss, rrs, ss2, rs2, rssh, rrsh, rssp, rrsp,
):
    me, before, after = flags(flip)
    ext[pl.ds(1, ROWS)] = x_ref[...]
    make_slab(ext, 1, send, 0, me, tmp)
    clear_edges(ext, 1)
    clear_edges(exth, 2)
    clear_edges(extp, 1)
    clear_groups(recv)
    clear_groups(recv2)
    greet()
    start_sides(send, recv, ss, rs)
    start_rows(ext, 1, rss, rrs)
    wait_sides_recv(send, recv, ss, rs)
    wait_rows_recv(ext, 1, rss, rrs)
    open_slab(recv, 1, 0, me, rim)
    widen(ext, 1, rim, wide1_ref)

    def act(n, carry):
        m = pl.multiple_of(n * STEP, STEP)
        pre = conv_block(wide1_ref, 1, k1_ref, m, STEP)
        s = jax.nn.sigmoid(pre)
        hid = (pre * s).astype(BF16)
        grad = (hg_ref[pl.ds(m, STEP), :] * s * (1.0 + pre * (1.0 - s))).astype(BF16)
        for q in range(STEP // COLS):
            row = n * (STEP // COLS) + q
            exth[2 + row] = hid[q * COLS : (q + 1) * COLS]
            extp[1 + row] = grad[q * COLS : (q + 1) * COLS]
        pg_ref[pl.ds(m, STEP), :] = grad
        return carry

    lax.fori_loop(0, CELLS // STEP, act, 0)
    make_slab(extp, 1, send2, 16, me, tmp)
    make_slab(exth, 2, send2, 0, me, tmp)
    start_sides(send2, recv2, ss2, rs2)
    start_rows(extp, 1, rssp, rrsp)
    start_rows(exth, 2, rssh, rrsh)
    wait_sides_recv(send2, recv2, ss2, rs2)
    wait_rows_recv(extp, 1, rssp, rrsp)
    open_slab(recv2, 1, 16, me, rim)
    split_rim(rim, 1, me, before, after, trim)
    widen(extp, 1, rim, widep)

    def fold(n, carry):
        m = pl.multiple_of(n * STEP, STEP)
        ing[pl.ds(m, STEP), :] = g_ref[pl.ds(m, STEP), :].astype(F32) + conv_block(widep, 1, k1t_ref, m, STEP)
        return carry

    lax.fori_loop(0, CELLS // STEP, fold, 0)
    turned_part(trim, 1, k1t_ref, ing)
    for q in range(4):
        part = ing[q * 256 : (q + 1) * 256, :].astype(BF16)
        rounded[q * 16 : (q + 1) * 16] = part.reshape(16, BT, CH)

    def pick(q, carry):
        back_ref[q] = rounded[ids[q]]
        return carry

    lax.fori_loop(0, 2 * PAIRS, pick, 0, unroll=4)
    wait_rows_recv(exth, 2, rssh, rrsh)
    open_slab(recv2, 2, 0, me, rim2)
    widen(exth, 2, rim2, wide2_ref)
    wait_sides_send(send, recv, ss, rs)
    wait_rows_send(ext, 1, rss, rrs)
    wait_sides_send(send2, recv2, ss2, rs2)
    wait_rows_send(exth, 2, rssh, rrsh)
    wait_rows_send(extp, 1, rssp, rrsp)


def mid(flip, ids, x, hidden_grad, grad, k1, k1t):
    dma = pltpu.SemaphoreType.DMA
    return pl.pallas_call(
        mid_kernel,
        name="middle",
        out_shape=(
            jax.ShapeDtypeStruct((2 * PAIRS, BT, CH), BF16),
            jax.ShapeDtypeStruct(((ROWS + 2) * COLS, 3 * CH), BF16),
            jax.ShapeDtypeStruct(((ROWS + 4) * COLS, 3 * CH), BF16),
            jax.ShapeDtypeStruct((CELLS, CH), BF16),
        ),
        in_specs=[SM, SM, VM, VM, VM, VM, VM],
        out_specs=(VM, VM, VM, VM),
        scratch_shapes=[
            pltpu.VMEM((ROWS + 2, COLS, CH), BF16),
            pltpu.VMEM((ROWS + 4, COLS, CH), BF16),
            pltpu.VMEM((ROWS + 2, COLS, CH), BF16),
            pltpu.VMEM((2, 16, CH), BF16),
            pltpu.VMEM((2, 3, 16, CH), BF16),
            pltpu.VMEM((2, 32, CH), BF16),
            pltpu.VMEM((2, 3, 32, CH), BF16),
            pltpu.VMEM((2, 16, CH), F32),
            pltpu.VMEM((2, 1, 16, CH), F32),
            pltpu.VMEM((2, 2, 16, CH), F32),
            pltpu.VMEM((2, 1, 16, CH), F32),
            pltpu.VMEM(((ROWS + 2) * COLS, 3 * CH), BF16),
            pltpu.VMEM((CELLS, CH), F32),
            pltpu.VMEM((BLOCKS, BT, CH), BF16),
            dma((2, 3)), dma((2, 3)), dma((2,)), dma((2,)),
            dma((2, 3)), dma((2, 3)), dma((2,)), dma((2,)), dma((2,)), dma((2,)),
        ],
        compiler_params=params(collective_id=2, has_side_effects=True),
        cost_estimate=pl.CostEstimate(flops=6 * 2**30, bytes_accessed=12 * 2**20, transcendentals=2**18),
    )(flip, ids, x, hidden_grad, grad, k1, k1t)


PART = 3 * CH


def axis_peer(axis, k):
    t, b, tiles, bands = place_in_mesh()
    at = list(spot(t, b))
    at[axis] = lax.rem(at[axis] + k, 4)
    return device_at(*at)


def twin():
    t, b, tiles, bands = place_in_mesh()
    return (t, b + 1 - 2 * lax.rem(b, 2))


def sum_kernel(
    wide1, pg, wide2, g, x_ref, k2_ref, mixed_ref, out_ref,
    acc, send1, recv1, send2, recv2, send3, recv3, recv4,
    s1, r1, s2, r2, s3, r3, s4, r4, s5, r5, s6, r6, s7, r7,
):
    t, b, tiles, bands = place_in_mesh()
    place = spot(t, b)
    core = place[3]
    barrier = pltpu.get_barrier_semaphore()
    pl.semaphore_signal(barrier, inc=1, device_id=twin(), device_id_type=MESH)
    for axis in range(3):
        for k in (1, 2, 3):
            pl.semaphore_signal(barrier, inc=1, device_id=axis_peer(axis, k), device_id_type=MESH)
    pl.semaphore_wait(barrier, 10)

    def axes(o):
        return o, (o + 1) % 3, (o + 2) % 3

    def copy(src, dst, ss, rs, to):
        return pltpu.make_async_remote_copy(
            src_ref=src, dst_ref=dst, send_sem=ss, recv_sem=rs, device_id=to, device_id_type=MESH
        )

    def first(o):
        return copy(send1.at[o], recv1.at[o], s1.at[o], r1.at[o], twin())

    def second(o, k):
        a = axes(o)[0]
        at = pl.ds(pl.multiple_of(lax.rem(place[a] + k, 4) * 192, 64), 192)
        return copy(send2.at[o, at], recv2.at[o, k - 1], s2.at[o, k - 1], r2.at[o, k - 1], axis_peer(a, k))

    def third(o, k):
        a = axes(o)[1]
        at = pl.ds(pl.multiple_of(lax.rem(place[a] + k, 4) * 48, 16), 48)
        return copy(send3.at[o, at], recv3.at[o, k - 1], s3.at[o, k - 1], r3.at[o, k - 1], axis_peer(a, k))

    def fourth(o, k):
        a = axes(o)[2]
        mine = recv4.at[o, place[a]]
        return copy(mine, mine, s4.at[o, k - 1], r4.at[o, k - 1], axis_peer(a, k))

    def fifth(o, k):
        a, c, _ = axes(o)
        rows = out_ref.at[core, o, pl.ds(pl.multiple_of(place[a] * 192 + place[c] * 48, 16), 48)]
        return copy(rows, rows, s5.at[o, k - 1], r5.at[o, k - 1], axis_peer(c, k))

    def sixth(o, k):
        a = axes(o)[0]
        rows = out_ref.at[core, o, pl.ds(pl.multiple_of(place[a] * 192, 64), 192)]
        return copy(rows, rows, s6.at[o, k - 1], r6.at[o, k - 1], axis_peer(a, k))

    def seventh(o):
        return copy(out_ref.at[core, o], out_ref.at[core, o], s7.at[o], r7.at[o], twin())

    for o in range(3):
        acc[1, o] = lax.dot_general(
            wide2[o * 2 * COLS : o * 2 * COLS + CELLS, :], g[...], (((0,), (0,)), ((), ())), preferred_element_type=F32
        )
        acc[0, o] = lax.dot_general(
            wide1[o * COLS : o * COLS + CELLS, :], pg[...], (((0,), (0,)), ((), ())), preferred_element_type=F32
        )
        send1[o] = acc[1 - core, o].astype(BF16)
        first(o).start()
    for o in range(3):
        first(o).wait_recv()
        total = acc[core, o] + recv1[o].astype(F32)
        acc[core, o] = total
        send2[o] = total.astype(BF16)
        for k in (1, 2, 3):
            second(o, k).start()

    def block(n, carry):
        m = pl.multiple_of(n * STEP, STEP)
        mixed_ref[pl.ds(m, STEP), :] = (
            x_ref[pl.ds(m, STEP), :].astype(F32) + conv_block(wide2, 2, k2_ref, m, STEP)
        ).astype(BF16)
        return carry

    lax.fori_loop(0, CELLS // STEP, block, 0)
    for o in range(3):
        a, c, e = axes(o)
        for k in (1, 2, 3):
            second(o, k).wait_recv()
        own = pl.ds(pl.multiple_of(place[a] * 192, 64), 192)
        total = acc[core, o, own, :]
        for k in (1, 2, 3):
            total = total + recv2[o, k - 1].astype(F32)
        acc[core, o, 0:192, :] = total
        send3[o] = total.astype(BF16)
        for k in (1, 2, 3):
            third(o, k).start()
    for o in range(3):
        a, c, e = axes(o)
        for k in (1, 2, 3):
            third(o, k).wait_recv()
        total = acc[core, o, pl.ds(pl.multiple_of(place[c] * 48, 16), 48), :]
        for k in (1, 2, 3):
            total = total + recv3[o, k - 1].astype(F32)
        recv4[o, place[e]] = total.astype(BF16)
        for k in (1, 2, 3):
            fourth(o, k).start()
    for o in range(3):
        a, c, e = axes(o)
        for k in (1, 2, 3):
            fourth(o, k).wait_recv()
        v = [recv4[o, q].astype(F32) for q in range(4)]
        total = ((v[0] + v[1]) + v[2]) + v[3]
        out_ref[core, o, pl.ds(pl.multiple_of(place[a] * 192 + place[c] * 48, 16), 48), :] = total.astype(BF16)
        for k in (1, 2, 3):
            fifth(o, k).start()
    for o in range(3):
        for k in (1, 2, 3):
            fifth(o, k).wait_recv()
        for k in (1, 2, 3):
            sixth(o, k).start()
    for o in range(3):
        for k in (1, 2, 3):
            sixth(o, k).wait_recv()
        seventh(o).start()
    for o in range(3):
        seventh(o).wait_recv()
    for o in range(3):
        first(o).wait_send()
        seventh(o).wait_send()
        for k in (1, 2, 3):
            for step in (second, third, fourth, fifth, sixth):
                step(o, k).wait_send()


def kernel_sums(wide1, pg, wide2, g, x, k2):
    dma = pltpu.SemaphoreType.DMA
    three, nine = [dma((3,))] * 2, [dma((3, 3))] * 2
    return pl.pallas_call(
        sum_kernel,
        name="kernel_sums",
        out_shape=(
            jax.ShapeDtypeStruct((CELLS, CH), BF16),
            jax.ShapeDtypeStruct((2, 3, PART, CH), BF16),
        ),
        in_specs=[VM] * 6,
        out_specs=(VM, VM),
        scratch_shapes=[
            pltpu.VMEM((2, 3, PART, CH), F32),
            pltpu.VMEM((3, PART, CH), BF16),
            pltpu.VMEM((3, PART, CH), BF16),
            pltpu.VMEM((3, PART, CH), BF16),
            pltpu.VMEM((3, 3, 192, CH), BF16),
            pltpu.VMEM((3, 192, CH), BF16),
            pltpu.VMEM((3, 3, 48, CH), BF16),
            pltpu.VMEM((3, 4, 48, CH), BF16),
            *three, *nine, *nine, *nine, *nine, *nine, *three,
        ],
        compiler_params=params(collective_id=3, has_side_effects=True),
        cost_estimate=pl.CostEstimate(flops=20 * 2**30, bytes_accessed=14 * 2**20, transcendentals=0),
    )(wide1, pg, wide2, g, x, k2)


def source_kernel(slot, got_ref, w_ref, ps_ref, sums_ref, out_ref, one_ref, two_ref, rows, wexp):
    for i in range(3):
        one_ref[i] = sums_ref[0, i].astype(F32)
        two_ref[i] = sums_ref[1, i].astype(F32)

    def take(p, carry):
        rows[pl.ds(pl.multiple_of(p * BT, BT), BT), :] = got_ref[slot[p]]
        return carry

    lax.fori_loop(0, PAIRS, take, 0, unroll=4)
    w = w_ref[...]
    ps = ps_ref[...]
    for s in range(SB):
        wexp[s * BL : (s + 1) * BL, :] = w * (ps == s).astype(F32).astype(BF16)
    for m in range(4):
        out_ref[m * 256 : (m + 1) * 256, :] = jnp.dot(
            wexp[m * 256 : (m + 1) * 256, :], rows[...], preferred_element_type=F32
        ).astype(BF16)


def source_side(slot, returned, w_cells, ps_cells, sums):
    return pl.pallas_call(
        source_kernel,
        name="source_grad",
        out_shape=(
            jax.ShapeDtypeStruct((SB * BL, CH), BF16),
            jax.ShapeDtypeStruct((3, PART, CH), F32),
            jax.ShapeDtypeStruct((3, PART, CH), F32),
        ),
        in_specs=[SM, VM, VM, VM, VM],
        out_specs=(VM, VM, VM),
        scratch_shapes=[
            pltpu.VMEM((PAIRS * BT, CH), BF16),
            pltpu.VMEM((SB * BL, PAIRS * BT), BF16),
        ],
        compiler_params=params(),
        cost_estimate=pl.CostEstimate(flops=2 * 2048 * 1024 * 256, bytes_accessed=4 * 2**20, transcendentals=0),
    )(slot, returned, w_cells, ps_cells, sums)


def local(
    source_cells, regrid_weights, pair_target, pair_block, pair_source, flip_codes, kernel_one, kernel_two, out_grad
):
    axes = ("tile", "band")
    me = lax.axis_index(axes)
    target = pair_target[:, 0]
    outgoing, slot = regrid(target, pair_source, regrid_weights, source_cells)
    arrived = lax.all_to_all(outgoing, axes, split_axis=0, concat_axis=0, tiled=True)
    upstream = out_grad[0]
    named = (target * BLOCKS + pair_block)[None, :]
    hidden_grad, k1_back, table = back(flip_codes, named, upstream, kernel_one, kernel_two)
    table = table[:, 0, :]
    order = lax.broadcasted_iota(jnp.int32, table.shape, 1)
    mine = (table // BLOCKS) == me
    first = jnp.min(jnp.where(mine, order, PAIRS), axis=1, keepdims=True)
    last = jnp.max(jnp.where(mine, order, -1), axis=1, keepdims=True)
    block = table % BLOCKS
    id_first = jnp.sum(jnp.where(order == first, block, 0), axis=1) + jnp.where(first[:, 0] == PAIRS, BLOCKS, 0)
    more = last > first
    id_last = jnp.sum(jnp.where((order == last) & more, block, 0), axis=1) + jnp.where(more[:, 0], 0, BLOCKS)
    ids = jnp.stack([id_first, id_last], axis=1).reshape(2 * PAIRS)
    regridded = gather_sum(ids, arrived)
    back_rows, wide1, wide2, pre_grad = mid(
        flip_codes,
        jnp.minimum(ids, BLOCKS - 1),
        regridded.reshape(ROWS, COLS, CH),
        hidden_grad,
        upstream.reshape(CELLS, CH),
        kernel_one.reshape(3, 3 * CH, CH),
        k1_back,
    )
    returned = lax.all_to_all(back_rows, axes, split_axis=0, concat_axis=0, tiled=True)
    mixed, sums = kernel_sums(
        wide1,
        pre_grad,
        wide2,
        upstream.reshape(CELLS, CH),
        regridded.reshape(CELLS, CH),
        kernel_two.reshape(3, PART, CH),
    )
    w_cells = regrid_weights.transpose(2, 0, 1).reshape(BL, PAIRS * BT)
    ps_cells = jnp.repeat(pair_source, BT)[None, :]
    source_grad, one, two = source_side(slot, returned, w_cells, ps_cells, sums)
    return (
        mixed.reshape(1, ROWS, COLS, CH),
        one.reshape(3, 3, CH, CH),
        two.reshape(3, 3, CH, CH),
        source_grad,
    )


def solution(mesh):
    placed = (
        P(("tile", "band"), None),
        P(("tile", "band"), None, None),
        P(("tile", "band"), None),
        P(("tile", "band")),
        P(("tile", "band")),
        P(),
        P(),
        P(),
        P("tile", "band", None, None),
    )
    return jax.shard_map(
        local,
        mesh=mesh,
        in_specs=placed,
        out_specs=(P("tile", "band", None, None), P(), P(), P(("tile", "band"), None)),
        check_vma=False,
    )
```

```python
import jax
import jax.numpy as jnp
from jax import lax
from jax.experimental import pallas as pl
from jax.experimental.pallas import tpu as pltpu
from jax.sharding import PartitionSpec as P

F32 = jnp.float32
BF16 = jnp.bfloat16
MESH = pl.DeviceIdType.MESH
VM = pl.BlockSpec(memory_space=pltpu.VMEM)
SM = pl.BlockSpec(memory_space=pltpu.SMEM)
LIMIT = 48 * 2**20
ROWS, COLS, CH = 8, 128, 256
PAIRS, BT, BL, SB, BLOCKS = 128, 16, 64, 16, 64
CELLS = ROWS * COLS


def params(**more):
    return pltpu.CompilerParams(vmem_limit_bytes=LIMIT, **more)


def regrid_kernel(tgt, psrc, w_ref, src_ref, out_ref, slot_ref, cnt, masks, wexp):
    lane = lax.broadcasted_iota(jnp.int32, (BT, 128), 1)
    masks[0] = (lane < BL).astype(F32).astype(BF16)
    masks[1] = (lane >= BL).astype(F32).astype(BF16)
    wexp[...] = jnp.zeros_like(wexp)

    def clear(i, c):
        cnt[i] = 0
        return c

    lax.fori_loop(0, PAIRS, clear, 0)

    def rank(p, c):
        t = tgt[p]
        r = cnt[t]
        cnt[t] = r + 1
        slot_ref[p] = jnp.minimum(r, 1) * PAIRS + t
        return c

    lax.fori_loop(0, PAIRS, rank, 0)

    def place(p, c):
        s = psrc[p]
        w = w_ref[p]
        ww = jnp.concatenate([w, w], axis=1) * masks[lax.rem(s, 2)]
        row = pl.multiple_of(p * BT, BT)
        col = pl.multiple_of((s // 2) * 128, 128)
        wexp[pl.ds(row, BT), pl.ds(col, 128)] = ww
        return c

    lax.fori_loop(0, PAIRS, place, 0, unroll=4)
    out_ref[...] = jnp.zeros_like(out_ref)
    for m in range(4):
        part = jnp.dot(wexp[m * 512 : (m + 1) * 512, :], src_ref[...], preferred_element_type=F32).astype(BF16)
        for q in range(32):
            at = slot_ref[m * 32 + q]
            for h in (0, 1):
                out_ref[h, at] = part[q * BT : (q + 1) * BT, h * 128 : (h + 1) * 128]


def regrid(tgt, psrc, weights, source):
    return pl.pallas_call(
        regrid_kernel,
        name="regrid",
        out_shape=(
            jax.ShapeDtypeStruct((2, 2 * PAIRS, BT, 128), BF16),
            jax.ShapeDtypeStruct((PAIRS,), jnp.int32),
        ),
        in_specs=[SM, SM, VM, VM],
        out_specs=(VM, SM),
        scratch_shapes=[
            pltpu.SMEM((PAIRS,), jnp.int32),
            pltpu.VMEM((2, BT, 128), BF16),
            pltpu.VMEM((PAIRS * BT, SB * BL), BF16),
        ],
        compiler_params=params(),
        cost_estimate=pl.CostEstimate(flops=2 * 2048 * 1024 * 256, bytes_accessed=6 * 2**20, transcendentals=0),
    )(tgt, psrc, weights, source)


def gather_sum_kernel(ids, got_ref, out_ref, acc):
    acc[...] = jnp.zeros_like(acc)

    def add(q, c):
        k = ids[q]
        for h in (0, 1):
            acc[k, :, h * 128 : (h + 1) * 128] += got_ref[h, q].astype(F32)
        return c

    lax.fori_loop(0, 2 * PAIRS, add, 0, unroll=8)
    out_ref[...] = acc[0:BLOCKS].astype(BF16)


def gather_sum(ids, arrived):
    return pl.pallas_call(
        gather_sum_kernel,
        name="gather_sum",
        out_shape=jax.ShapeDtypeStruct((BLOCKS, BT, CH), BF16),
        in_specs=[SM, VM],
        out_specs=VM,
        scratch_shapes=[pltpu.VMEM((BLOCKS + 1, BT, CH), F32)],
        compiler_params=params(),
        cost_estimate=pl.CostEstimate(flops=2**21, bytes_accessed=3 * 2**20, transcendentals=0),
    )(ids, arrived)


def place_in_mesh():
    return lax.axis_index("tile"), lax.axis_index("band"), lax.axis_size("tile"), lax.axis_size("band")


def greet(others=0):
    t, b, tiles, bands = place_in_mesh()
    barrier = pltpu.get_barrier_semaphore()
    for dt in (1, -1, 0):
        for db in (-1, 0, 1):
            if dt == 0 and db == 0:
                continue

            def say(dt=dt, db=db):
                pl.semaphore_signal(
                    barrier, inc=1, device_id=(lax.rem(t + dt + tiles, tiles), b + db), device_id_type=MESH
                )

            near_band(b, bands, db, say)
    near = 2 + jnp.where(b > 0, 3, 0) + jnp.where(b < bands - 1, 3, 0)
    pl.semaphore_wait(barrier, near + others)


def near_band(b, bands, db, action):
    if db == 0:
        action()
    elif db < 0:
        pl.when(b > 0)(action)
    else:
        pl.when(b < bands - 1)(action)


def side_copy(send, recv, ss, rs, way, db, group):
    t, b, tiles, bands = place_in_mesh()
    to = lax.rem(t + (1 if way == 0 else tiles - 1), tiles)
    return pltpu.make_async_remote_copy(
        src_ref=send.at[way],
        dst_ref=recv.at[way, group],
        send_sem=ss.at[way, 1 + db],
        recv_sem=rs.at[way, group],
        device_id=(to, b + db),
        device_id_type=MESH,
    )


def row_copy(ext, d, ss, rs, db):
    t, b, tiles, bands = place_in_mesh()
    if db < 0:
        src, dst, k = ext.at[pl.ds(d, d)], ext.at[pl.ds(ROWS + d, d)], 0
    else:
        src, dst, k = ext.at[pl.ds(ROWS, d)], ext.at[pl.ds(0, d)], 1
    return pltpu.make_async_remote_copy(
        src_ref=src, dst_ref=dst, send_sem=ss.at[k], recv_sem=rs.at[k], device_id=(t, b + db), device_id_type=MESH
    )


def start_sides(send, recv, ss, rs):
    b, bands = lax.axis_index("band"), lax.axis_size("band")
    for way in (0, 1):
        for db in (0, -1, 1):
            near_band(b, bands, db, lambda way=way, db=db: side_copy(send, recv, ss, rs, way, db, 1 - db).start())


def start_rows(ext, d, ss, rs):
    b, bands = lax.axis_index("band"), lax.axis_size("band")
    for db in (-1, 1):
        near_band(b, bands, db, lambda db=db: row_copy(ext, d, ss, rs, db).start())


def wait_sides_recv(send, recv, ss, rs):
    b, bands = lax.axis_index("band"), lax.axis_size("band")
    for way in (0, 1):
        for db in (0, -1, 1):
            near_band(b, bands, db, lambda way=way, db=db: side_copy(send, recv, ss, rs, way, 0, 1 + db).wait_recv())


def wait_sides_send(send, recv, ss, rs):
    b, bands = lax.axis_index("band"), lax.axis_size("band")
    for way in (0, 1):
        for db in (0, -1, 1):
            near_band(b, bands, db, lambda way=way, db=db: side_copy(send, recv, ss, rs, way, db, 1 - db).wait_send())


def wait_rows_recv(ext, d, ss, rs):
    b, bands = lax.axis_index("band"), lax.axis_size("band")
    near_band(b, bands, -1, lambda: row_copy(ext, d, ss, rs, 1).wait_recv())
    near_band(b, bands, 1, lambda: row_copy(ext, d, ss, rs, -1).wait_recv())


def wait_rows_send(ext, d, ss, rs):
    b, bands = lax.axis_index("band"), lax.axis_size("band")
    for db in (-1, 1):
        near_band(b, bands, db, lambda db=db: row_copy(ext, d, ss, rs, db).wait_send())


def clear_edges(ext, d):
    b, bands = lax.axis_index("band"), lax.axis_size("band")

    @pl.when(b == 0)
    def _():
        ext[0:d] = jnp.zeros((d, COLS, CH), BF16)

    @pl.when(b == bands - 1)
    def _():
        ext[ROWS + d : ROWS + 2 * d] = jnp.zeros((d, COLS, CH), BF16)


def clear_groups(recv):
    b, bands = lax.axis_index("band"), lax.axis_size("band")
    for way in (0, 1):

        @pl.when(b == 0)
        def _():
            recv[way, 0] = jnp.zeros(recv.shape[2:], BF16)

        @pl.when(b == bands - 1)
        def _():
            recv[way, 2] = jnp.zeros(recv.shape[2:], BF16)


def flags(flip):
    t, b, tiles, bands = place_in_mesh()
    me = flip[t]
    before = flip[lax.rem(t + tiles - 1, tiles)]
    after = flip[lax.rem(t + 1, tiles)]
    return me, before, after


def make_slab(ext, d, send, base, flip_me, tmp):
    if d == 1:
        tmp[...] = jnp.zeros_like(tmp)
    for r in range(ROWS):
        first = ext[d + r, 0:16, :].astype(F32)
        last = ext[d + r, COLS - 16 : COLS, :].astype(F32)
        for k in range(d):
            tmp[0, k * 8 + r : k * 8 + r + 1, :] = first[k : k + 1]
            tmp[1, k * 8 + r : k * 8 + r + 1, :] = last[15 - k : 16 - k]
    turned = jnp.full((16, CH), flip_me, jnp.int32) == 1
    left, right = tmp[0], tmp[1]
    send[0, base : base + 16] = jnp.where(turned, left, right).astype(BF16)
    send[1, base : base + 16] = jnp.where(turned, right, left).astype(BF16)


def open_slab(recv, d, base, flip_me, rim):
    turned = jnp.full((16, CH), flip_me, jnp.int32) == 1
    for g in range(3):
        before = recv[0, g, base : base + 16].astype(F32)
        after = recv[1, g, base : base + 16].astype(F32)
        sides = (jnp.where(turned, after, before), jnp.where(turned, before, after))
        for side in (0, 1):
            for k in range(d):
                part = sides[side][k * 8 : k * 8 + 8]
                if g == 0:
                    rim[side, k, 0:d, :] = part[8 - d :]
                elif g == 1:
                    rim[side, k, d : d + 8, :] = part
                else:
                    rim[side, k, d + 8 : 2 * d + 8, :] = part[:d]


def split_rim(rim, d, flip_me, flip_before, flip_after, turned_rim):
    odd_before = (flip_before != flip_me).astype(jnp.int32)
    odd_after = (flip_after != flip_me).astype(jnp.int32)
    odd_left = jnp.where(flip_me == 0, odd_before, odd_after)
    odd_right = jnp.where(flip_me == 0, odd_after, odd_before)
    for side, odd in ((0, odd_left), (1, odd_right)):
        mask = jnp.full((16, CH), odd, jnp.int32) == 1
        for k in range(d):
            whole = rim[side, k]
            turned_rim[side, k] = jnp.where(mask, whole, 0.0)
            rim[side, k] = jnp.where(mask, 0.0, whole)


def widen(ext, d, rim, wide):
    col = lax.broadcasted_iota(jnp.int32, (COLS, CH), 0)

    def one(row, carry):
        mid = ext[row]
        x = mid.astype(F32)
        left = pltpu.roll(x, d, 0)
        right = pltpu.roll(x, COLS - d, 0)
        for k in range(d):
            near = jnp.broadcast_to(rim[0, k, pl.ds(row, 1), :], (COLS, CH))
            left = jnp.where(col == d - 1 - k, near, left)
            near = jnp.broadcast_to(rim[1, k, pl.ds(row, 1), :], (COLS, CH))
            right = jnp.where(col == COLS - d + k, near, right)
        at = pl.ds(pl.multiple_of(row * COLS, COLS), COLS)
        wide[at, 0:CH] = left.astype(BF16)
        wide[at, CH : 2 * CH] = mid
        wide[at, 2 * CH : 3 * CH] = right.astype(BF16)
        return carry

    lax.fori_loop(0, ROWS + 2 * d, one, 0)


def conv_block(wide, d, taps, m, rows):
    total = None
    for i in range(3):
        lhs = wide[pl.ds(pl.multiple_of(m + i * d * COLS, COLS), rows), :]
        part = jnp.dot(lhs, taps[i], preferred_element_type=F32)
        total = part if total is None else total + part
    return total


def turned_part(turned_rim, d, taps, out):
    left, right = None, None
    for i in range(3):
        lhs_left = jnp.concatenate([turned_rim[0, d - 1 - c, i * d : i * d + 8, :] for c in range(d)], axis=0)
        lhs_right = jnp.concatenate([turned_rim[1, c, i * d : i * d + 8, :] for c in range(d)], axis=0)
        a = jnp.dot(lhs_left.astype(BF16), taps[i, 2 * CH : 3 * CH, :], preferred_element_type=F32)
        z = jnp.dot(lhs_right.astype(BF16), taps[i, 0:CH, :], preferred_element_type=F32)
        left = a if left is None else left + a
        right = z if right is None else right + z
    for c in range(d):
        for r in range(ROWS):
            at = r * COLS + c
            out[at : at + 1, :] += left[c * 8 + r : c * 8 + r + 1]
            at = r * COLS + COLS - d + c
            out[at : at + 1, :] += right[c * 8 + r : c * 8 + r + 1]


STEP = 256


def spot(t, b):
    x = lax.rem(t, 4)
    y = lax.div(t, 8)
    z = lax.rem(lax.div(t, 4), 2) * 2 + lax.div(b, 2)
    return x, y, z, lax.rem(b, 2)


def device_at(x, y, z, core):
    return (y * 8 + lax.div(z, 2) * 4 + x, lax.rem(z, 2) * 2 + core)


WORLD = (4, 4, 2, 4, 2, 2, BT, 128)
UNITS = [(hs, c) for c in (0, 1) for hs in range(4)]


def axis_peer(axis, k):
    t, b, tiles, bands = place_in_mesh()
    at = list(spot(t, b))
    at[axis] = lax.rem(at[axis] + k, 4)
    return device_at(*at)


def twin():
    t, b, tiles, bands = place_in_mesh()
    return (t, b + 1 - 2 * lax.rem(b, 2))


def greet_axes():
    barrier = pltpu.get_barrier_semaphore()
    pl.semaphore_signal(barrier, inc=1, device_id=twin(), device_id_type=MESH)
    for axis in range(3):
        for k in (1, 2, 3):
            pl.semaphore_signal(barrier, inc=1, device_id=axis_peer(axis, k), device_id_type=MESH)


AXIS_PEERS = 10


def along(ref, unit, axis, v):
    hs, c = UNITS[unit]
    if axis == 0:
        return ref.at[hs, :, :, v, :, c]
    if axis == 1:
        return ref.at[hs, v, :, :, :, c]
    return ref.at[hs, :, lax.div(v, 2), :, lax.rem(v, 2), c]


def remote(src, dst, ss, rs, to):
    return pltpu.make_async_remote_copy(
        src_ref=src, dst_ref=dst, send_sem=ss, recv_sem=rs, device_id=to, device_id_type=MESH
    )


class Swap:
    def __init__(self, bufs, sems):
        self.bufs, self.sems = bufs, sems
        t, b, tiles, bands = place_in_mesh()
        self.place = spot(t, b)

    def core_copy(self, hs):
        me = self.place[3]
        src, dst = self.bufs[0], self.bufs[1]
        ss, rs = self.sems[0], self.sems[1]
        return remote(
            src.at[hs, :, :, :, :, 1 - me], dst.at[hs, :, :, :, :, me], ss.at[hs], rs.at[hs], twin()
        )

    def core_own(self, hs):
        me = self.place[3]
        src, dst = self.bufs[0], self.bufs[1]
        return pltpu.make_async_copy(src.at[hs, :, :, :, :, me], dst.at[hs, :, :, :, :, me], self.sems[2].at[hs])

    def core_start(self, hs):
        self.core_copy(hs).start()
        self.core_own(hs).start()

    def core_wait(self, hs):
        self.core_copy(hs).wait_recv()
        self.core_own(hs).wait()

    def hop(self, stage, u, k):
        axis = (u + stage) % 3
        me = self.place[axis]
        src, dst = self.bufs[1 + stage], self.bufs[2 + stage]
        return remote(
            along(src, u, axis, lax.rem(me + k, 4)), along(dst, u, axis, me),
            self.sems[3].at[stage, u, k - 1], self.sems[4].at[stage, u, k - 1], axis_peer(axis, k),
        )

    def own(self, stage, u):
        axis = (u + stage) % 3
        me = self.place[axis]
        src, dst = self.bufs[1 + stage], self.bufs[2 + stage]
        return pltpu.make_async_copy(along(src, u, axis, me), along(dst, u, axis, me), self.sems[5].at[stage, u])

    def start(self, stage, u):
        for k in (2, 1, 3):
            self.hop(stage, u, k).start()
        self.own(stage, u).start()

    def wait(self, stage, u):
        for k in (1, 2, 3):
            self.hop(stage, u, k).wait_recv()
        self.own(stage, u).wait()

    def first_stage(self):
        done = set()
        for u in range(8):
            hs = UNITS[u][0]
            if hs not in done:
                self.core_wait(hs)
                done.add(hs)
            self.start(0, u)

    def next_stage(self, stage):
        for u in range(8):
            self.wait(stage - 1, u)
            self.start(stage, u)

    def last_wait(self):
        for u in range(8):
            self.wait(2, u)

    def drain(self):
        for hs in range(4):
            self.core_copy(hs).wait_send()
        for stage in range(3):
            for u in range(8):
                for k in (1, 2, 3):
                    self.hop(stage, u, k).wait_send()


def swap_sems():
    dma = pltpu.SemaphoreType.DMA
    return [dma((4,)), dma((4,)), dma((4,)), dma((3, 8, 3)), dma((3, 8, 3)), dma((3, 8))]


def table_peer(stage, k):
    t, b, tiles, bands = place_in_mesh()
    x, y, z, core = spot(t, b)
    if stage == 0:
        return (t, lax.rem(b + k, 4))
    if stage == 1:
        return (t - x + lax.rem(x + k, 4), b)
    if stage == 2:
        return (t + 4 - 8 * lax.rem(lax.div(t, 4), 2), b)
    return (lax.rem(t + 8 * k, 32), b)


TABLE_PEERS = (3, 3, 1, 3)
TABLE_ROWS = (1, 4, 16, 32)


def table_copy(tab, ss, rs, stage, k):
    t, b, tiles, bands = place_in_mesh()
    n = TABLE_ROWS[stage]
    at = lax.div(t * 4 + b, n) * n
    rows = tab.at[pl.ds(at, n)]
    return pltpu.make_async_remote_copy(
        src_ref=rows, dst_ref=rows, send_sem=ss.at[stage, k - 1], recv_sem=rs.at[stage, k - 1],
        device_id=table_peer(stage, k), device_id_type=MESH,
    )


def table_start(tab, ss, rs, stage):
    for k in range(1, TABLE_PEERS[stage] + 1):
        table_copy(tab, ss, rs, stage, k).start()


def table_wait(tab, ss, rs, stage):
    for k in range(1, TABLE_PEERS[stage] + 1):
        table_copy(tab, ss, rs, stage, k).wait()


def greet_table():
    barrier = pltpu.get_barrier_semaphore()
    for stage in range(4):
        for k in range(1, TABLE_PEERS[stage] + 1):
            pl.semaphore_signal(barrier, inc=1, device_id=table_peer(stage, k), device_id_type=MESH)


def back_kernel(
    flip, own_ref, g_ref, k1_ref, k2_ref, outgoing, hg_ref, k1t_ref, tab, arrived,
    ext, send, recv, tmp, rim, trim, wide, k2t, b1, b2, b3, ss, rs, rss, rrs, tss, trs, *sems,
):
    d = 2
    swap = Swap((outgoing, b1, b2, b3, arrived), sems)
    t, b, tiles, bands = place_in_mesh()
    tab[t * 4 + b] = own_ref[...]
    me, before, after = flags(flip)
    ext[pl.ds(d, ROWS)] = g_ref[...]
    make_slab(ext, d, send, 0, me, tmp)
    clear_edges(ext, d)
    clear_groups(recv)
    greet_table()
    greet_axes()
    greet(sum(TABLE_PEERS) + AXIS_PEERS)
    for hs in range(4):
        swap.core_start(hs)
    table_start(tab, tss, trs, 0)
    start_sides(send, recv, ss, rs)
    start_rows(ext, d, rss, rrs)
    table_wait(tab, tss, trs, 0)
    table_start(tab, tss, trs, 1)
    swap.first_stage()
    for i in range(3):
        for j in range(3):
            k2t[i, j * CH : (j + 1) * CH, :] = k2_ref[2 - i, 2 - j].T
            k1t_ref[i, j * CH : (j + 1) * CH, :] = k1_ref[2 - i, 2 - j].T
    table_wait(tab, tss, trs, 1)
    table_start(tab, tss, trs, 2)
    wait_sides_recv(send, recv, ss, rs)
    wait_rows_recv(ext, d, rss, rrs)
    open_slab(recv, d, 0, me, rim)
    split_rim(rim, d, me, before, after, trim)
    widen(ext, d, rim, wide)
    table_wait(tab, tss, trs, 2)
    table_start(tab, tss, trs, 3)
    swap.next_stage(1)

    def block(n, carry):
        m = pl.multiple_of(n * STEP, STEP)
        hg_ref[pl.ds(m, STEP), :] = conv_block(wide, d, k2t, m, STEP)
        return carry

    lax.fori_loop(0, CELLS // STEP, block, 0)
    turned_part(trim, d, k2t, hg_ref)
    swap.next_stage(2)
    table_wait(tab, tss, trs, 3)
    wait_sides_send(send, recv, ss, rs)
    wait_rows_send(ext, d, rss, rrs)
    swap.last_wait()
    swap.drain()


def back(flip, own, grad, k1, k2, outgoing):
    d = 2
    return pl.pallas_call(
        back_kernel,
        name="hidden_adjoint",
        out_shape=(
            jax.ShapeDtypeStruct((CELLS, CH), F32),
            jax.ShapeDtypeStruct((3, 3 * CH, CH), BF16),
            jax.ShapeDtypeStruct((PAIRS, 1, PAIRS), jnp.int32),
            jax.ShapeDtypeStruct(WORLD, BF16),
        ),
        in_specs=[SM, VM, VM, VM, VM, VM],
        out_specs=(VM, VM, VM, VM),
        scratch_shapes=[
            pltpu.VMEM((ROWS + 2 * d, COLS, CH), BF16),
            pltpu.VMEM((2, 16, CH), BF16),
            pltpu.VMEM((2, 3, 16, CH), BF16),
            pltpu.VMEM((2, 16, CH), F32),
            pltpu.VMEM((2, d, 16, CH), F32),
            pltpu.VMEM((2, d, 16, CH), F32),
            pltpu.VMEM(((ROWS + 2 * d) * COLS, 3 * CH), BF16),
            pltpu.VMEM((3, 3 * CH, CH), BF16),
            pltpu.VMEM(WORLD, BF16),
            pltpu.VMEM(WORLD, BF16),
            pltpu.VMEM(WORLD, BF16),
            pltpu.SemaphoreType.DMA((2, 3)),
            pltpu.SemaphoreType.DMA((2, 3)),
            pltpu.SemaphoreType.DMA((2,)),
            pltpu.SemaphoreType.DMA((2,)),
            pltpu.SemaphoreType.DMA((4, 3)),
            pltpu.SemaphoreType.DMA((4, 3)),
            *swap_sems(),
        ],
        compiler_params=params(collective_id=1, has_side_effects=True),
        cost_estimate=pl.CostEstimate(flops=6 * 2**30, bytes_accessed=8 * 2**20, transcendentals=0),
    )(flip, own, grad, k1, k2, outgoing)


def mid_kernel(
    flip, ids, slot, x_ref, hg_ref, g_ref, k1_ref, k1t_ref, k2_ref, w_ref, ps_ref,
    mixed_ref, out_ref, source_ref,
    ext, exth, extp, send, recv, send2, recv2, tmp, rim, rim2, trim, wide1_ref, wide2_ref, widep, pg_ref, ing, rounded,
    b0, b1, b2, b3, b4, rows, wexp,
    acc, send1, recv1, sent2, got2, sent3, got3, got4,
    ss, rs, rss, rrs, ss2, rs2, rssh, rrsh, rssp, rrsp,
    s1, r1, s2, r2, s3, r3, s4, r4, s5, r5, s6, r6, s7, r7, *sems,
):
    swap = Swap((b0, b1, b2, b3, b4), sems)
    sums = Sums(out_ref, acc, send1, recv1, sent2, got2, sent3, got3, got4, (s1, r1, s2, r2, s3, r3, s4, r4, s5, r5, s6, r6, s7, r7))
    me, before, after = flags(flip)
    ext[pl.ds(1, ROWS)] = x_ref[...]
    make_slab(ext, 1, send, 0, me, tmp)
    clear_edges(ext, 1)
    clear_edges(exth, 2)
    clear_edges(extp, 1)
    clear_groups(recv)
    clear_groups(recv2)
    greet_axes()
    greet(AXIS_PEERS)
    start_sides(send, recv, ss, rs)
    start_rows(ext, 1, rss, rrs)
    wait_sides_recv(send, recv, ss, rs)
    wait_rows_recv(ext, 1, rss, rrs)
    open_slab(recv, 1, 0, me, rim)
    widen(ext, 1, rim, wide1_ref)

    def act(n, carry):
        m = pl.multiple_of(n * STEP, STEP)
        pre = conv_block(wide1_ref, 1, k1_ref, m, STEP)
        s = jax.nn.sigmoid(pre)
        hid = (pre * s).astype(BF16)
        grad = (hg_ref[pl.ds(m, STEP), :] * s * (1.0 + pre * (1.0 - s))).astype(BF16)
        for q in range(STEP // COLS):
            row = n * (STEP // COLS) + q
            exth[2 + row] = hid[q * COLS : (q + 1) * COLS]
            extp[1 + row] = grad[q * COLS : (q + 1) * COLS]
        pg_ref[pl.ds(m, STEP), :] = grad
        return carry

    lax.fori_loop(0, CELLS // STEP, act, 0)
    make_slab(extp, 1, send2, 16, me, tmp)
    make_slab(exth, 2, send2, 0, me, tmp)
    start_sides(send2, recv2, ss2, rs2)
    start_rows(extp, 1, rssp, rrsp)
    start_rows(exth, 2, rssh, rrsh)
    wait_sides_recv(send2, recv2, ss2, rs2)
    wait_rows_recv(extp, 1, rssp, rrsp)
    open_slab(recv2, 1, 16, me, rim)
    split_rim(rim, 1, me, before, after, trim)
    widen(extp, 1, rim, widep)

    def fold(n, carry):
        m = pl.multiple_of(n * STEP, STEP)
        ing[pl.ds(m, STEP), :] = g_ref[pl.ds(m, STEP), :].astype(F32) + conv_block(widep, 1, k1t_ref, m, STEP)
        return carry

    lax.fori_loop(0, CELLS // STEP, fold, 0)
    turned_part(trim, 1, k1t_ref, ing)
    for q in range(4):
        part = ing[q * 256 : (q + 1) * 256, :].astype(BF16)
        rounded[q * 16 : (q + 1) * 16] = part.reshape(16, BT, CH)

    for half in (0, 1):

        def pick(q, carry):
            block = rounded[ids[half * PAIRS + q]]
            y, zh, x = lax.div(q, 32), lax.rem(lax.div(q, 16), 2), lax.rem(lax.div(q, 4), 4)
            zl, c = lax.rem(lax.div(q, 2), 2), lax.rem(q, 2)
            b0[half, y, zh, x, zl, c] = block[:, 0:128]
            b0[2 + half, y, zh, x, zl, c] = block[:, 128:256]
            return carry

        lax.fori_loop(0, PAIRS, pick, 0, unroll=4)
        swap.core_start(half)
        swap.core_start(2 + half)
    wait_rows_recv(exth, 2, rssh, rrsh)
    open_slab(recv2, 2, 0, me, rim2)
    widen(exth, 2, rim2, wide2_ref)
    swap.first_stage()
    for o in range(3):
        acc[1, o] = lax.dot_general(
            wide2_ref[o * 2 * COLS : o * 2 * COLS + CELLS, :],
            g_ref[...],
            (((0,), (0,)), ((), ())),
            preferred_element_type=F32,
        )
        acc[0, o] = lax.dot_general(
            wide1_ref[o * COLS : o * COLS + CELLS, :],
            pg_ref[...],
            (((0,), (0,)), ((), ())),
            preferred_element_type=F32,
        )
        sums.start(o)
    sums.to_second()
    swap.next_stage(1)

    def block(n, carry):
        m = pl.multiple_of(n * STEP, STEP)
        mixed_ref[pl.ds(m, STEP), :] = (
            x_ref[pl.ds(m // COLS, STEP // COLS)].reshape(STEP, CH).astype(F32)
            + conv_block(wide2_ref, 2, k2_ref, m, STEP)
        ).astype(BF16)
        return carry

    lax.fori_loop(0, CELLS // STEP, block, 0)
    w = w_ref[...]
    ps = ps_ref[...]
    for n in range(SB):
        wexp[n * BL : (n + 1) * BL, :] = w * (ps == n).astype(F32).astype(BF16)
    sums.to_third()
    swap.next_stage(2)
    sums.to_fourth()
    sums.to_fifth()
    sums.to_sixth()
    swap.last_wait()

    def take(p, carry):
        q = slot[p]
        half, t = lax.div(q, PAIRS), lax.rem(q, PAIRS)
        y, zh, x = lax.div(t, 32), lax.rem(lax.div(t, 16), 2), lax.rem(lax.div(t, 4), 4)
        zl, c = lax.rem(lax.div(t, 2), 2), lax.rem(t, 2)
        at = pl.ds(pl.multiple_of(p * BT, BT), BT)
        rows[at, 0:128] = b4[half, y, zh, x, zl, c]
        rows[at, 128:256] = b4[2 + half, y, zh, x, zl, c]
        return carry

    lax.fori_loop(0, PAIRS, take, 0, unroll=4)
    for m in range(4):
        source_ref[m * 256 : (m + 1) * 256, :] = jnp.dot(
            wexp[m * 256 : (m + 1) * 256, :], rows[...], preferred_element_type=F32
        ).astype(BF16)
    sums.to_seventh()
    sums.finish()
    wait_sides_send(send, recv, ss, rs)
    wait_rows_send(ext, 1, rss, rrs)
    wait_sides_send(send2, recv2, ss2, rs2)
    wait_rows_send(exth, 2, rssh, rrsh)
    wait_rows_send(extp, 1, rssp, rrsp)
    swap.drain()


def mid(flip, ids, slot, x, hidden_grad, grad, k1, k1t, k2, w_cells, ps_cells):
    dma = pltpu.SemaphoreType.DMA
    three, nine = [dma((3,))] * 2, [dma((3, 3))] * 2
    return pl.pallas_call(
        mid_kernel,
        name="middle",
        out_shape=(
            jax.ShapeDtypeStruct((CELLS, CH), BF16),
            jax.ShapeDtypeStruct((2, 3, PART, CH), BF16),
            jax.ShapeDtypeStruct((SB * BL, CH), BF16),
        ),
        in_specs=[SM, SM, SM] + [VM] * 8,
        out_specs=(VM, VM, VM),
        scratch_shapes=[
            pltpu.VMEM((ROWS + 2, COLS, CH), BF16),
            pltpu.VMEM((ROWS + 4, COLS, CH), BF16),
            pltpu.VMEM((ROWS + 2, COLS, CH), BF16),
            pltpu.VMEM((2, 16, CH), BF16),
            pltpu.VMEM((2, 3, 16, CH), BF16),
            pltpu.VMEM((2, 32, CH), BF16),
            pltpu.VMEM((2, 3, 32, CH), BF16),
            pltpu.VMEM((2, 16, CH), F32),
            pltpu.VMEM((2, 1, 16, CH), F32),
            pltpu.VMEM((2, 2, 16, CH), F32),
            pltpu.VMEM((2, 1, 16, CH), F32),
            pltpu.VMEM(((ROWS + 2) * COLS, 3 * CH), BF16),
            pltpu.VMEM(((ROWS + 4) * COLS, 3 * CH), BF16),
            pltpu.VMEM(((ROWS + 2) * COLS, 3 * CH), BF16),
            pltpu.VMEM((CELLS, CH), BF16),
            pltpu.VMEM((CELLS, CH), F32),
            pltpu.VMEM((BLOCKS, BT, CH), BF16),
            *[pltpu.VMEM(WORLD, BF16)] * 5,
            pltpu.VMEM((PAIRS * BT, CH), BF16),
            pltpu.VMEM((SB * BL, PAIRS * BT), BF16),
            pltpu.VMEM((2, 3, PART, CH), F32),
            pltpu.VMEM((3, PART, CH), BF16),
            pltpu.VMEM((3, PART, CH), BF16),
            pltpu.VMEM((3, PART, CH), BF16),
            pltpu.VMEM((3, 3, 192, CH), BF16),
            pltpu.VMEM((3, 192, CH), BF16),
            pltpu.VMEM((3, 3, 48, CH), BF16),
            pltpu.VMEM((3, 4, 48, CH), BF16),
            dma((2, 3)), dma((2, 3)), dma((2,)), dma((2,)),
            dma((2, 3)), dma((2, 3)), dma((2,)), dma((2,)), dma((2,)), dma((2,)),
            *three, *nine, *nine, *nine, *nine, *nine, *three,
            *swap_sems(),
        ],
        compiler_params=pltpu.CompilerParams(vmem_limit_bytes=58 * 2**20, collective_id=2, has_side_effects=True),
        cost_estimate=pl.CostEstimate(flops=6 * 2**30, bytes_accessed=12 * 2**20, transcendentals=2**18),
    )(flip, ids, slot, x, hidden_grad, grad, k1, k1t, k2, w_cells, ps_cells)


PART = 3 * CH


def axes_of(o):
    return o, (o + 1) % 3, (o + 2) % 3


class Sums:
    def __init__(self, out, acc, send1, recv1, sent2, got2, sent3, got3, got4, sems):
        self.out, self.acc, self.send1, self.recv1 = out, acc, send1, recv1
        self.sent2, self.got2, self.sent3, self.got3, self.got4, self.sems = sent2, got2, sent3, got3, got4, sems
        t, b, tiles, bands = place_in_mesh()
        self.place = spot(t, b)
        self.core = self.place[3]

    def first(self, o):
        s, r = self.sems[0:2]
        return remote(self.send1.at[o], self.recv1.at[o], s.at[o], r.at[o], twin())

    def second(self, o, k):
        s, r = self.sems[2:4]
        a = axes_of(o)[0]
        at = pl.ds(pl.multiple_of(lax.rem(self.place[a] + k, 4) * 192, 64), 192)
        return remote(self.sent2.at[o, at], self.got2.at[o, k - 1], s.at[o, k - 1], r.at[o, k - 1], axis_peer(a, k))

    def third(self, o, k):
        s, r = self.sems[4:6]
        a = axes_of(o)[1]
        at = pl.ds(pl.multiple_of(lax.rem(self.place[a] + k, 4) * 48, 16), 48)
        return remote(self.sent3.at[o, at], self.got3.at[o, k - 1], s.at[o, k - 1], r.at[o, k - 1], axis_peer(a, k))

    def fourth(self, o, k):
        s, r = self.sems[6:8]
        a = axes_of(o)[2]
        mine = self.got4.at[o, self.place[a]]
        return remote(mine, mine, s.at[o, k - 1], r.at[o, k - 1], axis_peer(a, k))

    def rows(self, o, wide):
        a, c, _ = axes_of(o)
        if wide:
            return pl.ds(pl.multiple_of(self.place[a] * 192, 64), 192)
        return pl.ds(pl.multiple_of(self.place[a] * 192 + self.place[c] * 48, 16), 48)

    def fifth(self, o, k):
        s, r = self.sems[8:10]
        rows = self.out.at[self.core, o, self.rows(o, False)]
        return remote(rows, rows, s.at[o, k - 1], r.at[o, k - 1], axis_peer(axes_of(o)[1], k))

    def sixth(self, o, k):
        s, r = self.sems[10:12]
        rows = self.out.at[self.core, o, self.rows(o, True)]
        return remote(rows, rows, s.at[o, k - 1], r.at[o, k - 1], axis_peer(axes_of(o)[0], k))

    def seventh(self, o):
        s, r = self.sems[12:14]
        whole = self.out.at[self.core, o]
        return remote(whole, whole, s.at[o], r.at[o], twin())

    def start(self, o):
        self.send1[o] = self.acc[1 - self.core, o].astype(BF16)
        self.first(o).start()

    def to_second(self):
        for o in range(3):
            self.first(o).wait_recv()
            total = self.acc[self.core, o] + self.recv1[o].astype(F32)
            self.acc[self.core, o] = total
            self.sent2[o] = total.astype(BF16)
            for k in (2, 1, 3):
                self.second(o, k).start()

    def to_third(self):
        for o in range(3):
            for k in (1, 2, 3):
                self.second(o, k).wait_recv()
            total = self.acc[self.core, o, self.rows(o, True), :]
            for k in (1, 2, 3):
                total = total + self.got2[o, k - 1].astype(F32)
            self.acc[self.core, o, 0:192, :] = total
            self.sent3[o] = total.astype(BF16)
            for k in (2, 1, 3):
                self.third(o, k).start()

    def to_fourth(self):
        for o in range(3):
            a, c, e = axes_of(o)
            for k in (1, 2, 3):
                self.third(o, k).wait_recv()
            total = self.acc[self.core, o, pl.ds(pl.multiple_of(self.place[c] * 48, 16), 48), :]
            for k in (1, 2, 3):
                total = total + self.got3[o, k - 1].astype(F32)
            self.got4[o, self.place[e]] = total.astype(BF16)
            for k in (2, 1, 3):
                self.fourth(o, k).start()

    def to_fifth(self):
        for o in range(3):
            for k in (1, 2, 3):
                self.fourth(o, k).wait_recv()
            v = [self.got4[o, q].astype(F32) for q in range(4)]
            self.out[self.core, o, self.rows(o, False), :] = (((v[0] + v[1]) + v[2]) + v[3]).astype(BF16)
            for k in (2, 1, 3):
                self.fifth(o, k).start()

    def to_sixth(self):
        for o in range(3):
            for k in (1, 2, 3):
                self.fifth(o, k).wait_recv()
            for k in (2, 1, 3):
                self.sixth(o, k).start()

    def to_seventh(self):
        for o in range(3):
            for k in (1, 2, 3):
                self.sixth(o, k).wait_recv()
            self.seventh(o).start()

    def finish(self):
        for o in range(3):
            self.seventh(o).wait_recv()
        for o in range(3):
            self.first(o).wait_send()
            self.seventh(o).wait_send()
            for k in (1, 2, 3):
                for step in (self.second, self.third, self.fourth, self.fifth, self.sixth):
                    step(o, k).wait_send()


def local(
    source_cells, regrid_weights, pair_target, pair_block, pair_source, flip_codes, kernel_one, kernel_two, out_grad
):
    axes = ("tile", "band")
    me = lax.axis_index(axes)
    target = pair_target[:, 0]
    outgoing, slot = regrid(target, pair_source, regrid_weights, source_cells)
    upstream = out_grad[0]
    named = (target * BLOCKS + pair_block)[None, :]
    hidden_grad, k1_back, table, arrived = back(
        flip_codes, named, upstream, kernel_one, kernel_two, outgoing.reshape(WORLD)
    )
    table = table[:, 0, :]
    order = lax.broadcasted_iota(jnp.int32, table.shape, 1)
    mine = (table // BLOCKS) == me
    first = jnp.min(jnp.where(mine, order, PAIRS), axis=1, keepdims=True)
    last = jnp.max(jnp.where(mine, order, -1), axis=1, keepdims=True)
    block = table % BLOCKS
    id_first = jnp.sum(jnp.where(order == first, block, 0), axis=1) + jnp.where(first[:, 0] == PAIRS, BLOCKS, 0)
    more = last > first
    id_last = jnp.sum(jnp.where((order == last) & more, block, 0), axis=1) + jnp.where(more[:, 0], 0, BLOCKS)
    ids = jnp.concatenate([id_first, id_last])
    regridded = gather_sum(ids, arrived.reshape(2, 2 * PAIRS, BT, 128))
    w_cells = regrid_weights.transpose(2, 0, 1).reshape(BL, PAIRS * BT)
    ps_cells = jnp.repeat(pair_source, BT)[None, :]
    mixed, sums, source_grad = mid(
        flip_codes,
        jnp.minimum(ids, BLOCKS - 1),
        slot,
        regridded.reshape(ROWS, COLS, CH),
        hidden_grad,
        upstream.reshape(CELLS, CH),
        kernel_one.reshape(3, PART, CH),
        k1_back,
        kernel_two.reshape(3, PART, CH),
        w_cells,
        ps_cells,
    )
    return (
        mixed.reshape(1, ROWS, COLS, CH),
        sums[0].astype(F32).reshape(3, 3, CH, CH),
        sums[1].astype(F32).reshape(3, 3, CH, CH),
        source_grad,
    )


def solution(mesh):
    placed = (
        P(("tile", "band"), None),
        P(("tile", "band"), None, None),
        P(("tile", "band"), None),
        P(("tile", "band")),
        P(("tile", "band")),
        P(),
        P(),
        P(),
        P("tile", "band", None, None),
    )
    return jax.shard_map(
        local,
        mesh=mesh,
        in_specs=placed,
        out_specs=(P("tile", "band", None, None), P(), P(), P(("tile", "band"), None)),
        check_vma=False,
    )
```

```python
import jax
import jax.numpy as jnp
from jax import lax
from jax.experimental import pallas as pl
from jax.experimental.pallas import tpu as pltpu
from jax.sharding import PartitionSpec as P

F32 = jnp.float32
BF16 = jnp.bfloat16
MESH = pl.DeviceIdType.MESH
VM = pl.BlockSpec(memory_space=pltpu.VMEM)
SM = pl.BlockSpec(memory_space=pltpu.SMEM)
LIMIT = 16 * 2**20
ROWS, COLS, CH = 8, 128, 256
PAIRS, BT, BL, SB, BLOCKS = 128, 16, 64, 16, 64
CELLS = ROWS * COLS


def params(**more):
    return pltpu.CompilerParams(vmem_limit_bytes=LIMIT, **more)


def regrid_kernel(tgt, psrc, w_ref, src_ref, out_ref, slot_ref, cnt, masks, wexp):
    lane = lax.broadcasted_iota(jnp.int32, (BT, 128), 1)
    masks[0] = (lane < BL).astype(F32).astype(BF16)
    masks[1] = (lane >= BL).astype(F32).astype(BF16)
    wexp[...] = jnp.zeros_like(wexp)

    def clear(i, c):
        cnt[i] = 0
        return c

    lax.fori_loop(0, PAIRS, clear, 0)

    def rank(p, c):
        t = tgt[p]
        r = cnt[t]
        cnt[t] = r + 1
        slot_ref[p] = jnp.minimum(r, 1) * PAIRS + t
        return c

    lax.fori_loop(0, PAIRS, rank, 0)

    def place(p, c):
        s = psrc[p]
        w = w_ref[p]
        ww = jnp.concatenate([w, w], axis=1) * masks[lax.rem(s, 2)]
        row = pl.multiple_of(p * BT, BT)
        col = pl.multiple_of((s // 2) * 128, 128)
        wexp[pl.ds(row, BT), pl.ds(col, 128)] = ww
        return c

    lax.fori_loop(0, PAIRS, place, 0, unroll=4)
    out_ref[...] = jnp.zeros_like(out_ref)
    for m in range(4):
        part = jnp.dot(wexp[m * 512 : (m + 1) * 512, :], src_ref[...], preferred_element_type=F32).astype(BF16)
        for q in range(32):
            at = slot_ref[m * 32 + q]
            for h in (0, 1):
                out_ref[h, at] = part[q * BT : (q + 1) * BT, h * 128 : (h + 1) * 128]


def regrid(tgt, psrc, weights, source):
    return pl.pallas_call(
        regrid_kernel,
        name="regrid",
        out_shape=(
            jax.ShapeDtypeStruct((2, 2 * PAIRS, BT, 128), BF16),
            jax.ShapeDtypeStruct((PAIRS,), jnp.int32),
        ),
        in_specs=[SM, SM, VM, VM],
        out_specs=(VM, SM),
        scratch_shapes=[
            pltpu.SMEM((PAIRS,), jnp.int32),
            pltpu.VMEM((2, BT, 128), BF16),
            pltpu.VMEM((PAIRS * BT, SB * BL), BF16),
        ],
        compiler_params=params(),
        cost_estimate=pl.CostEstimate(flops=2 * 2048 * 1024 * 256, bytes_accessed=6 * 2**20, transcendentals=0),
    )(tgt, psrc, weights, source)


def gather_sum_kernel(ids, got_ref, out_ref, acc):
    acc[...] = jnp.zeros_like(acc)

    def add(q, c):
        k = ids[lax.div(q, PAIRS), lax.rem(q, PAIRS)]
        for h in (0, 1):
            acc[k, :, h * 128 : (h + 1) * 128] += got_ref[h, q].astype(F32)
        return c

    lax.fori_loop(0, 2 * PAIRS, add, 0, unroll=8)
    out_ref[...] = acc[0:BLOCKS].astype(BF16)


def gather_sum(ids, arrived):
    return pl.pallas_call(
        gather_sum_kernel,
        name="gather_sum",
        out_shape=jax.ShapeDtypeStruct((BLOCKS, BT, CH), BF16),
        in_specs=[SM, VM],
        out_specs=VM,
        scratch_shapes=[pltpu.VMEM((BLOCKS + 1, BT, CH), F32)],
        compiler_params=params(),
        cost_estimate=pl.CostEstimate(flops=2**21, bytes_accessed=3 * 2**20, transcendentals=0),
    )(ids, arrived)


def place_in_mesh():
    return lax.axis_index("tile"), lax.axis_index("band"), lax.axis_size("tile"), lax.axis_size("band")


def greet(others=0):
    t, b, tiles, bands = place_in_mesh()
    barrier = pltpu.get_barrier_semaphore()
    for dt in (1, -1, 0):
        for db in (-1, 0, 1):
            if dt == 0 and db == 0:
                continue

            def say(dt=dt, db=db):
                pl.semaphore_signal(
                    barrier, inc=1, device_id=(lax.rem(t + dt + tiles, tiles), b + db), device_id_type=MESH
                )

            near_band(b, bands, db, say)
    near = 2 + jnp.where(b > 0, 3, 0) + jnp.where(b < bands - 1, 3, 0)
    pl.semaphore_wait(barrier, near + others)


def near_band(b, bands, db, action):
    if db == 0:
        action()
    elif db < 0:
        pl.when(b > 0)(action)
    else:
        pl.when(b < bands - 1)(action)


def side_copy(send, recv, ss, rs, way, db, group):
    t, b, tiles, bands = place_in_mesh()
    to = lax.rem(t + (1 if way == 0 else tiles - 1), tiles)
    return pltpu.make_async_remote_copy(
        src_ref=send.at[way],
        dst_ref=recv.at[way, group],
        send_sem=ss.at[way, 1 + db],
        recv_sem=rs.at[way, group],
        device_id=(to, b + db),
        device_id_type=MESH,
    )


def row_copy(ext, d, ss, rs, db):
    t, b, tiles, bands = place_in_mesh()
    if db < 0:
        src, dst, k = ext.at[pl.ds(d, d)], ext.at[pl.ds(ROWS + d, d)], 0
    else:
        src, dst, k = ext.at[pl.ds(ROWS, d)], ext.at[pl.ds(0, d)], 1
    return pltpu.make_async_remote_copy(
        src_ref=src, dst_ref=dst, send_sem=ss.at[k], recv_sem=rs.at[k], device_id=(t, b + db), device_id_type=MESH
    )


def start_sides(send, recv, ss, rs):
    b, bands = lax.axis_index("band"), lax.axis_size("band")
    for way in (0, 1):
        for db in (0, -1, 1):
            near_band(b, bands, db, lambda way=way, db=db: side_copy(send, recv, ss, rs, way, db, 1 - db).start())


def start_rows(ext, d, ss, rs):
    b, bands = lax.axis_index("band"), lax.axis_size("band")
    for db in (-1, 1):
        near_band(b, bands, db, lambda db=db: row_copy(ext, d, ss, rs, db).start())


def wait_sides_recv(send, recv, ss, rs):
    b, bands = lax.axis_index("band"), lax.axis_size("band")
    for way in (0, 1):
        for db in (0, -1, 1):
            near_band(b, bands, db, lambda way=way, db=db: side_copy(send, recv, ss, rs, way, 0, 1 + db).wait_recv())


def wait_sides_send(send, recv, ss, rs):
    b, bands = lax.axis_index("band"), lax.axis_size("band")
    for way in (0, 1):
        for db in (0, -1, 1):
            near_band(b, bands, db, lambda way=way, db=db: side_copy(send, recv, ss, rs, way, db, 1 - db).wait_send())


def wait_rows_recv(ext, d, ss, rs):
    b, bands = lax.axis_index("band"), lax.axis_size("band")
    near_band(b, bands, -1, lambda: row_copy(ext, d, ss, rs, 1).wait_recv())
    near_band(b, bands, 1, lambda: row_copy(ext, d, ss, rs, -1).wait_recv())


def wait_rows_send(ext, d, ss, rs):
    b, bands = lax.axis_index("band"), lax.axis_size("band")
    for db in (-1, 1):
        near_band(b, bands, db, lambda db=db: row_copy(ext, d, ss, rs, db).wait_send())


def clear_edges(ext, d):
    b, bands = lax.axis_index("band"), lax.axis_size("band")

    @pl.when(b == 0)
    def _():
        ext[0:d] = jnp.zeros((d, COLS, CH), BF16)

    @pl.when(b == bands - 1)
    def _():
        ext[ROWS + d : ROWS + 2 * d] = jnp.zeros((d, COLS, CH), BF16)


def clear_groups(recv):
    b, bands = lax.axis_index("band"), lax.axis_size("band")
    for way in (0, 1):

        @pl.when(b == 0)
        def _():
            recv[way, 0] = jnp.zeros(recv.shape[2:], BF16)

        @pl.when(b == bands - 1)
        def _():
            recv[way, 2] = jnp.zeros(recv.shape[2:], BF16)


def flags(flip):
    t, b, tiles, bands = place_in_mesh()
    me = flip[t]
    before = flip[lax.rem(t + tiles - 1, tiles)]
    after = flip[lax.rem(t + 1, tiles)]
    return me, before, after


def make_slab(ext, d, send, base, flip_me, tmp):
    if d == 1:
        tmp[...] = jnp.zeros_like(tmp)
    for r in range(ROWS):
        first = ext[d + r, 0:16, :].astype(F32)
        last = ext[d + r, COLS - 16 : COLS, :].astype(F32)
        for k in range(d):
            tmp[0, k * 8 + r : k * 8 + r + 1, :] = first[k : k + 1]
            tmp[1, k * 8 + r : k * 8 + r + 1, :] = last[15 - k : 16 - k]
    turned = jnp.full((16, CH), flip_me, jnp.int32) == 1
    left, right = tmp[0], tmp[1]
    send[0, base : base + 16] = jnp.where(turned, left, right).astype(BF16)
    send[1, base : base + 16] = jnp.where(turned, right, left).astype(BF16)


def open_slab(recv, d, base, flip_me, rim):
    turned = jnp.full((16, CH), flip_me, jnp.int32) == 1
    for g in range(3):
        before = recv[0, g, base : base + 16].astype(F32)
        after = recv[1, g, base : base + 16].astype(F32)
        sides = (jnp.where(turned, after, before), jnp.where(turned, before, after))
        for side in (0, 1):
            for k in range(d):
                part = sides[side][k * 8 : k * 8 + 8]
                if g == 0:
                    rim[side, k, 0:d, :] = part[8 - d :]
                elif g == 1:
                    rim[side, k, d : d + 8, :] = part
                else:
                    rim[side, k, d + 8 : 2 * d + 8, :] = part[:d]


def split_rim(rim, d, flip_me, flip_before, flip_after, turned_rim):
    odd_before = (flip_before != flip_me).astype(jnp.int32)
    odd_after = (flip_after != flip_me).astype(jnp.int32)
    odd_left = jnp.where(flip_me == 0, odd_before, odd_after)
    odd_right = jnp.where(flip_me == 0, odd_after, odd_before)
    for side, odd in ((0, odd_left), (1, odd_right)):
        mask = jnp.full((16, CH), odd, jnp.int32) == 1
        for k in range(d):
            whole = rim[side, k]
            turned_rim[side, k] = jnp.where(mask, whole, 0.0)
            rim[side, k] = jnp.where(mask, 0.0, whole)


def widen(ext, d, rim, wide):
    col = lax.broadcasted_iota(jnp.int32, (COLS, CH), 0)

    def one(row, carry):
        mid = ext[row]
        x = mid.astype(F32)
        left = pltpu.roll(x, d, 0)
        right = pltpu.roll(x, COLS - d, 0)
        for k in range(d):
            near = jnp.broadcast_to(rim[0, k, pl.ds(row, 1), :], (COLS, CH))
            left = jnp.where(col == d - 1 - k, near, left)
            near = jnp.broadcast_to(rim[1, k, pl.ds(row, 1), :], (COLS, CH))
            right = jnp.where(col == COLS - d + k, near, right)
        at = pl.ds(pl.multiple_of(row * COLS, COLS), COLS)
        wide[at, 0:CH] = left.astype(BF16)
        wide[at, CH : 2 * CH] = mid
        wide[at, 2 * CH : 3 * CH] = right.astype(BF16)
        return carry

    lax.fori_loop(0, ROWS + 2 * d, one, 0)


def conv_block(wide, d, taps, m, rows):
    total = None
    for i in range(3):
        lhs = wide[pl.ds(pl.multiple_of(m + i * d * COLS, COLS), rows), :]
        part = jnp.dot(lhs, taps[i], preferred_element_type=F32)
        total = part if total is None else total + part
    return total


def turned_part(turned_rim, d, taps, out):
    left, right = None, None
    for i in range(3):
        lhs_left = jnp.concatenate([turned_rim[0, d - 1 - c, i * d : i * d + 8, :] for c in range(d)], axis=0)
        lhs_right = jnp.concatenate([turned_rim[1, c, i * d : i * d + 8, :] for c in range(d)], axis=0)
        a = jnp.dot(lhs_left.astype(BF16), taps[i, 2 * CH : 3 * CH, :], preferred_element_type=F32)
        z = jnp.dot(lhs_right.astype(BF16), taps[i, 0:CH, :], preferred_element_type=F32)
        left = a if left is None else left + a
        right = z if right is None else right + z
    for c in range(d):
        for r in range(ROWS):
            at = r * COLS + c
            out[at : at + 1, :] += left[c * 8 + r : c * 8 + r + 1]
            at = r * COLS + COLS - d + c
            out[at : at + 1, :] += right[c * 8 + r : c * 8 + r + 1]


STEP = 256


def spot(t, b):
    x = lax.rem(t, 4)
    y = lax.div(t, 8)
    z = lax.rem(lax.div(t, 4), 2) * 2 + lax.div(b, 2)
    return x, y, z, lax.rem(b, 2)


def device_at(x, y, z, core):
    return (y * 8 + lax.div(z, 2) * 4 + x, lax.rem(z, 2) * 2 + core)


WORLD = (4, 4, 2, 4, 2, 2, BT, 128)
UNITS = [(hs, c) for c in (0, 1) for hs in range(4)]


def axis_peer(axis, k):
    t, b, tiles, bands = place_in_mesh()
    at = list(spot(t, b))
    at[axis] = lax.rem(at[axis] + k, 4)
    return device_at(*at)


def twin():
    t, b, tiles, bands = place_in_mesh()
    return (t, b + 1 - 2 * lax.rem(b, 2))


def greet_axes():
    barrier = pltpu.get_barrier_semaphore()
    pl.semaphore_signal(barrier, inc=1, device_id=twin(), device_id_type=MESH)
    for axis in range(3):
        for k in (1, 2, 3):
            pl.semaphore_signal(barrier, inc=1, device_id=axis_peer(axis, k), device_id_type=MESH)


AXIS_PEERS = 10


def along(ref, unit, axis, v):
    hs, c = UNITS[unit]
    if axis == 0:
        return ref.at[hs, :, :, v, :, c]
    if axis == 1:
        return ref.at[hs, v, :, :, :, c]
    return ref.at[hs, :, lax.div(v, 2), :, lax.rem(v, 2), c]


def remote(src, dst, ss, rs, to):
    return pltpu.make_async_remote_copy(
        src_ref=src, dst_ref=dst, send_sem=ss, recv_sem=rs, device_id=to, device_id_type=MESH
    )


class Swap:
    def __init__(self, bufs, sems):
        self.bufs, self.sems = bufs, sems
        t, b, tiles, bands = place_in_mesh()
        self.place = spot(t, b)

    def core_copy(self, hs):
        me = self.place[3]
        src, dst = self.bufs[0], self.bufs[1]
        ss, rs = self.sems[0], self.sems[1]
        return remote(
            src.at[hs, :, :, :, :, 1 - me], dst.at[hs, :, :, :, :, me], ss.at[hs], rs.at[hs], twin()
        )

    def core_own(self, hs):
        me = self.place[3]
        src, dst = self.bufs[0], self.bufs[1]
        return pltpu.make_async_copy(src.at[hs, :, :, :, :, me], dst.at[hs, :, :, :, :, me], self.sems[2].at[hs])

    def core_start(self, hs):
        self.core_copy(hs).start()
        self.core_own(hs).start()

    def core_wait(self, hs):
        self.core_copy(hs).wait_recv()
        self.core_own(hs).wait()

    def hop(self, stage, u, k):
        axis = (u + stage) % 3
        me = self.place[axis]
        src, dst = self.bufs[1 + stage], self.bufs[2 + stage]
        return remote(
            along(src, u, axis, lax.rem(me + k, 4)), along(dst, u, axis, me),
            self.sems[3].at[stage, u, k - 1], self.sems[4].at[stage, u, k - 1], axis_peer(axis, k),
        )

    def own(self, stage, u):
        axis = (u + stage) % 3
        me = self.place[axis]
        src, dst = self.bufs[1 + stage], self.bufs[2 + stage]
        return pltpu.make_async_copy(along(src, u, axis, me), along(dst, u, axis, me), self.sems[5].at[stage, u])

    def start(self, stage, u):
        for k in (2, 1, 3):
            self.hop(stage, u, k).start()
        self.own(stage, u).start()

    def wait(self, stage, u):
        for k in (1, 2, 3):
            self.hop(stage, u, k).wait_recv()
        self.own(stage, u).wait()

    def first_stage(self):
        done = set()
        for u in range(8):
            hs = UNITS[u][0]
            if hs not in done:
                self.core_wait(hs)
                done.add(hs)
            self.start(0, u)

    def next_stage(self, stage):
        for u in range(8):
            self.wait(stage - 1, u)
            self.start(stage, u)

    def last_wait(self):
        for u in range(8):
            self.wait(2, u)

    def drain(self):
        for hs in range(4):
            self.core_copy(hs).wait_send()
        for stage in range(3):
            for u in range(8):
                for k in (1, 2, 3):
                    self.hop(stage, u, k).wait_send()


def swap_sems():
    dma = pltpu.SemaphoreType.DMA
    return [dma((4,)), dma((4,)), dma((4,)), dma((3, 8, 3)), dma((3, 8, 3)), dma((3, 8))]


def table_peer(stage, k):
    t, b, tiles, bands = place_in_mesh()
    x, y, z, core = spot(t, b)
    if stage == 0:
        return (t, lax.rem(b + k, 4))
    if stage == 1:
        return (t - x + lax.rem(x + k, 4), b)
    if stage == 2:
        return (t + 4 - 8 * lax.rem(lax.div(t, 4), 2), b)
    return (lax.rem(t + 8 * k, 32), b)


TABLE_PEERS = (3, 3, 1, 3)
TABLE_ROWS = (1, 4, 16, 32)


def table_copy(tab, ss, rs, stage, k):
    t, b, tiles, bands = place_in_mesh()
    n = TABLE_ROWS[stage]
    at = lax.div(t * 4 + b, n) * n
    rows = tab.at[pl.ds(at, n)]
    return pltpu.make_async_remote_copy(
        src_ref=rows, dst_ref=rows, send_sem=ss.at[stage, k - 1], recv_sem=rs.at[stage, k - 1],
        device_id=table_peer(stage, k), device_id_type=MESH,
    )


def table_start(tab, ss, rs, stage):
    for k in range(1, TABLE_PEERS[stage] + 1):
        table_copy(tab, ss, rs, stage, k).start()


def table_wait(tab, ss, rs, stage):
    for k in range(1, TABLE_PEERS[stage] + 1):
        table_copy(tab, ss, rs, stage, k).wait()


def greet_table():
    barrier = pltpu.get_barrier_semaphore()
    for stage in range(4):
        for k in range(1, TABLE_PEERS[stage] + 1):
            pl.semaphore_signal(barrier, inc=1, device_id=table_peer(stage, k), device_id_type=MESH)


def back_kernel(
    flip, tgt_ref, blk_ref, src_row, w_ref, g_ref, k1_ref, k2_ref, outgoing,
    hg_ref, k1t_ref, arrived, ids_ref, safe_ref, w_cells, ps_cells,
    tab, ext, send, recv, tmp, rim, trim, wide, k2t, b1, b2, b3, ss, rs, rss, rrs, tss, trs, *sems,
):
    d = 2
    swap = Swap((outgoing, b1, b2, b3, arrived), sems)
    t, b, tiles, bands = place_in_mesh()
    tab[t * 4 + b] = tgt_ref[...] * BLOCKS + blk_ref[...]
    me, before, after = flags(flip)
    ext[pl.ds(d, ROWS)] = g_ref[...]
    make_slab(ext, d, send, 0, me, tmp)
    clear_edges(ext, d)
    clear_groups(recv)
    greet_table()
    greet_axes()
    greet(sum(TABLE_PEERS) + AXIS_PEERS)
    table_start(tab, tss, trs, 0)
    start_sides(send, recv, ss, rs)
    start_rows(ext, d, rss, rrs)
    for hs in range(4):
        swap.core_start(hs)
    for i in range(3):
        for j in range(3):
            k2t[i, j * CH : (j + 1) * CH, :] = k2_ref[2 - i, 2 - j].T
    table_wait(tab, tss, trs, 0)
    table_start(tab, tss, trs, 1)
    swap.first_stage()
    wait_sides_recv(send, recv, ss, rs)
    wait_rows_recv(ext, d, rss, rrs)
    open_slab(recv, d, 0, me, rim)
    split_rim(rim, d, me, before, after, trim)
    widen(ext, d, rim, wide)
    table_wait(tab, tss, trs, 1)
    table_start(tab, tss, trs, 2)
    swap.next_stage(1)

    def block(n, carry):
        m = pl.multiple_of(n * STEP, STEP)
        hg_ref[pl.ds(m, STEP), :] = conv_block(wide, d, k2t, m, STEP)
        return carry

    lax.fori_loop(0, CELLS // STEP, block, 0)
    turned_part(trim, d, k2t, hg_ref)
    table_wait(tab, tss, trs, 2)
    table_start(tab, tss, trs, 3)
    swap.next_stage(2)
    for i in range(3):
        for j in range(3):
            k1t_ref[i, j * CH : (j + 1) * CH, :] = k1_ref[2 - i, 2 - j].T
    for n in range(SB):
        part = w_ref[n * 8 : (n + 1) * 8].reshape(128, BL).astype(F32)
        part = jnp.concatenate([part, part], axis=1).T
        w_cells[:, n * 128 : (n + 1) * 128] = part[0:BL].astype(BF16)
    spread = (
        lax.broadcasted_iota(jnp.int32, (PAIRS, PAIRS * BT), 1) // BT
        == lax.broadcasted_iota(jnp.int32, (PAIRS, PAIRS * BT), 0)
    ).astype(F32)
    own = jnp.broadcast_to(src_row[...], (8, PAIRS)).astype(F32)
    ps_cells[...] = jnp.dot(own.astype(BF16), spread.astype(BF16), preferred_element_type=F32)
    table_wait(tab, tss, trs, 3)
    table = tab[...].reshape(PAIRS, PAIRS).T
    order = lax.broadcasted_iota(jnp.int32, (PAIRS, PAIRS), 0)
    block_of = lax.bitwise_and(table, BLOCKS - 1)
    mine = lax.shift_right_logical(table, 6) == t * 4 + b
    first = jnp.min(jnp.where(mine, order, PAIRS), axis=0, keepdims=True)
    last = jnp.max(jnp.where(mine, order, -1), axis=0, keepdims=True)
    id_first = jnp.sum(jnp.where(order == first, block_of, 0), axis=0, keepdims=True)
    id_last = jnp.sum(jnp.where(order == last, block_of, 0), axis=0, keepdims=True)
    ids_ref[0:1, :] = jnp.where(first < PAIRS, id_first, BLOCKS)
    ids_ref[1:2, :] = jnp.where(last > first, id_last, BLOCKS)
    safe_ref[0:1, :] = id_first
    safe_ref[1:2, :] = id_last
    wait_sides_send(send, recv, ss, rs)
    wait_rows_send(ext, d, rss, rrs)
    swap.last_wait()
    swap.drain()


def back(flip, target, block, source, weights, grad, k1, k2, outgoing):
    d = 2
    return pl.pallas_call(
        back_kernel,
        name="hidden_adjoint",
        out_shape=(
            jax.ShapeDtypeStruct((CELLS, CH), F32),
            jax.ShapeDtypeStruct((3, 3 * CH, CH), BF16),
            jax.ShapeDtypeStruct(WORLD, BF16),
            jax.ShapeDtypeStruct((2, PAIRS), jnp.int32),
            jax.ShapeDtypeStruct((2, PAIRS), jnp.int32),
            jax.ShapeDtypeStruct((BL, PAIRS * BT), BF16),
            jax.ShapeDtypeStruct((8, PAIRS * BT), F32),
        ),
        in_specs=[SM] + [VM] * 8,
        out_specs=(VM,) * 7,
        scratch_shapes=[
            pltpu.VMEM((PAIRS, 1, PAIRS), jnp.int32),
            pltpu.VMEM((ROWS + 2 * d, COLS, CH), BF16),
            pltpu.VMEM((2, 16, CH), BF16),
            pltpu.VMEM((2, 3, 16, CH), BF16),
            pltpu.VMEM((2, 16, CH), F32),
            pltpu.VMEM((2, d, 16, CH), F32),
            pltpu.VMEM((2, d, 16, CH), F32),
            pltpu.VMEM(((ROWS + 2 * d) * COLS, 3 * CH), BF16),
            pltpu.VMEM((3, 3 * CH, CH), BF16),
            pltpu.VMEM(WORLD, BF16),
            pltpu.VMEM(WORLD, BF16),
            pltpu.VMEM(WORLD, BF16),
            pltpu.SemaphoreType.DMA((2, 3)),
            pltpu.SemaphoreType.DMA((2, 3)),
            pltpu.SemaphoreType.DMA((2,)),
            pltpu.SemaphoreType.DMA((2,)),
            pltpu.SemaphoreType.DMA((4, 3)),
            pltpu.SemaphoreType.DMA((4, 3)),
            *swap_sems(),
        ],
        compiler_params=pltpu.CompilerParams(vmem_limit_bytes=18 * 2**20, collective_id=1, has_side_effects=True),
        cost_estimate=pl.CostEstimate(flops=6 * 2**30, bytes_accessed=8 * 2**20, transcendentals=0),
    )(flip, target, block, source, weights, grad, k1, k2, outgoing)


def mid_kernel(
    flip, ids, slot, x_ref, hg_ref, g_ref, k1_ref, k1t_ref, k2_ref, w_ref, ps_ref,
    mixed_ref, out_ref, source_ref,
    ext, exth, extp, send, recv, send2, recv2, tmp, rim, rim2, trim, wide1_ref, wide2_ref, widep, pg_ref, ing, rounded,
    b0, b1, b2, b3, b4, rows, wexp,
    acc, send1, recv1, sent2, got2, sent3, got3, got4,
    ss, rs, rss, rrs, ss2, rs2, rssh, rrsh, rssp, rrsp,
    s1, r1, s2, r2, s3, r3, s4, r4, s5, r5, s6, r6, s7, r7, *sems,
):
    swap = Swap((b0, b1, b2, b3, b4), sems)
    sums = Sums(out_ref, acc, send1, recv1, sent2, got2, sent3, got3, got4, (s1, r1, s2, r2, s3, r3, s4, r4, s5, r5, s6, r6, s7, r7))
    me, before, after = flags(flip)
    ext[pl.ds(1, ROWS)] = x_ref[...]
    make_slab(ext, 1, send, 0, me, tmp)
    clear_edges(ext, 1)
    clear_edges(exth, 2)
    clear_edges(extp, 1)
    clear_groups(recv)
    clear_groups(recv2)
    greet_axes()
    greet(AXIS_PEERS)
    start_sides(send, recv, ss, rs)
    start_rows(ext, 1, rss, rrs)
    wait_sides_recv(send, recv, ss, rs)
    wait_rows_recv(ext, 1, rss, rrs)
    open_slab(recv, 1, 0, me, rim)
    widen(ext, 1, rim, wide1_ref)

    def act(n, carry):
        m = pl.multiple_of(n * STEP, STEP)
        pre = conv_block(wide1_ref, 1, k1_ref, m, STEP)
        s = jax.nn.sigmoid(pre)
        hid = (pre * s).astype(BF16)
        grad = (hg_ref[pl.ds(m, STEP), :] * s * (1.0 + pre * (1.0 - s))).astype(BF16)
        for q in range(STEP // COLS):
            row = n * (STEP // COLS) + q
            exth[2 + row] = hid[q * COLS : (q + 1) * COLS]
            extp[1 + row] = grad[q * COLS : (q + 1) * COLS]
        pg_ref[pl.ds(m, STEP), :] = grad
        return carry

    lax.fori_loop(0, CELLS // STEP, act, 0)
    make_slab(extp, 1, send2, 16, me, tmp)
    make_slab(exth, 2, send2, 0, me, tmp)
    start_sides(send2, recv2, ss2, rs2)
    start_rows(extp, 1, rssp, rrsp)
    start_rows(exth, 2, rssh, rrsh)
    wait_sides_recv(send2, recv2, ss2, rs2)
    wait_rows_recv(extp, 1, rssp, rrsp)
    open_slab(recv2, 1, 16, me, rim)
    split_rim(rim, 1, me, before, after, trim)
    widen(extp, 1, rim, widep)

    def fold(n, carry):
        m = pl.multiple_of(n * STEP, STEP)
        ing[pl.ds(m, STEP), :] = g_ref[pl.ds(m, STEP), :].astype(F32) + conv_block(widep, 1, k1t_ref, m, STEP)
        return carry

    lax.fori_loop(0, CELLS // STEP, fold, 0)
    turned_part(trim, 1, k1t_ref, ing)
    for q in range(4):
        part = ing[q * 256 : (q + 1) * 256, :].astype(BF16)
        rounded[q * 16 : (q + 1) * 16] = part.reshape(16, BT, CH)

    for half in (0, 1):

        def pick(q, carry):
            block = rounded[ids[half, q]]
            y, zh, x = lax.div(q, 32), lax.rem(lax.div(q, 16), 2), lax.rem(lax.div(q, 4), 4)
            zl, c = lax.rem(lax.div(q, 2), 2), lax.rem(q, 2)
            b0[half, y, zh, x, zl, c] = block[:, 0:128]
            b0[2 + half, y, zh, x, zl, c] = block[:, 128:256]
            return carry

        lax.fori_loop(0, PAIRS, pick, 0, unroll=4)
        swap.core_start(half)
        swap.core_start(2 + half)
    wait_rows_recv(exth, 2, rssh, rrsh)
    open_slab(recv2, 2, 0, me, rim2)
    widen(exth, 2, rim2, wide2_ref)
    swap.first_stage()
    for o in range(3):
        acc[1, o] = lax.dot_general(
            wide2_ref[o * 2 * COLS : o * 2 * COLS + CELLS, :],
            g_ref[...],
            (((0,), (0,)), ((), ())),
            preferred_element_type=F32,
        )
        acc[0, o] = lax.dot_general(
            wide1_ref[o * COLS : o * COLS + CELLS, :],
            pg_ref[...],
            (((0,), (0,)), ((), ())),
            preferred_element_type=F32,
        )
        sums.start(o)
    sums.to_second()
    swap.next_stage(1)

    def block(n, carry):
        m = pl.multiple_of(n * STEP, STEP)
        mixed_ref[pl.ds(m, STEP), :] = (
            x_ref[pl.ds(m // COLS, STEP // COLS)].reshape(STEP, CH).astype(F32)
            + conv_block(wide2_ref, 2, k2_ref, m, STEP)
        ).astype(BF16)
        return carry

    lax.fori_loop(0, CELLS // STEP, block, 0)
    w = w_ref[...]
    ps = ps_ref[0:1, :]
    for n in range(SB):
        wexp[n * BL : (n + 1) * BL, :] = w * (ps == n).astype(F32).astype(BF16)
    sums.to_third()
    swap.next_stage(2)
    sums.to_fourth()
    sums.to_fifth()
    sums.to_sixth()
    swap.last_wait()

    def take(p, carry):
        q = slot[p]
        half, t = lax.div(q, PAIRS), lax.rem(q, PAIRS)
        y, zh, x = lax.div(t, 32), lax.rem(lax.div(t, 16), 2), lax.rem(lax.div(t, 4), 4)
        zl, c = lax.rem(lax.div(t, 2), 2), lax.rem(t, 2)
        at = pl.ds(pl.multiple_of(p * BT, BT), BT)
        rows[at, 0:128] = b4[half, y, zh, x, zl, c]
        rows[at, 128:256] = b4[2 + half, y, zh, x, zl, c]
        return carry

    lax.fori_loop(0, PAIRS, take, 0, unroll=4)
    for m in range(4):
        source_ref[m * 256 : (m + 1) * 256, :] = jnp.dot(
            wexp[m * 256 : (m + 1) * 256, :], rows[...], preferred_element_type=F32
        ).astype(BF16)
    sums.to_seventh()
    sums.finish()
    wait_sides_send(send, recv, ss, rs)
    wait_rows_send(ext, 1, rss, rrs)
    wait_sides_send(send2, recv2, ss2, rs2)
    wait_rows_send(exth, 2, rssh, rrsh)
    wait_rows_send(extp, 1, rssp, rrsp)
    swap.drain()


def mid(flip, ids, slot, x, hidden_grad, grad, k1, k1t, k2, w_cells, ps_cells):
    dma = pltpu.SemaphoreType.DMA
    three, nine = [dma((3,))] * 2, [dma((3, 3))] * 2
    return pl.pallas_call(
        mid_kernel,
        name="middle",
        out_shape=(
            jax.ShapeDtypeStruct((CELLS, CH), BF16),
            jax.ShapeDtypeStruct((2, 3, PART, CH), BF16),
            jax.ShapeDtypeStruct((SB * BL, CH), BF16),
        ),
        in_specs=[SM, SM, SM] + [VM] * 8,
        out_specs=(VM, VM, VM),
        scratch_shapes=[
            pltpu.VMEM((ROWS + 2, COLS, CH), BF16),
            pltpu.VMEM((ROWS + 4, COLS, CH), BF16),
            pltpu.VMEM((ROWS + 2, COLS, CH), BF16),
            pltpu.VMEM((2, 16, CH), BF16),
            pltpu.VMEM((2, 3, 16, CH), BF16),
            pltpu.VMEM((2, 32, CH), BF16),
            pltpu.VMEM((2, 3, 32, CH), BF16),
            pltpu.VMEM((2, 16, CH), F32),
            pltpu.VMEM((2, 1, 16, CH), F32),
            pltpu.VMEM((2, 2, 16, CH), F32),
            pltpu.VMEM((2, 1, 16, CH), F32),
            pltpu.VMEM(((ROWS + 2) * COLS, 3 * CH), BF16),
            pltpu.VMEM(((ROWS + 4) * COLS, 3 * CH), BF16),
            pltpu.VMEM(((ROWS + 2) * COLS, 3 * CH), BF16),
            pltpu.VMEM((CELLS, CH), BF16),
            pltpu.VMEM((CELLS, CH), F32),
            pltpu.VMEM((BLOCKS, BT, CH), BF16),
            *[pltpu.VMEM(WORLD, BF16)] * 5,
            pltpu.VMEM((PAIRS * BT, CH), BF16),
            pltpu.VMEM((SB * BL, PAIRS * BT), BF16),
            pltpu.VMEM((2, 3, PART, CH), F32),
            pltpu.VMEM((3, PART, CH), BF16),
            pltpu.VMEM((3, PART, CH), BF16),
            pltpu.VMEM((3, PART, CH), BF16),
            pltpu.VMEM((3, 3, 192, CH), BF16),
            pltpu.VMEM((3, 192, CH), BF16),
            pltpu.VMEM((3, 3, 48, CH), BF16),
            pltpu.VMEM((3, 4, 48, CH), BF16),
            dma((2, 3)), dma((2, 3)), dma((2,)), dma((2,)),
            dma((2, 3)), dma((2, 3)), dma((2,)), dma((2,)), dma((2,)), dma((2,)),
            *three, *nine, *nine, *nine, *nine, *nine, *three,
            *swap_sems(),
        ],
        compiler_params=pltpu.CompilerParams(vmem_limit_bytes=42 * 2**20, collective_id=2, has_side_effects=True),
        cost_estimate=pl.CostEstimate(flops=6 * 2**30, bytes_accessed=12 * 2**20, transcendentals=2**18),
    )(flip, ids, slot, x, hidden_grad, grad, k1, k1t, k2, w_cells, ps_cells)


PART = 3 * CH


def axes_of(o):
    return o, (o + 1) % 3, (o + 2) % 3


class Sums:
    def __init__(self, out, acc, send1, recv1, sent2, got2, sent3, got3, got4, sems):
        self.out, self.acc, self.send1, self.recv1 = out, acc, send1, recv1
        self.sent2, self.got2, self.sent3, self.got3, self.got4, self.sems = sent2, got2, sent3, got3, got4, sems
        t, b, tiles, bands = place_in_mesh()
        self.place = spot(t, b)
        self.core = self.place[3]

    def first(self, o):
        s, r = self.sems[0:2]
        return remote(self.send1.at[o], self.recv1.at[o], s.at[o], r.at[o], twin())

    def second(self, o, k):
        s, r = self.sems[2:4]
        a = axes_of(o)[0]
        at = pl.ds(pl.multiple_of(lax.rem(self.place[a] + k, 4) * 192, 64), 192)
        return remote(self.sent2.at[o, at], self.got2.at[o, k - 1], s.at[o, k - 1], r.at[o, k - 1], axis_peer(a, k))

    def third(self, o, k):
        s, r = self.sems[4:6]
        a = axes_of(o)[1]
        at = pl.ds(pl.multiple_of(lax.rem(self.place[a] + k, 4) * 48, 16), 48)
        return remote(self.sent3.at[o, at], self.got3.at[o, k - 1], s.at[o, k - 1], r.at[o, k - 1], axis_peer(a, k))

    def fourth(self, o, k):
        s, r = self.sems[6:8]
        a = axes_of(o)[2]
        mine = self.got4.at[o, self.place[a]]
        return remote(mine, mine, s.at[o, k - 1], r.at[o, k - 1], axis_peer(a, k))

    def rows(self, o, wide):
        a, c, _ = axes_of(o)
        if wide:
            return pl.ds(pl.multiple_of(self.place[a] * 192, 64), 192)
        return pl.ds(pl.multiple_of(self.place[a] * 192 + self.place[c] * 48, 16), 48)

    def fifth(self, o, k):
        s, r = self.sems[8:10]
        rows = self.out.at[self.core, o, self.rows(o, False)]
        return remote(rows, rows, s.at[o, k - 1], r.at[o, k - 1], axis_peer(axes_of(o)[1], k))

    def sixth(self, o, k):
        s, r = self.sems[10:12]
        rows = self.out.at[self.core, o, self.rows(o, True)]
        return remote(rows, rows, s.at[o, k - 1], r.at[o, k - 1], axis_peer(axes_of(o)[0], k))

    def seventh(self, o):
        s, r = self.sems[12:14]
        whole = self.out.at[self.core, o]
        return remote(whole, whole, s.at[o], r.at[o], twin())

    def start(self, o):
        self.send1[o] = self.acc[1 - self.core, o].astype(BF16)
        self.first(o).start()

    def to_second(self):
        for o in range(3):
            self.first(o).wait_recv()
            total = self.acc[self.core, o] + self.recv1[o].astype(F32)
            self.acc[self.core, o] = total
            self.sent2[o] = total.astype(BF16)
            for k in (2, 1, 3):
                self.second(o, k).start()

    def to_third(self):
        for o in range(3):
            for k in (1, 2, 3):
                self.second(o, k).wait_recv()
            total = self.acc[self.core, o, self.rows(o, True), :]
            for k in (1, 2, 3):
                total = total + self.got2[o, k - 1].astype(F32)
            self.acc[self.core, o, 0:192, :] = total
            self.sent3[o] = total.astype(BF16)
            for k in (2, 1, 3):
                self.third(o, k).start()

    def to_fourth(self):
        for o in range(3):
            a, c, e = axes_of(o)
            for k in (1, 2, 3):
                self.third(o, k).wait_recv()
            total = self.acc[self.core, o, pl.ds(pl.multiple_of(self.place[c] * 48, 16), 48), :]
            for k in (1, 2, 3):
                total = total + self.got3[o, k - 1].astype(F32)
            self.got4[o, self.place[e]] = total.astype(BF16)
            for k in (2, 1, 3):
                self.fourth(o, k).start()

    def to_fifth(self):
        for o in range(3):
            for k in (1, 2, 3):
                self.fourth(o, k).wait_recv()
            v = [self.got4[o, q].astype(F32) for q in range(4)]
            self.out[self.core, o, self.rows(o, False), :] = (((v[0] + v[1]) + v[2]) + v[3]).astype(BF16)
            for k in (2, 1, 3):
                self.fifth(o, k).start()

    def to_sixth(self):
        for o in range(3):
            for k in (1, 2, 3):
                self.fifth(o, k).wait_recv()
            for k in (2, 1, 3):
                self.sixth(o, k).start()

    def to_seventh(self):
        for o in range(3):
            for k in (1, 2, 3):
                self.sixth(o, k).wait_recv()
            self.seventh(o).start()

    def finish(self):
        for o in range(3):
            self.seventh(o).wait_recv()
        for o in range(3):
            self.first(o).wait_send()
            self.seventh(o).wait_send()
            for k in (1, 2, 3):
                for step in (self.second, self.third, self.fourth, self.fifth, self.sixth):
                    step(o, k).wait_send()


def finish_kernel(sums, mixed, source, one, two, mixed_out, source_out, wide, sems):
    copies = [
        pltpu.make_async_copy(mixed, mixed_out, sems.at[6]),
        pltpu.make_async_copy(source, source_out, sems.at[7]),
    ]
    for copy in copies:
        copy.start()
    for n, out in ((0, one), (1, two)):
        for i in range(3):
            wide[n, i] = sums[n, i].astype(F32)
            copy = pltpu.make_async_copy(wide.at[n, i], out.at[i], sems.at[n * 3 + i])
            copy.start()
            copies.append(copy)
    for copy in copies:
        copy.wait()


def finish(sums, mixed, source):
    away = pl.BlockSpec(memory_space=pltpu.HBM)
    return pl.pallas_call(
        finish_kernel,
        name="finish",
        out_shape=(
            jax.ShapeDtypeStruct((3, PART, CH), F32),
            jax.ShapeDtypeStruct((3, PART, CH), F32),
            jax.ShapeDtypeStruct((CELLS, CH), BF16),
            jax.ShapeDtypeStruct((SB * BL, CH), BF16),
        ),
        in_specs=[VM] * 3,
        out_specs=(away,) * 4,
        scratch_shapes=[pltpu.VMEM((2, 3, PART, CH), F32), pltpu.SemaphoreType.DMA((8,))],
        compiler_params=params(),
        cost_estimate=pl.CostEstimate(flops=2**20, bytes_accessed=8 * 2**20, transcendentals=0),
    )(sums, mixed, source)


def local(
    source_cells, regrid_weights, pair_target, pair_block, pair_source, flip_codes, kernel_one, kernel_two, out_grad
):
    target = pair_target[:, 0]
    outgoing, slot = regrid(target, pair_source, regrid_weights, source_cells)
    upstream = out_grad[0]
    hidden_grad, k1_back, arrived, ids, safe_ids, w_cells, ps_cells = back(
        flip_codes,
        pair_target.reshape(1, PAIRS),
        pair_block.reshape(1, PAIRS),
        pair_source.reshape(1, PAIRS),
        regrid_weights,
        upstream,
        kernel_one,
        kernel_two,
        outgoing.reshape(WORLD),
    )
    regridded = gather_sum(ids, arrived.reshape(2, 2 * PAIRS, BT, 128))
    mixed, sums, source_grad = mid(
        flip_codes,
        safe_ids,
        slot,
        regridded.reshape(ROWS, COLS, CH),
        hidden_grad,
        upstream.reshape(CELLS, CH),
        kernel_one.reshape(3, PART, CH),
        k1_back,
        kernel_two.reshape(3, PART, CH),
        w_cells,
        ps_cells,
    )
    one, two, mixed, source_grad = finish(sums, mixed, source_grad)
    return (
        mixed.reshape(1, ROWS, COLS, CH),
        one.reshape(3, 3, CH, CH),
        two.reshape(3, 3, CH, CH),
        source_grad,
    )


def solution(mesh):
    placed = (
        P(("tile", "band"), None),
        P(("tile", "band"), None, None),
        P(("tile", "band"), None),
        P(("tile", "band")),
        P(("tile", "band")),
        P(),
        P(),
        P(),
        P("tile", "band", None, None),
    )
    return jax.shard_map(
        local,
        mesh=mesh,
        in_specs=placed,
        out_specs=(P("tile", "band", None, None), P(), P(), P(("tile", "band"), None)),
        check_vma=False,
    )
```

```python
import jax
import jax.numpy as jnp
from jax import lax
from jax.experimental import pallas as pl
from jax.experimental.pallas import tpu as pltpu
from jax.sharding import PartitionSpec as P

F32 = jnp.float32
BF16 = jnp.bfloat16
MESH = pl.DeviceIdType.MESH
VM = pl.BlockSpec(memory_space=pltpu.VMEM)
SM = pl.BlockSpec(memory_space=pltpu.SMEM)
FAR = pl.BlockSpec(memory_space=pltpu.HBM)
LIMIT = 16 * 2**20
ROWS, COLS, CH = 8, 128, 256
PAIRS, BT, BL, SB, BLOCKS = 128, 16, 64, 16, 64
CELLS = ROWS * COLS


def params(**more):
    return pltpu.CompilerParams(vmem_limit_bytes=LIMIT, **more)


def regrid_kernel(tgt_far, psrc_far, w_ref, src_far, out_ref, slot_ref, cnt, masks, wexp, tgt, psrc, src_ref, sems):
    copies = [
        pltpu.make_async_copy(tgt_far, tgt, sems.at[0]),
        pltpu.make_async_copy(psrc_far, psrc, sems.at[1]),
        pltpu.make_async_copy(src_far, src_ref, sems.at[2]),
    ]
    for copy in copies:
        copy.start()
    lane = lax.broadcasted_iota(jnp.int32, (BT, 128), 1)
    masks[0] = (lane < BL).astype(F32).astype(BF16)
    masks[1] = (lane >= BL).astype(F32).astype(BF16)
    wexp[...] = jnp.zeros_like(wexp)

    def clear(i, c):
        cnt[i] = 0
        return c

    lax.fori_loop(0, PAIRS, clear, 0, unroll=8)
    copies[0].wait()
    copies[1].wait()

    def place(p, c):
        t = tgt[p]
        r = cnt[t]
        cnt[t] = r + 1
        slot_ref[p] = jnp.minimum(r, 1) * PAIRS + t
        s = psrc[p]
        w = w_ref[p]
        ww = jnp.concatenate([w, w], axis=1) * masks[lax.rem(s, 2)]
        row = pl.multiple_of(p * BT, BT)
        col = pl.multiple_of((s // 2) * 128, 128)
        wexp[pl.ds(row, BT), pl.ds(col, 128)] = ww
        return c

    lax.fori_loop(0, PAIRS, place, 0, unroll=8)
    copies[2].wait()
    for m in range(4):
        part = jnp.dot(wexp[m * 512 : (m + 1) * 512, :], src_ref[...], preferred_element_type=F32).astype(BF16)
        for q in range(32):
            at = slot_ref[m * 32 + q]
            for h in (0, 1):
                out_ref[h, at] = part[q * BT : (q + 1) * BT, h * 128 : (h + 1) * 128]


def regrid(tgt, psrc, weights, source):
    return pl.pallas_call(
        regrid_kernel,
        name="regrid",
        out_shape=(
            jax.ShapeDtypeStruct((2, 2 * PAIRS, BT, 128), BF16),
            jax.ShapeDtypeStruct((PAIRS,), jnp.int32),
        ),
        in_specs=[FAR, FAR, VM, FAR],
        out_specs=(VM, SM),
        scratch_shapes=[
            pltpu.SMEM((PAIRS,), jnp.int32),
            pltpu.VMEM((2, BT, 128), BF16),
            pltpu.VMEM((PAIRS * BT, SB * BL), BF16),
            pltpu.SMEM((PAIRS,), jnp.int32),
            pltpu.SMEM((PAIRS,), jnp.int32),
            pltpu.VMEM((SB * BL, CH), BF16),
            pltpu.SemaphoreType.DMA((3,)),
        ],
        compiler_params=params(),
        cost_estimate=pl.CostEstimate(flops=2 * 2048 * 1024 * 256, bytes_accessed=6 * 2**20, transcendentals=0),
    )(tgt, psrc, weights, source)


def gather_sum_kernel(ids, got_ref, out_ref, acc, more):
    acc[...] = jnp.zeros_like(acc)
    more[...] = jnp.zeros_like(more)

    def add(q, c):
        k, n = ids[0, q], ids[1, q]
        for h in (0, 1):
            acc[h, k] += got_ref[h, q].astype(F32)
            more[h, n] += got_ref[h, PAIRS + q].astype(F32)
        return c

    lax.fori_loop(0, PAIRS, add, 0, unroll=8)
    for h in (0, 1):
        out_ref[:, :, h * 128 : (h + 1) * 128] = (acc[h, 0:BLOCKS] + more[h, 0:BLOCKS]).astype(BF16)


def gather_sum(ids, arrived):
    return pl.pallas_call(
        gather_sum_kernel,
        name="gather_sum",
        out_shape=jax.ShapeDtypeStruct((BLOCKS, BT, CH), BF16),
        in_specs=[SM, VM],
        out_specs=VM,
        scratch_shapes=[pltpu.VMEM((2, BLOCKS + 1, BT, 128), F32)] * 2,
        compiler_params=params(),
        cost_estimate=pl.CostEstimate(flops=2**21, bytes_accessed=3 * 2**20, transcendentals=0),
    )(ids, arrived)


def place_in_mesh():
    return lax.axis_index("tile"), lax.axis_index("band"), lax.axis_size("tile"), lax.axis_size("band")


def greet():
    t, b, tiles, bands = place_in_mesh()
    barrier = pltpu.get_barrier_semaphore()
    for dt in (1, -1, 0):
        for db in (-1, 0, 1):
            if dt == 0 and db == 0:
                continue

            def say(dt=dt, db=db):
                pl.semaphore_signal(
                    barrier, inc=1, device_id=(lax.rem(t + dt + tiles, tiles), b + db), device_id_type=MESH
                )

            near_band(b, bands, db, say)


def greet_wait(others):
    b, bands = lax.axis_index("band"), lax.axis_size("band")
    near = 2 + jnp.where(b > 0, 3, 0) + jnp.where(b < bands - 1, 3, 0)
    pl.semaphore_wait(pltpu.get_barrier_semaphore(), near + others)


def near_band(b, bands, db, action):
    if db == 0:
        action()
    elif db < 0:
        pl.when(b > 0)(action)
    else:
        pl.when(b < bands - 1)(action)


def side_copy(send, recv, ss, rs, way, db, group):
    t, b, tiles, bands = place_in_mesh()
    to = lax.rem(t + (1 if way == 0 else tiles - 1), tiles)
    return pltpu.make_async_remote_copy(
        src_ref=send.at[way],
        dst_ref=recv.at[way, group],
        send_sem=ss.at[way, 1 + db],
        recv_sem=rs.at[way, group],
        device_id=(to, b + db),
        device_id_type=MESH,
    )


def row_copy(ext, d, ss, rs, db):
    t, b, tiles, bands = place_in_mesh()
    if db < 0:
        src, dst, k = ext.at[pl.ds(d, d)], ext.at[pl.ds(ROWS + d, d)], 0
    else:
        src, dst, k = ext.at[pl.ds(ROWS, d)], ext.at[pl.ds(0, d)], 1
    return pltpu.make_async_remote_copy(
        src_ref=src, dst_ref=dst, send_sem=ss.at[k], recv_sem=rs.at[k], device_id=(t, b + db), device_id_type=MESH
    )


def start_sides(send, recv, ss, rs):
    b, bands = lax.axis_index("band"), lax.axis_size("band")
    for way in (0, 1):
        for db in (0, -1, 1):
            near_band(b, bands, db, lambda way=way, db=db: side_copy(send, recv, ss, rs, way, db, 1 - db).start())


def start_rows(ext, d, ss, rs):
    b, bands = lax.axis_index("band"), lax.axis_size("band")
    for db in (-1, 1):
        near_band(b, bands, db, lambda db=db: row_copy(ext, d, ss, rs, db).start())


def wait_sides_recv(send, recv, ss, rs):
    b, bands = lax.axis_index("band"), lax.axis_size("band")
    for way in (0, 1):
        for db in (0, -1, 1):
            near_band(b, bands, db, lambda way=way, db=db: side_copy(send, recv, ss, rs, way, 0, 1 + db).wait_recv())


def wait_sides_send(send, recv, ss, rs):
    b, bands = lax.axis_index("band"), lax.axis_size("band")
    for way in (0, 1):
        for db in (0, -1, 1):
            near_band(b, bands, db, lambda way=way, db=db: side_copy(send, recv, ss, rs, way, db, 1 - db).wait_send())


def wait_rows_recv(ext, d, ss, rs):
    b, bands = lax.axis_index("band"), lax.axis_size("band")
    near_band(b, bands, -1, lambda: row_copy(ext, d, ss, rs, 1).wait_recv())
    near_band(b, bands, 1, lambda: row_copy(ext, d, ss, rs, -1).wait_recv())


def wait_rows_send(ext, d, ss, rs):
    b, bands = lax.axis_index("band"), lax.axis_size("band")
    for db in (-1, 1):
        near_band(b, bands, db, lambda db=db: row_copy(ext, d, ss, rs, db).wait_send())


def clear_edges(ext, d):
    b, bands = lax.axis_index("band"), lax.axis_size("band")

    @pl.when(b == 0)
    def _():
        ext[0:d] = jnp.zeros((d, COLS, CH), BF16)

    @pl.when(b == bands - 1)
    def _():
        ext[ROWS + d : ROWS + 2 * d] = jnp.zeros((d, COLS, CH), BF16)


def clear_groups(recv):
    b, bands = lax.axis_index("band"), lax.axis_size("band")
    for way in (0, 1):

        @pl.when(b == 0)
        def _():
            recv[way, 0] = jnp.zeros(recv.shape[2:], BF16)

        @pl.when(b == bands - 1)
        def _():
            recv[way, 2] = jnp.zeros(recv.shape[2:], BF16)


def flags(flip):
    t, b, tiles, bands = place_in_mesh()
    me = flip[t]
    before = flip[lax.rem(t + tiles - 1, tiles)]
    after = flip[lax.rem(t + 1, tiles)]
    return me, before, after


def make_slab(ext, d, send, base, flip_me, tmp):
    if d == 1:
        tmp[...] = jnp.zeros_like(tmp)
    for r in range(ROWS):
        first = ext[d + r, 0:16, :].astype(F32)
        last = ext[d + r, COLS - 16 : COLS, :].astype(F32)
        for k in range(d):
            tmp[0, k * 8 + r : k * 8 + r + 1, :] = first[k : k + 1]
            tmp[1, k * 8 + r : k * 8 + r + 1, :] = last[15 - k : 16 - k]
    turned = jnp.full((16, CH), flip_me, jnp.int32) == 1
    left, right = tmp[0], tmp[1]
    send[0, base : base + 16] = jnp.where(turned, left, right).astype(BF16)
    send[1, base : base + 16] = jnp.where(turned, right, left).astype(BF16)


def open_slab(recv, d, base, flip_me, rim):
    turned = jnp.full((16, CH), flip_me, jnp.int32) == 1
    for g in range(3):
        before = recv[0, g, base : base + 16].astype(F32)
        after = recv[1, g, base : base + 16].astype(F32)
        sides = (jnp.where(turned, after, before), jnp.where(turned, before, after))
        for side in (0, 1):
            for k in range(d):
                part = sides[side][k * 8 : k * 8 + 8]
                if g == 0:
                    rim[side, k, 0:d, :] = part[8 - d :]
                elif g == 1:
                    rim[side, k, d : d + 8, :] = part
                else:
                    rim[side, k, d + 8 : 2 * d + 8, :] = part[:d]


def split_rim(rim, d, flip_me, flip_before, flip_after, turned_rim):
    odd_before = (flip_before != flip_me).astype(jnp.int32)
    odd_after = (flip_after != flip_me).astype(jnp.int32)
    odd_left = jnp.where(flip_me == 0, odd_before, odd_after)
    odd_right = jnp.where(flip_me == 0, odd_after, odd_before)
    for side, odd in ((0, odd_left), (1, odd_right)):
        mask = jnp.full((16, CH), odd, jnp.int32) == 1
        for k in range(d):
            whole = rim[side, k]
            turned_rim[side, k] = jnp.where(mask, whole, 0.0)
            rim[side, k] = jnp.where(mask, 0.0, whole)


def widen(ext, d, rim, wide):
    col = lax.broadcasted_iota(jnp.int32, (COLS, CH), 0)

    def one(row, carry):
        mid = ext[row]
        x = mid.astype(F32)
        left = pltpu.roll(x, d, 0)
        right = pltpu.roll(x, COLS - d, 0)
        for k in range(d):
            near = jnp.broadcast_to(rim[0, k, pl.ds(row, 1), :], (COLS, CH))
            left = jnp.where(col == d - 1 - k, near, left)
            near = jnp.broadcast_to(rim[1, k, pl.ds(row, 1), :], (COLS, CH))
            right = jnp.where(col == COLS - d + k, near, right)
        at = pl.ds(pl.multiple_of(row * COLS, COLS), COLS)
        wide[at, 0:CH] = left.astype(BF16)
        wide[at, CH : 2 * CH] = mid
        wide[at, 2 * CH : 3 * CH] = right.astype(BF16)
        return carry

    lax.fori_loop(0, ROWS + 2 * d, one, 0)


def widen_own(ext, wide, first, count):
    col = lax.broadcasted_iota(jnp.int32, (COLS, CH), 0)

    def one(row, carry):
        mid = ext[row]
        x = mid.astype(F32)
        left = jnp.where(col == 0, 0.0, pltpu.roll(x, 1, 0))
        right = jnp.where(col == COLS - 1, 0.0, pltpu.roll(x, COLS - 1, 0))
        at = pl.ds(pl.multiple_of(row * COLS, COLS), COLS)
        wide[at, 0:CH] = left.astype(BF16)
        wide[at, CH : 2 * CH] = mid
        wide[at, 2 * CH : 3 * CH] = right.astype(BF16)
        return carry

    lax.fori_loop(first, first + count, one, 0)


def side_part(rim, turned_rim, taps, out):
    total = None
    none = jnp.zeros((ROWS, CH), F32)
    for i in range(3):
        near = [rim[side, 0, i : i + ROWS, :] for side in (0, 1)]
        turned = [none, none] if turned_rim is None else [turned_rim[side, 0, i : i + ROWS, :] for side in (0, 1)]
        lhs = jnp.concatenate(
            [
                jnp.concatenate([near[0], none, turned[0]], axis=1),
                jnp.concatenate([turned[1], none, near[1]], axis=1),
            ],
            axis=0,
        )
        part = jnp.dot(lhs.astype(BF16), taps[i], preferred_element_type=F32)
        total = part if total is None else total + part
    for r in range(ROWS):
        at = r * COLS
        out[at : at + 1, :] += total[r : r + 1]
        at = r * COLS + COLS - 1
        out[at : at + 1, :] += total[ROWS + r : ROWS + r + 1]


def patch_sides(wide, rim):
    row = lax.broadcasted_iota(jnp.int32, (16, CH), 0)
    for r in range(ROWS + 2):
        at = r * COLS
        tile = wide[at : at + 16, 0:CH].astype(F32)
        near = jnp.broadcast_to(rim[0, 0, r : r + 1, :], (16, CH))
        wide[at : at + 16, 0:CH] = jnp.where(row == 0, near, tile).astype(BF16)
        at = r * COLS + COLS - 16
        tile = wide[at : at + 16, 2 * CH : 3 * CH].astype(F32)
        near = jnp.broadcast_to(rim[1, 0, r : r + 1, :], (16, CH))
        wide[at : at + 16, 2 * CH : 3 * CH] = jnp.where(row == 15, near, tile).astype(BF16)


def conv_block(wide, d, taps, m, rows):
    total = None
    for i in range(3):
        lhs = wide[pl.ds(pl.multiple_of(m + i * d * COLS, COLS), rows), :]
        part = jnp.dot(lhs, taps[i], preferred_element_type=F32)
        total = part if total is None else total + part
    return total


def turned_part(turned_rim, d, taps, out):
    left, right = None, None
    for i in range(3):
        lhs_left = jnp.concatenate([turned_rim[0, d - 1 - c, i * d : i * d + 8, :] for c in range(d)], axis=0)
        lhs_right = jnp.concatenate([turned_rim[1, c, i * d : i * d + 8, :] for c in range(d)], axis=0)
        a = jnp.dot(lhs_left.astype(BF16), taps[i, 2 * CH : 3 * CH, :], preferred_element_type=F32)
        z = jnp.dot(lhs_right.astype(BF16), taps[i, 0:CH, :], preferred_element_type=F32)
        left = a if left is None else left + a
        right = z if right is None else right + z
    for c in range(d):
        for r in range(ROWS):
            at = r * COLS + c
            out[at : at + 1, :] += left[c * 8 + r : c * 8 + r + 1]
            at = r * COLS + COLS - d + c
            out[at : at + 1, :] += right[c * 8 + r : c * 8 + r + 1]


STEP = 256


def spot(t, b):
    x = lax.rem(t, 4)
    y = lax.div(t, 8)
    z = lax.rem(lax.div(t, 4), 2) * 2 + lax.div(b, 2)
    return x, y, z, lax.rem(b, 2)


def device_at(x, y, z, core):
    return (y * 8 + lax.div(z, 2) * 4 + x, lax.rem(z, 2) * 2 + core)


WORLD = (4, 4, 2, 4, 2, 2, BT, 128)
UNITS = [(hs, c) for c in (0, 1) for hs in range(4)]


def axis_peer(axis, k):
    t, b, tiles, bands = place_in_mesh()
    at = list(spot(t, b))
    at[axis] = lax.rem(at[axis] + k, 4)
    return device_at(*at)


def twin():
    t, b, tiles, bands = place_in_mesh()
    return (t, b + 1 - 2 * lax.rem(b, 2))


def greet_axes():
    barrier = pltpu.get_barrier_semaphore()
    pl.semaphore_signal(barrier, inc=1, device_id=twin(), device_id_type=MESH)
    for axis in range(3):
        for k in (1, 2, 3):
            pl.semaphore_signal(barrier, inc=1, device_id=axis_peer(axis, k), device_id_type=MESH)


AXIS_PEERS = 10


def along(ref, unit, axis, v):
    hs, c = UNITS[unit]
    if axis == 0:
        return ref.at[hs, :, :, v, :, c]
    if axis == 1:
        return ref.at[hs, v, :, :, :, c]
    return ref.at[hs, :, lax.div(v, 2), :, lax.rem(v, 2), c]


def remote(src, dst, ss, rs, to):
    return pltpu.make_async_remote_copy(
        src_ref=src, dst_ref=dst, send_sem=ss, recv_sem=rs, device_id=to, device_id_type=MESH
    )


class Swap:
    def __init__(self, bufs, sems):
        self.bufs, self.sems, self.come = bufs, sems, set()
        t, b, tiles, bands = place_in_mesh()
        self.place = spot(t, b)

    def core_copy(self, hs):
        me = self.place[3]
        src, dst = self.bufs[0], self.bufs[1]
        ss, rs = self.sems[0], self.sems[1]
        return remote(
            src.at[hs, :, :, :, :, 1 - me], dst.at[hs, :, :, :, :, me], ss.at[hs], rs.at[hs], twin()
        )

    def core_own(self, hs):
        me = self.place[3]
        src, dst = self.bufs[0], self.bufs[1]
        return pltpu.make_async_copy(src.at[hs, :, :, :, :, me], dst.at[hs, :, :, :, :, me], self.sems[2].at[hs])

    def core_start(self, hs):
        self.core_copy(hs).start()
        self.core_own(hs).start()

    def core_wait(self, hs):
        self.core_copy(hs).wait_recv()
        self.core_own(hs).wait()

    def hop(self, stage, u, k):
        axis = (u + stage) % 3
        me = self.place[axis]
        src, dst = self.bufs[1 + stage], self.bufs[2 + stage]
        return remote(
            along(src, u, axis, lax.rem(me + k, 4)), along(dst, u, axis, me),
            self.sems[3].at[stage, u, k - 1], self.sems[4].at[stage, u, k - 1], axis_peer(axis, k),
        )

    def own(self, stage, u):
        axis = (u + stage) % 3
        me = self.place[axis]
        src, dst = self.bufs[1 + stage], self.bufs[2 + stage]
        return pltpu.make_async_copy(along(src, u, axis, me), along(dst, u, axis, me), self.sems[5].at[stage, u])

    def start(self, stage, u):
        for k in (2, 1, 3):
            self.hop(stage, u, k).start()
        self.own(stage, u).start()

    def wait(self, stage, u):
        for k in (1, 2, 3):
            self.hop(stage, u, k).wait_recv()
        self.own(stage, u).wait()

    def advance(self, stage, u):
        if stage > 0:
            self.wait(stage - 1, u)
        elif UNITS[u][0] not in self.come:
            self.come.add(UNITS[u][0])
            self.core_wait(UNITS[u][0])
        self.start(stage, u)

    def first_stage(self):
        done = set()
        for u in range(8):
            hs = UNITS[u][0]
            if hs not in done:
                self.core_wait(hs)
                done.add(hs)
            self.start(0, u)

    def next_stage(self, stage):
        for u in range(8):
            self.wait(stage - 1, u)
            self.start(stage, u)

    def last_wait(self):
        for u in range(8):
            self.wait(2, u)

    def drain(self, *stages):
        for stage in stages:
            if stage == 0:
                for hs in range(4):
                    self.core_copy(hs).wait_send()
            for u in range(8):
                for k in (1, 2, 3):
                    self.hop(stage, u, k).wait_send()


def swap_sems():
    dma = pltpu.SemaphoreType.DMA
    return [dma((4,)), dma((4,)), dma((4,)), dma((3, 8, 3)), dma((3, 8, 3)), dma((3, 8))]


def table_peer(stage, k):
    t, b, tiles, bands = place_in_mesh()
    x, y, z, core = spot(t, b)
    if stage == 0:
        return (t, lax.rem(b + k, 4))
    if stage == 1:
        return (t - x + lax.rem(x + k, 4), b)
    if stage == 2:
        return (t + 4 - 8 * lax.rem(lax.div(t, 4), 2), b)
    return (lax.rem(t + 8 * k, 32), b)


TABLE_PEERS = (3, 3, 1, 3)
TABLE_ROWS = (1, 4, 16, 32)


def table_copy(tab, ss, rs, stage, k):
    t, b, tiles, bands = place_in_mesh()
    n = TABLE_ROWS[stage]
    at = lax.div(t * 4 + b, n) * n
    rows = tab.at[pl.ds(at, n)]
    return pltpu.make_async_remote_copy(
        src_ref=rows, dst_ref=rows, send_sem=ss.at[stage, k - 1], recv_sem=rs.at[stage, k - 1],
        device_id=table_peer(stage, k), device_id_type=MESH,
    )


def table_start(tab, ss, rs, stage):
    for k in range(1, TABLE_PEERS[stage] + 1):
        table_copy(tab, ss, rs, stage, k).start()


def table_wait(tab, ss, rs, stage):
    for k in range(1, TABLE_PEERS[stage] + 1):
        table_copy(tab, ss, rs, stage, k).wait()


def greet_table():
    barrier = pltpu.get_barrier_semaphore()
    for stage in range(4):
        for k in range(1, TABLE_PEERS[stage] + 1):
            pl.semaphore_signal(barrier, inc=1, device_id=table_peer(stage, k), device_id_type=MESH)


def back_kernel(
    flip, tgt_ref, blk_ref, src_row, w_ref, g_ref, k1_ref, k2_ref, outgoing,
    hg_ref, k1t_ref, arrived, ids_ref, safe_ref, w_cells, ps_cells,
    tab, ext, send, recv, tmp, rim, trim, wide, k2t, b1, b2, b3, ss, rs, rss, rrs, tss, trs, *sems,
):
    d = 2
    swap = Swap((outgoing, b1, b2, b3, arrived), sems)
    greet_table()
    greet_axes()
    greet()
    t, b, tiles, bands = place_in_mesh()
    tab[t * 4 + b] = tgt_ref[...] * BLOCKS + blk_ref[...]
    me, before, after = flags(flip)
    ext[pl.ds(d, ROWS)] = g_ref[...]
    make_slab(ext, d, send, 0, me, tmp)
    clear_edges(ext, d)
    clear_groups(recv)
    greet_wait(sum(TABLE_PEERS) + AXIS_PEERS)
    table_start(tab, tss, trs, 0)
    start_sides(send, recv, ss, rs)
    start_rows(ext, d, rss, rrs)
    for hs in range(4):
        swap.core_start(hs)
    for i in range(3):
        for j in range(3):
            k2t[i, j * CH : (j + 1) * CH, :] = k2_ref[2 - i, 2 - j].T
    table_wait(tab, tss, trs, 0)
    table_start(tab, tss, trs, 1)
    swap.first_stage()
    wait_sides_recv(send, recv, ss, rs)
    wait_rows_recv(ext, d, rss, rrs)
    open_slab(recv, d, 0, me, rim)
    split_rim(rim, d, me, before, after, trim)
    widen(ext, d, rim, wide)
    table_wait(tab, tss, trs, 1)
    table_start(tab, tss, trs, 2)
    swap.next_stage(1)

    def block(n, carry):
        m = pl.multiple_of(n * STEP, STEP)
        hg_ref[pl.ds(m, STEP), :] = conv_block(wide, d, k2t, m, STEP)
        return carry

    lax.fori_loop(0, CELLS // STEP, block, 0)
    turned_part(trim, d, k2t, hg_ref)
    table_wait(tab, tss, trs, 2)
    table_start(tab, tss, trs, 3)
    swap.next_stage(2)
    for i in range(3):
        for j in range(3):
            k1t_ref[i, j * CH : (j + 1) * CH, :] = k1_ref[2 - i, 2 - j].T
    for n in range(SB):
        part = w_ref[n * 8 : (n + 1) * 8].reshape(128, BL).astype(F32)
        part = jnp.concatenate([part, part], axis=1).T
        w_cells[:, n * 128 : (n + 1) * 128] = part[0:BL].astype(BF16)
    spread = (
        lax.broadcasted_iota(jnp.int32, (PAIRS, PAIRS * BT), 1) // BT
        == lax.broadcasted_iota(jnp.int32, (PAIRS, PAIRS * BT), 0)
    ).astype(F32)
    own = jnp.broadcast_to(src_row[...], (8, PAIRS)).astype(F32)
    ps_cells[...] = jnp.dot(own.astype(BF16), spread.astype(BF16), preferred_element_type=F32)
    table_wait(tab, tss, trs, 3)
    table = tab[...].reshape(PAIRS, PAIRS).T
    order = lax.broadcasted_iota(jnp.int32, (PAIRS, PAIRS), 0)
    block_of = lax.bitwise_and(table, BLOCKS - 1)
    mine = lax.shift_right_logical(table, 6) == t * 4 + b
    first = jnp.min(jnp.where(mine, order, PAIRS), axis=0, keepdims=True)
    last = jnp.max(jnp.where(mine, order, -1), axis=0, keepdims=True)
    id_first = jnp.sum(jnp.where(order == first, block_of, 0), axis=0, keepdims=True)
    id_last = jnp.sum(jnp.where(order == last, block_of, 0), axis=0, keepdims=True)
    ids_ref[0:1, :] = jnp.where(first < PAIRS, id_first, BLOCKS)
    ids_ref[1:2, :] = jnp.where(last > first, id_last, BLOCKS)
    safe_ref[0:1, :] = id_first
    safe_ref[1:2, :] = id_last
    wait_sides_send(send, recv, ss, rs)
    wait_rows_send(ext, d, rss, rrs)
    swap.drain(0, 1)
    swap.last_wait()
    swap.drain(2)


def back(flip, target, block, source, weights, grad, k1, k2, outgoing):
    d = 2
    return pl.pallas_call(
        back_kernel,
        name="hidden_adjoint",
        out_shape=(
            jax.ShapeDtypeStruct((CELLS, CH), F32),
            jax.ShapeDtypeStruct((3, 3 * CH, CH), BF16),
            jax.ShapeDtypeStruct(WORLD, BF16),
            jax.ShapeDtypeStruct((2, PAIRS), jnp.int32),
            jax.ShapeDtypeStruct((2, PAIRS), jnp.int32),
            jax.ShapeDtypeStruct((BL, PAIRS * BT), BF16),
            jax.ShapeDtypeStruct((8, PAIRS * BT), F32),
        ),
        in_specs=[SM] + [VM] * 8,
        out_specs=(VM,) * 7,
        scratch_shapes=[
            pltpu.VMEM((PAIRS, 1, PAIRS), jnp.int32),
            pltpu.VMEM((ROWS + 2 * d, COLS, CH), BF16),
            pltpu.VMEM((2, 16, CH), BF16),
            pltpu.VMEM((2, 3, 16, CH), BF16),
            pltpu.VMEM((2, 16, CH), F32),
            pltpu.VMEM((2, d, 16, CH), F32),
            pltpu.VMEM((2, d, 16, CH), F32),
            pltpu.VMEM(((ROWS + 2 * d) * COLS, 3 * CH), BF16),
            pltpu.VMEM((3, 3 * CH, CH), BF16),
            pltpu.VMEM(WORLD, BF16),
            pltpu.VMEM(WORLD, BF16),
            pltpu.VMEM(WORLD, BF16),
            pltpu.SemaphoreType.DMA((2, 3)),
            pltpu.SemaphoreType.DMA((2, 3)),
            pltpu.SemaphoreType.DMA((2,)),
            pltpu.SemaphoreType.DMA((2,)),
            pltpu.SemaphoreType.DMA((4, 3)),
            pltpu.SemaphoreType.DMA((4, 3)),
            *swap_sems(),
        ],
        compiler_params=pltpu.CompilerParams(vmem_limit_bytes=18 * 2**20, collective_id=1, has_side_effects=True),
        cost_estimate=pl.CostEstimate(flops=6 * 2**30, bytes_accessed=8 * 2**20, transcendentals=0),
    )(flip, target, block, source, weights, grad, k1, k2, outgoing)


ORDER = "H a012 K0 a345 K1 20 K2 21 a67 22 b012 30 b345 M b67 31 32 W c012 4012 c345 5012 c67 6012 x d01234567 S 7012 y"


def mid_kernel(
    flip, ids, slot, x_ref, hg_ref, g_ref, k1_ref, k1t_ref, k2_ref, w_ref, ps_ref,
    mixed_ref, out_ref, source_ref,
    ext, exth, extp, send, recv, send2, recv2, tmp, rim, rim2, trim, wide1_ref, wide2_ref, widep, pg_ref, ing, rounded,
    b0, b1, b2, b3, b4, rows, wexp,
    acc, send1, recv1, sent2, got2, sent3, got3, got4,
    ss, rs, rss, rrs, ss2, rs2, rssh, rrsh, rssp, rrsp,
    s1, r1, s2, r2, s3, r3, s4, r4, s5, r5, s6, r6, s7, r7, *sems,
):
    swap = Swap((b0, b1, b2, b3, b4), sems)
    sums = Sums(out_ref, acc, send1, recv1, sent2, got2, sent3, got3, got4, (s1, r1, s2, r2, s3, r3, s4, r4, s5, r5, s6, r6, s7, r7))
    greet_axes()
    greet()
    me, before, after = flags(flip)
    ext[pl.ds(1, ROWS)] = x_ref[...]
    make_slab(ext, 1, send, 0, me, tmp)
    clear_edges(ext, 1)
    clear_edges(exth, 2)
    clear_edges(extp, 1)
    clear_groups(recv)
    clear_groups(recv2)
    greet_wait(AXIS_PEERS)
    start_sides(send, recv, ss, rs)
    start_rows(ext, 1, rss, rrs)
    widen_own(ext, wide1_ref, 1, ROWS)

    def inner_pre(n, carry):
        m = pl.multiple_of(COLS + n * STEP, COLS)
        ing[pl.ds(m, STEP), :] = conv_block(wide1_ref, 1, k1_ref, m, STEP)
        return carry

    lax.fori_loop(0, 3, inner_pre, 0)
    wait_sides_recv(send, recv, ss, rs)
    wait_rows_recv(ext, 1, rss, rrs)
    open_slab(recv, 1, 0, me, rim)
    for edge in (0, ROWS - 1):
        widen_own(ext, wide1_ref, 0 if edge == 0 else ROWS + 1, 1)
        ing[edge * COLS : (edge + 1) * COLS, :] = conv_block(wide1_ref, 1, k1_ref, edge * COLS, COLS)
    side_part(rim, None, k1_ref, ing)

    def act(n, carry):
        m = pl.multiple_of(n * STEP, STEP)
        pre = ing[pl.ds(m, STEP), :]
        s = jax.nn.sigmoid(pre)
        hid = (pre * s).astype(BF16)
        grad = (hg_ref[pl.ds(m, STEP), :] * s * (1.0 + pre * (1.0 - s))).astype(BF16)
        for q in range(STEP // COLS):
            row = n * (STEP // COLS) + q
            exth[2 + row] = hid[q * COLS : (q + 1) * COLS]
            extp[1 + row] = grad[q * COLS : (q + 1) * COLS]
        pg_ref[pl.ds(m, STEP), :] = grad
        return carry

    lax.fori_loop(0, CELLS // STEP, act, 0)
    make_slab(extp, 1, send2, 16, me, tmp)
    make_slab(exth, 2, send2, 0, me, tmp)
    start_sides(send2, recv2, ss2, rs2)
    start_rows(extp, 1, rssp, rrsp)
    start_rows(exth, 2, rssh, rrsh)
    widen_own(extp, widep, 1, ROWS)

    def inner_fold(n, carry):
        m = pl.multiple_of(COLS + n * STEP, COLS)
        ing[pl.ds(m, STEP), :] = g_ref[pl.ds(m, STEP), :].astype(F32) + conv_block(widep, 1, k1t_ref, m, STEP)
        return carry

    lax.fori_loop(0, 3, inner_fold, 0)
    patch_sides(wide1_ref, rim)
    wait_sides_recv(send2, recv2, ss2, rs2)
    wait_rows_recv(extp, 1, rssp, rrsp)
    open_slab(recv2, 1, 16, me, rim)
    split_rim(rim, 1, me, before, after, trim)
    for edge in (0, ROWS - 1):
        widen_own(extp, widep, 0 if edge == 0 else ROWS + 1, 1)
        ing[edge * COLS : (edge + 1) * COLS, :] = g_ref[edge * COLS : (edge + 1) * COLS, :].astype(F32) + conv_block(
            widep, 1, k1t_ref, edge * COLS, COLS
        )
    side_part(rim, trim, k1t_ref, ing)
    for q in range(4):
        part = ing[q * 256 : (q + 1) * 256, :].astype(BF16)
        rounded[q * 16 : (q + 1) * 16] = part.reshape(16, BT, CH)

    for half in (0, 1):

        def pick(q, carry):
            block = rounded[ids[half, q]]
            y, zh, x = lax.div(q, 32), lax.rem(lax.div(q, 16), 2), lax.rem(lax.div(q, 4), 4)
            zl, c = lax.rem(lax.div(q, 2), 2), lax.rem(q, 2)
            b0[half, y, zh, x, zl, c] = block[:, 0:128]
            b0[2 + half, y, zh, x, zl, c] = block[:, 128:256]
            return carry

        lax.fori_loop(0, PAIRS, pick, 0, unroll=4)
        swap.core_start(half)
        swap.core_start(2 + half)

    def hidden_rows():
        wait_rows_recv(exth, 2, rssh, rrsh)
        open_slab(recv2, 2, 0, me, rim2)
        widen(exth, 2, rim2, wide2_ref)

    def kernel_grads(o):
        acc[1, o] = lax.dot_general(
            wide2_ref[o * 2 * COLS : o * 2 * COLS + CELLS, :],
            g_ref[...],
            (((0,), (0,)), ((), ())),
            preferred_element_type=F32,
        )
        acc[0, o] = lax.dot_general(
            wide1_ref[o * COLS : o * COLS + CELLS, :],
            pg_ref[...],
            (((0,), (0,)), ((), ())),
            preferred_element_type=F32,
        )
        sums.start(o)

    def mixed():
        def block(n, carry):
            m = pl.multiple_of(n * STEP, STEP)
            mixed_ref[pl.ds(m, STEP), :] = (
                x_ref[pl.ds(m // COLS, STEP // COLS)].reshape(STEP, CH).astype(F32)
                + conv_block(wide2_ref, 2, k2_ref, m, STEP)
            ).astype(BF16)
            return carry

        lax.fori_loop(0, CELLS // STEP, block, 0)

    def spread_weights():
        w = w_ref[...]
        ps = ps_ref[0:1, :]
        for n in range(SB):
            wexp[n * BL : (n + 1) * BL, :] = w * (ps == n).astype(F32).astype(BF16)

    def source():
        def take(p, carry):
            q = slot[p]
            half, t = lax.div(q, PAIRS), lax.rem(q, PAIRS)
            y, zh, x = lax.div(t, 32), lax.rem(lax.div(t, 16), 2), lax.rem(lax.div(t, 4), 4)
            zl, c = lax.rem(lax.div(t, 2), 2), lax.rem(t, 2)
            at = pl.ds(pl.multiple_of(p * BT, BT), BT)
            rows[at, 0:128] = b4[half, y, zh, x, zl, c]
            rows[at, 128:256] = b4[2 + half, y, zh, x, zl, c]
            return carry

        lax.fori_loop(0, PAIRS, take, 0, unroll=4)
        for m in range(4):
            source_ref[m * 256 : (m + 1) * 256, :] = jnp.dot(
                wexp[m * 256 : (m + 1) * 256, :], rows[...], preferred_element_type=F32
            ).astype(BF16)

    def drained():
        wait_sides_send(send, recv, ss, rs)
        wait_rows_send(ext, 1, rss, rrs)
        wait_sides_send(send2, recv2, ss2, rs2)
        wait_rows_send(exth, 2, rssh, rrsh)
        wait_rows_send(extp, 1, rssp, rrsp)
        swap.drain(0, 1)

    steps = {
        "x": drained, "y": lambda: swap.drain(2),
        "H": hidden_rows, "K": kernel_grads, "M": mixed, "W": spread_weights, "S": source,
        "a": lambda u: swap.advance(0, u), "b": lambda u: swap.advance(1, u),
        "c": lambda u: swap.advance(2, u), "d": lambda u: swap.wait(2, u),
        "2": sums.to_second, "3": sums.to_third, "4": sums.to_fourth,
        "5": sums.to_fifth, "6": sums.to_sixth, "7": sums.to_seventh,
    }
    for word in ORDER.split():
        if len(word) == 1:
            steps[word]()
        for n in word[1:]:
            steps[word[0]](int(n))
    sums.finish()


def mid(flip, ids, slot, x, hidden_grad, grad, k1, k1t, k2, w_cells, ps_cells):
    dma = pltpu.SemaphoreType.DMA
    three, nine = [dma((3,))] * 2, [dma((3, 3))] * 2
    return pl.pallas_call(
        mid_kernel,
        name="middle",
        out_shape=(
            jax.ShapeDtypeStruct((CELLS, CH), BF16),
            jax.ShapeDtypeStruct((2, 3, PART, CH), BF16),
            jax.ShapeDtypeStruct((SB * BL, CH), BF16),
        ),
        in_specs=[SM, SM, SM] + [VM] * 8,
        out_specs=(VM, VM, VM),
        scratch_shapes=[
            pltpu.VMEM((ROWS + 2, COLS, CH), BF16),
            pltpu.VMEM((ROWS + 4, COLS, CH), BF16),
            pltpu.VMEM((ROWS + 2, COLS, CH), BF16),
            pltpu.VMEM((2, 16, CH), BF16),
            pltpu.VMEM((2, 3, 16, CH), BF16),
            pltpu.VMEM((2, 32, CH), BF16),
            pltpu.VMEM((2, 3, 32, CH), BF16),
            pltpu.VMEM((2, 16, CH), F32),
            pltpu.VMEM((2, 1, 16, CH), F32),
            pltpu.VMEM((2, 2, 16, CH), F32),
            pltpu.VMEM((2, 1, 16, CH), F32),
            pltpu.VMEM(((ROWS + 2) * COLS, 3 * CH), BF16),
            pltpu.VMEM(((ROWS + 4) * COLS, 3 * CH), BF16),
            pltpu.VMEM(((ROWS + 2) * COLS, 3 * CH), BF16),
            pltpu.VMEM((CELLS, CH), BF16),
            pltpu.VMEM((CELLS, CH), F32),
            pltpu.VMEM((BLOCKS, BT, CH), BF16),
            *[pltpu.VMEM(WORLD, BF16)] * 5,
            pltpu.VMEM((PAIRS * BT, CH), BF16),
            pltpu.VMEM((SB * BL, PAIRS * BT), BF16),
            pltpu.VMEM((2, 3, PART, CH), F32),
            pltpu.VMEM((3, PART, CH), BF16),
            pltpu.VMEM((3, PART, CH), BF16),
            pltpu.VMEM((3, PART, CH), BF16),
            pltpu.VMEM((3, 3, 192, CH), BF16),
            pltpu.VMEM((3, 192, CH), BF16),
            pltpu.VMEM((3, 3, 48, CH), BF16),
            pltpu.VMEM((3, 4, 48, CH), BF16),
            dma((2, 3)), dma((2, 3)), dma((2,)), dma((2,)),
            dma((2, 3)), dma((2, 3)), dma((2,)), dma((2,)), dma((2,)), dma((2,)),
            *three, *nine, *nine, *nine, *nine, *nine, *three,
            *swap_sems(),
        ],
        compiler_params=pltpu.CompilerParams(vmem_limit_bytes=42 * 2**20, collective_id=2, has_side_effects=True),
        cost_estimate=pl.CostEstimate(flops=6 * 2**30, bytes_accessed=12 * 2**20, transcendentals=2**18),
    )(flip, ids, slot, x, hidden_grad, grad, k1, k1t, k2, w_cells, ps_cells)


PART = 3 * CH


def axes_of(o):
    return o, (o + 1) % 3, (o + 2) % 3


class Sums:
    def __init__(self, out, acc, send1, recv1, sent2, got2, sent3, got3, got4, sems):
        self.out, self.acc, self.send1, self.recv1 = out, acc, send1, recv1
        self.sent2, self.got2, self.sent3, self.got3, self.got4, self.sems = sent2, got2, sent3, got3, got4, sems
        t, b, tiles, bands = place_in_mesh()
        self.place = spot(t, b)
        self.core = self.place[3]

    def first(self, o):
        s, r = self.sems[0:2]
        return remote(self.send1.at[o], self.recv1.at[o], s.at[o], r.at[o], twin())

    def second(self, o, k):
        s, r = self.sems[2:4]
        a = axes_of(o)[0]
        at = pl.ds(pl.multiple_of(lax.rem(self.place[a] + k, 4) * 192, 64), 192)
        return remote(self.sent2.at[o, at], self.got2.at[o, k - 1], s.at[o, k - 1], r.at[o, k - 1], axis_peer(a, k))

    def third(self, o, k):
        s, r = self.sems[4:6]
        a = axes_of(o)[1]
        at = pl.ds(pl.multiple_of(lax.rem(self.place[a] + k, 4) * 48, 16), 48)
        return remote(self.sent3.at[o, at], self.got3.at[o, k - 1], s.at[o, k - 1], r.at[o, k - 1], axis_peer(a, k))

    def fourth(self, o, k):
        s, r = self.sems[6:8]
        a = axes_of(o)[2]
        mine = self.got4.at[o, self.place[a]]
        return remote(mine, mine, s.at[o, k - 1], r.at[o, k - 1], axis_peer(a, k))

    def rows(self, o, wide):
        a, c, _ = axes_of(o)
        if wide:
            return pl.ds(pl.multiple_of(self.place[a] * 192, 64), 192)
        return pl.ds(pl.multiple_of(self.place[a] * 192 + self.place[c] * 48, 16), 48)

    def fifth(self, o, k):
        s, r = self.sems[8:10]
        rows = self.out.at[self.core, o, self.rows(o, False)]
        return remote(rows, rows, s.at[o, k - 1], r.at[o, k - 1], axis_peer(axes_of(o)[1], k))

    def sixth(self, o, k):
        s, r = self.sems[10:12]
        rows = self.out.at[self.core, o, self.rows(o, True)]
        return remote(rows, rows, s.at[o, k - 1], r.at[o, k - 1], axis_peer(axes_of(o)[0], k))

    def seventh(self, o):
        s, r = self.sems[12:14]
        whole = self.out.at[self.core, o]
        return remote(whole, whole, s.at[o], r.at[o], twin())

    def start(self, o):
        self.send1[o] = self.acc[1 - self.core, o].astype(BF16)
        self.first(o).start()

    def to_second(self, o):
        self.first(o).wait_recv()
        total = self.acc[self.core, o] + self.recv1[o].astype(F32)
        self.acc[self.core, o] = total
        self.sent2[o] = total.astype(BF16)
        for k in (2, 1, 3):
            self.second(o, k).start()

    def to_third(self, o):
        for k in (1, 2, 3):
            self.second(o, k).wait_recv()
        total = self.acc[self.core, o, self.rows(o, True), :]
        for k in (1, 2, 3):
            total = total + self.got2[o, k - 1].astype(F32)
        self.acc[self.core, o, 0:192, :] = total
        self.sent3[o] = total.astype(BF16)
        for k in (2, 1, 3):
            self.third(o, k).start()

    def to_fourth(self, o):
        a, c, e = axes_of(o)
        for k in (1, 2, 3):
            self.third(o, k).wait_recv()
        total = self.acc[self.core, o, pl.ds(pl.multiple_of(self.place[c] * 48, 16), 48), :]
        for k in (1, 2, 3):
            total = total + self.got3[o, k - 1].astype(F32)
        self.got4[o, self.place[e]] = total.astype(BF16)
        for k in (2, 1, 3):
            self.fourth(o, k).start()

    def to_fifth(self, o):
        for k in (1, 2, 3):
            self.fourth(o, k).wait_recv()
        v = [self.got4[o, q].astype(F32) for q in range(4)]
        self.out[self.core, o, self.rows(o, False), :] = (((v[0] + v[1]) + v[2]) + v[3]).astype(BF16)
        for k in (2, 1, 3):
            self.fifth(o, k).start()

    def to_sixth(self, o):
        for k in (1, 2, 3):
            self.fifth(o, k).wait_recv()
        for k in (2, 1, 3):
            self.sixth(o, k).start()

    def to_seventh(self, o):
        for k in (1, 2, 3):
            self.sixth(o, k).wait_recv()
        self.seventh(o).start()

    def finish(self):
        for o in range(3):
            self.first(o).wait_send()
            for k in (1, 2, 3):
                for step in (self.second, self.third, self.fourth, self.fifth, self.sixth):
                    step(o, k).wait_send()
        for o in range(3):
            self.seventh(o).wait()


def finish_kernel(sums, mixed, source, one, two, mixed_out, source_out, wide, sems):
    copies = [
        pltpu.make_async_copy(mixed, mixed_out, sems.at[6]),
        pltpu.make_async_copy(source, source_out, sems.at[7]),
    ]
    for copy in copies:
        copy.start()
    for n, out in ((0, one), (1, two)):
        for i in range(3):
            wide[n, i] = sums[n, i].astype(F32)
            copy = pltpu.make_async_copy(wide.at[n, i], out.at[i], sems.at[n * 3 + i])
            copy.start()
            copies.append(copy)
    for copy in copies:
        copy.wait()


def finish(sums, mixed, source):
    away = pl.BlockSpec(memory_space=pltpu.HBM)
    return pl.pallas_call(
        finish_kernel,
        name="finish",
        out_shape=(
            jax.ShapeDtypeStruct((3, PART, CH), F32),
            jax.ShapeDtypeStruct((3, PART, CH), F32),
            jax.ShapeDtypeStruct((CELLS, CH), BF16),
            jax.ShapeDtypeStruct((SB * BL, CH), BF16),
        ),
        in_specs=[VM] * 3,
        out_specs=(away,) * 4,
        scratch_shapes=[pltpu.VMEM((2, 3, PART, CH), F32), pltpu.SemaphoreType.DMA((8,))],
        compiler_params=params(),
        cost_estimate=pl.CostEstimate(flops=2**20, bytes_accessed=8 * 2**20, transcendentals=0),
    )(sums, mixed, source)


def local(
    source_cells, regrid_weights, pair_target, pair_block, pair_source, flip_codes, kernel_one, kernel_two, out_grad
):
    target = pair_target[:, 0]
    outgoing, slot = regrid(target, pair_source, regrid_weights, source_cells)
    upstream = out_grad[0]
    hidden_grad, k1_back, arrived, ids, safe_ids, w_cells, ps_cells = back(
        flip_codes,
        pair_target.reshape(1, PAIRS),
        pair_block.reshape(1, PAIRS),
        pair_source.reshape(1, PAIRS),
        regrid_weights,
        upstream,
        kernel_one,
        kernel_two,
        outgoing.reshape(WORLD),
    )
    regridded = gather_sum(ids, arrived.reshape(2, 2 * PAIRS, BT, 128))
    mixed, sums, source_grad = mid(
        flip_codes,
        safe_ids,
        slot,
        regridded.reshape(ROWS, COLS, CH),
        hidden_grad,
        upstream.reshape(CELLS, CH),
        kernel_one.reshape(3, PART, CH),
        k1_back,
        kernel_two.reshape(3, PART, CH),
        w_cells,
        ps_cells,
    )
    one, two, mixed, source_grad = finish(sums, mixed, source_grad)
    return (
        mixed.reshape(1, ROWS, COLS, CH),
        one.reshape(3, 3, CH, CH),
        two.reshape(3, 3, CH, CH),
        source_grad,
    )


def solution(mesh):
    placed = (
        P(("tile", "band"), None),
        P(("tile", "band"), None, None),
        P(("tile", "band"), None),
        P(("tile", "band")),
        P(("tile", "band")),
        P(),
        P(),
        P(),
        P("tile", "band", None, None),
    )
    return jax.shard_map(
        local,
        mesh=mesh,
        in_specs=placed,
        out_specs=(P("tile", "band", None, None), P(), P(), P(("tile", "band"), None)),
        check_vma=False,
    )
```

```python
import jax
import jax.numpy as jnp
from jax import lax
from jax.experimental import pallas as pl
from jax.experimental.pallas import tpu as pltpu
from jax.sharding import PartitionSpec as P

F32 = jnp.float32
BF16 = jnp.bfloat16
MESH = pl.DeviceIdType.MESH
VM = pl.BlockSpec(memory_space=pltpu.VMEM)
SM = pl.BlockSpec(memory_space=pltpu.SMEM)
FAR = pl.BlockSpec(memory_space=pltpu.HBM)
LIMIT = 16 * 2**20
ROWS, COLS, CH = 8, 128, 256
PAIRS, BT, BL, SB, BLOCKS = 128, 16, 64, 16, 64
CELLS = ROWS * COLS


def params(**more):
    return pltpu.CompilerParams(vmem_limit_bytes=LIMIT, **more)


def regrid_kernel(tgt_far, psrc_far, w_ref, src_far, out_ref, slot_ref, cnt, masks, wexp, tgt, psrc, src_ref, sems):
    copies = [
        pltpu.make_async_copy(tgt_far, tgt, sems.at[0]),
        pltpu.make_async_copy(psrc_far, psrc, sems.at[1]),
        pltpu.make_async_copy(src_far, src_ref, sems.at[2]),
    ]
    for copy in copies:
        copy.start()
    lane = lax.broadcasted_iota(jnp.int32, (BT, 128), 1)
    masks[0] = (lane < BL).astype(F32).astype(BF16)
    masks[1] = (lane >= BL).astype(F32).astype(BF16)
    wexp[...] = jnp.zeros_like(wexp)

    def clear(i, c):
        cnt[i] = 0
        return c

    lax.fori_loop(0, PAIRS, clear, 0, unroll=8)
    copies[0].wait()
    copies[1].wait()

    def place(p, c):
        t = tgt[p]
        r = cnt[t]
        cnt[t] = r + 1
        slot_ref[p] = jnp.minimum(r, 1) * PAIRS + t
        s = psrc[p]
        w = w_ref[p]
        ww = jnp.concatenate([w, w], axis=1) * masks[lax.rem(s, 2)]
        row = pl.multiple_of(p * BT, BT)
        col = pl.multiple_of((s // 2) * 128, 128)
        wexp[pl.ds(row, BT), pl.ds(col, 128)] = ww
        return c

    lax.fori_loop(0, PAIRS, place, 0, unroll=8)
    copies[2].wait()
    for m in range(4):
        part = jnp.dot(wexp[m * 512 : (m + 1) * 512, :], src_ref[...], preferred_element_type=F32).astype(BF16)
        for q in range(32):
            at = slot_ref[m * 32 + q]
            for h in (0, 1):
                out_ref[h, at] = part[q * BT : (q + 1) * BT, h * 128 : (h + 1) * 128]


def regrid(tgt, psrc, weights, source):
    return pl.pallas_call(
        regrid_kernel,
        name="regrid",
        out_shape=(
            jax.ShapeDtypeStruct((2, 2 * PAIRS, BT, 128), BF16),
            jax.ShapeDtypeStruct((PAIRS,), jnp.int32),
        ),
        in_specs=[FAR, FAR, VM, FAR],
        out_specs=(VM, SM),
        scratch_shapes=[
            pltpu.SMEM((PAIRS,), jnp.int32),
            pltpu.VMEM((2, BT, 128), BF16),
            pltpu.VMEM((PAIRS * BT, SB * BL), BF16),
            pltpu.SMEM((PAIRS,), jnp.int32),
            pltpu.SMEM((PAIRS,), jnp.int32),
            pltpu.VMEM((SB * BL, CH), BF16),
            pltpu.SemaphoreType.DMA((3,)),
        ],
        compiler_params=params(),
        cost_estimate=pl.CostEstimate(flops=2 * 2048 * 1024 * 256, bytes_accessed=6 * 2**20, transcendentals=0),
    )(tgt, psrc, weights, source)


def gather_sum_kernel(ids, got_ref, out_ref, acc, more):
    acc[...] = jnp.zeros_like(acc)
    more[...] = jnp.zeros_like(more)

    def add(q, c):
        k, n = ids[0, q], ids[1, q]
        for h in (0, 1):
            acc[h, k] += got_ref[h, q].astype(F32)
            more[h, n] += got_ref[h, PAIRS + q].astype(F32)
        return c

    lax.fori_loop(0, PAIRS, add, 0, unroll=8)
    for h in (0, 1):
        out_ref[:, :, h * 128 : (h + 1) * 128] = (acc[h, 0:BLOCKS] + more[h, 0:BLOCKS]).astype(BF16)


def gather_sum(ids, arrived):
    return pl.pallas_call(
        gather_sum_kernel,
        name="gather_sum",
        out_shape=jax.ShapeDtypeStruct((BLOCKS, BT, CH), BF16),
        in_specs=[SM, VM],
        out_specs=VM,
        scratch_shapes=[pltpu.VMEM((2, BLOCKS + 1, BT, 128), F32)] * 2,
        compiler_params=params(),
        cost_estimate=pl.CostEstimate(flops=2**21, bytes_accessed=3 * 2**20, transcendentals=0),
    )(ids, arrived)


def place_in_mesh():
    return lax.axis_index("tile"), lax.axis_index("band"), lax.axis_size("tile"), lax.axis_size("band")


def greet():
    t, b, tiles, bands = place_in_mesh()
    barrier = pltpu.get_barrier_semaphore()
    for dt in (1, -1, 0):
        for db in (-1, 0, 1):
            if dt == 0 and db == 0:
                continue

            def say(dt=dt, db=db):
                pl.semaphore_signal(
                    barrier, inc=1, device_id=(lax.rem(t + dt + tiles, tiles), b + db), device_id_type=MESH
                )

            near_band(b, bands, db, say)


def greet_wait(others):
    b, bands = lax.axis_index("band"), lax.axis_size("band")
    near = 2 + jnp.where(b > 0, 3, 0) + jnp.where(b < bands - 1, 3, 0)
    pl.semaphore_wait(pltpu.get_barrier_semaphore(), near + others)


def near_band(b, bands, db, action):
    if db == 0:
        action()
    elif db < 0:
        pl.when(b > 0)(action)
    else:
        pl.when(b < bands - 1)(action)


def side_copy(send, recv, ss, rs, way, db, group):
    t, b, tiles, bands = place_in_mesh()
    to = lax.rem(t + (1 if way == 0 else tiles - 1), tiles)
    return pltpu.make_async_remote_copy(
        src_ref=send.at[way],
        dst_ref=recv.at[way, group],
        send_sem=ss.at[way, 1 + db],
        recv_sem=rs.at[way, group],
        device_id=(to, b + db),
        device_id_type=MESH,
    )


def row_copy(ext, d, ss, rs, db):
    t, b, tiles, bands = place_in_mesh()
    if db < 0:
        src, dst, k = ext.at[pl.ds(d, d)], ext.at[pl.ds(ROWS + d, d)], 0
    else:
        src, dst, k = ext.at[pl.ds(ROWS, d)], ext.at[pl.ds(0, d)], 1
    return pltpu.make_async_remote_copy(
        src_ref=src, dst_ref=dst, send_sem=ss.at[k], recv_sem=rs.at[k], device_id=(t, b + db), device_id_type=MESH
    )


def start_sides(send, recv, ss, rs):
    b, bands = lax.axis_index("band"), lax.axis_size("band")
    for way in (0, 1):
        for db in (0, -1, 1):
            near_band(b, bands, db, lambda way=way, db=db: side_copy(send, recv, ss, rs, way, db, 1 - db).start())


def start_rows(ext, d, ss, rs):
    b, bands = lax.axis_index("band"), lax.axis_size("band")
    for db in (-1, 1):
        near_band(b, bands, db, lambda db=db: row_copy(ext, d, ss, rs, db).start())


def wait_sides_recv(send, recv, ss, rs):
    b, bands = lax.axis_index("band"), lax.axis_size("band")
    for way in (0, 1):
        for db in (0, -1, 1):
            near_band(b, bands, db, lambda way=way, db=db: side_copy(send, recv, ss, rs, way, 0, 1 + db).wait_recv())


def wait_sides_send(send, recv, ss, rs):
    b, bands = lax.axis_index("band"), lax.axis_size("band")
    for way in (0, 1):
        for db in (0, -1, 1):
            near_band(b, bands, db, lambda way=way, db=db: side_copy(send, recv, ss, rs, way, db, 1 - db).wait_send())


def wait_rows_recv(ext, d, ss, rs):
    b, bands = lax.axis_index("band"), lax.axis_size("band")
    near_band(b, bands, -1, lambda: row_copy(ext, d, ss, rs, 1).wait_recv())
    near_band(b, bands, 1, lambda: row_copy(ext, d, ss, rs, -1).wait_recv())


def wait_rows_send(ext, d, ss, rs):
    b, bands = lax.axis_index("band"), lax.axis_size("band")
    for db in (-1, 1):
        near_band(b, bands, db, lambda db=db: row_copy(ext, d, ss, rs, db).wait_send())


def clear_edges(ext, d):
    b, bands = lax.axis_index("band"), lax.axis_size("band")

    @pl.when(b == 0)
    def _():
        ext[0:d] = jnp.zeros((d, COLS, CH), BF16)

    @pl.when(b == bands - 1)
    def _():
        ext[ROWS + d : ROWS + 2 * d] = jnp.zeros((d, COLS, CH), BF16)


def clear_groups(recv):
    b, bands = lax.axis_index("band"), lax.axis_size("band")
    for way in (0, 1):

        @pl.when(b == 0)
        def _():
            recv[way, 0] = jnp.zeros(recv.shape[2:], BF16)

        @pl.when(b == bands - 1)
        def _():
            recv[way, 2] = jnp.zeros(recv.shape[2:], BF16)


def flags(flip):
    t, b, tiles, bands = place_in_mesh()
    me = flip[t]
    before = flip[lax.rem(t + tiles - 1, tiles)]
    after = flip[lax.rem(t + 1, tiles)]
    return me, before, after


def make_slab(ext, d, send, base, flip_me, tmp):
    if d == 1:
        tmp[...] = jnp.zeros_like(tmp)
    for r in range(ROWS):
        first = ext[d + r, 0:16, :].astype(F32)
        last = ext[d + r, COLS - 16 : COLS, :].astype(F32)
        for k in range(d):
            tmp[0, k * 8 + r : k * 8 + r + 1, :] = first[k : k + 1]
            tmp[1, k * 8 + r : k * 8 + r + 1, :] = last[15 - k : 16 - k]
    turned = jnp.full((16, CH), flip_me, jnp.int32) == 1
    left, right = tmp[0], tmp[1]
    send[0, base : base + 16] = jnp.where(turned, left, right).astype(BF16)
    send[1, base : base + 16] = jnp.where(turned, right, left).astype(BF16)


def open_slab(recv, d, base, flip_me, rim):
    turned = jnp.full((16, CH), flip_me, jnp.int32) == 1
    for g in range(3):
        before = recv[0, g, base : base + 16].astype(F32)
        after = recv[1, g, base : base + 16].astype(F32)
        sides = (jnp.where(turned, after, before), jnp.where(turned, before, after))
        for side in (0, 1):
            for k in range(d):
                part = sides[side][k * 8 : k * 8 + 8]
                if g == 0:
                    rim[side, k, 0:d, :] = part[8 - d :]
                elif g == 1:
                    rim[side, k, d : d + 8, :] = part
                else:
                    rim[side, k, d + 8 : 2 * d + 8, :] = part[:d]


def split_rim(rim, d, flip_me, flip_before, flip_after, turned_rim):
    odd_before = (flip_before != flip_me).astype(jnp.int32)
    odd_after = (flip_after != flip_me).astype(jnp.int32)
    odd_left = jnp.where(flip_me == 0, odd_before, odd_after)
    odd_right = jnp.where(flip_me == 0, odd_after, odd_before)
    for side, odd in ((0, odd_left), (1, odd_right)):
        mask = jnp.full((16, CH), odd, jnp.int32) == 1
        for k in range(d):
            whole = rim[side, k]
            turned_rim[side, k] = jnp.where(mask, whole, 0.0)
            rim[side, k] = jnp.where(mask, 0.0, whole)


def widen(ext, d, rim, wide):
    col = lax.broadcasted_iota(jnp.int32, (COLS, CH), 0)

    def one(row, carry):
        mid = ext[row]
        x = mid.astype(F32)
        left = pltpu.roll(x, d, 0)
        right = pltpu.roll(x, COLS - d, 0)
        for k in range(d):
            near = jnp.broadcast_to(rim[0, k, pl.ds(row, 1), :], (COLS, CH))
            left = jnp.where(col == d - 1 - k, near, left)
            near = jnp.broadcast_to(rim[1, k, pl.ds(row, 1), :], (COLS, CH))
            right = jnp.where(col == COLS - d + k, near, right)
        at = pl.ds(pl.multiple_of(row * COLS, COLS), COLS)
        wide[at, 0:CH] = left.astype(BF16)
        wide[at, CH : 2 * CH] = mid
        wide[at, 2 * CH : 3 * CH] = right.astype(BF16)
        return carry

    lax.fori_loop(0, ROWS + 2 * d, one, 0)


def widen_own(ext, wide, first, count):
    col = lax.broadcasted_iota(jnp.int32, (COLS, CH), 0)

    def one(row, carry):
        mid = ext[row]
        x = mid.astype(F32)
        left = jnp.where(col == 0, 0.0, pltpu.roll(x, 1, 0))
        right = jnp.where(col == COLS - 1, 0.0, pltpu.roll(x, COLS - 1, 0))
        at = pl.ds(pl.multiple_of(row * COLS, COLS), COLS)
        wide[at, 0:CH] = left.astype(BF16)
        wide[at, CH : 2 * CH] = mid
        wide[at, 2 * CH : 3 * CH] = right.astype(BF16)
        return carry

    lax.fori_loop(first, first + count, one, 0)


def side_part(rim, turned_rim, taps, out):
    total = None
    none = jnp.zeros((ROWS, CH), F32)
    for i in range(3):
        near = [rim[side, 0, i : i + ROWS, :] for side in (0, 1)]
        turned = [none, none] if turned_rim is None else [turned_rim[side, 0, i : i + ROWS, :] for side in (0, 1)]
        lhs = jnp.concatenate(
            [
                jnp.concatenate([near[0], none, turned[0]], axis=1),
                jnp.concatenate([turned[1], none, near[1]], axis=1),
            ],
            axis=0,
        )
        part = jnp.dot(lhs.astype(BF16), taps[i], preferred_element_type=F32)
        total = part if total is None else total + part
    for r in range(ROWS):
        at = r * COLS
        out[at : at + 1, :] += total[r : r + 1]
        at = r * COLS + COLS - 1
        out[at : at + 1, :] += total[ROWS + r : ROWS + r + 1]


def patch_sides(wide, rim):
    row = lax.broadcasted_iota(jnp.int32, (16, CH), 0)
    for r in range(ROWS + 2):
        at = r * COLS
        tile = wide[at : at + 16, 0:CH].astype(F32)
        near = jnp.broadcast_to(rim[0, 0, r : r + 1, :], (16, CH))
        wide[at : at + 16, 0:CH] = jnp.where(row == 0, near, tile).astype(BF16)
        at = r * COLS + COLS - 16
        tile = wide[at : at + 16, 2 * CH : 3 * CH].astype(F32)
        near = jnp.broadcast_to(rim[1, 0, r : r + 1, :], (16, CH))
        wide[at : at + 16, 2 * CH : 3 * CH] = jnp.where(row == 15, near, tile).astype(BF16)


def conv_block(wide, d, taps, m, rows):
    total = None
    for i in range(3):
        lhs = wide[pl.ds(pl.multiple_of(m + i * d * COLS, COLS), rows), :]
        part = jnp.dot(lhs, taps[i], preferred_element_type=F32)
        total = part if total is None else total + part
    return total


def turned_part(turned_rim, d, taps, out):
    left, right = None, None
    for i in range(3):
        lhs_left = jnp.concatenate([turned_rim[0, d - 1 - c, i * d : i * d + 8, :] for c in range(d)], axis=0)
        lhs_right = jnp.concatenate([turned_rim[1, c, i * d : i * d + 8, :] for c in range(d)], axis=0)
        a = jnp.dot(lhs_left.astype(BF16), taps[i, 2 * CH : 3 * CH, :], preferred_element_type=F32)
        z = jnp.dot(lhs_right.astype(BF16), taps[i, 0:CH, :], preferred_element_type=F32)
        left = a if left is None else left + a
        right = z if right is None else right + z
    for c in range(d):
        for r in range(ROWS):
            at = r * COLS + c
            out[at : at + 1, :] += left[c * 8 + r : c * 8 + r + 1]
            at = r * COLS + COLS - d + c
            out[at : at + 1, :] += right[c * 8 + r : c * 8 + r + 1]


STEP = 256


def spot(t, b):
    x = lax.rem(t, 4)
    y = lax.div(t, 8)
    z = lax.rem(lax.div(t, 4), 2) * 2 + lax.div(b, 2)
    return x, y, z, lax.rem(b, 2)


def device_at(x, y, z, core):
    return (y * 8 + lax.div(z, 2) * 4 + x, lax.rem(z, 2) * 2 + core)


WORLD = (4, 4, 2, 4, 2, 2, BT, 128)
UNITS = [(hs, other) for other in (0, 1) for hs in range(4)]


def axis_peer(axis, k):
    t, b, tiles, bands = place_in_mesh()
    at = list(spot(t, b))
    at[axis] = lax.rem(at[axis] + k, 4)
    return device_at(*at)


def twin():
    t, b, tiles, bands = place_in_mesh()
    return (t, b + 1 - 2 * lax.rem(b, 2))


def greet_axes():
    barrier = pltpu.get_barrier_semaphore()
    pl.semaphore_signal(barrier, inc=1, device_id=twin(), device_id_type=MESH)
    for axis in range(3):
        for k in (1, 2, 3):
            pl.semaphore_signal(barrier, inc=1, device_id=axis_peer(axis, k), device_id_type=MESH)


AXIS_PEERS = 10


def along(ref, unit, axis, v):
    hs, other = UNITS[unit]
    c = lax.rem(lax.axis_index("band") + other, 2)
    if axis == 0:
        return ref.at[hs, :, :, v, :, c]
    if axis == 1:
        return ref.at[hs, v, :, :, :, c]
    return ref.at[hs, :, lax.div(v, 2), :, lax.rem(v, 2), c]


def remote(src, dst, ss, rs, to):
    return pltpu.make_async_remote_copy(
        src_ref=src, dst_ref=dst, send_sem=ss, recv_sem=rs, device_id=to, device_id_type=MESH
    )


class Swap:
    def __init__(self, bufs, sems):
        self.bufs, self.sems = bufs, sems
        t, b, tiles, bands = place_in_mesh()
        self.place = spot(t, b)

    def core_copy(self, hs):
        me = self.place[3]
        src, dst = self.bufs[0], self.bufs[1]
        ss, rs = self.sems[0], self.sems[1]
        return remote(
            src.at[hs, :, :, :, :, 1 - me], dst.at[hs, :, :, :, :, me], ss.at[hs], rs.at[hs], twin()
        )

    def core_start(self, hs):
        self.core_copy(hs).start()

    def source(self, stage, u):
        return self.bufs[0] if stage == 0 and UNITS[u][1] == 0 else self.bufs[1 + stage]

    def hop(self, stage, u, k):
        axis = (u + stage) % 3
        me = self.place[axis]
        src, dst = self.source(stage, u), self.bufs[2 + stage]
        return remote(
            along(src, u, axis, lax.rem(me + k, 4)), along(dst, u, axis, me),
            self.sems[2].at[stage, u, k - 1], self.sems[3].at[stage, u, k - 1], axis_peer(axis, k),
        )

    def own(self, stage, u):
        axis = (u + stage) % 3
        me = self.place[axis]
        src, dst = self.source(stage, u), self.bufs[2 + stage]
        return pltpu.make_async_copy(along(src, u, axis, me), along(dst, u, axis, me), self.sems[4].at[stage, u])

    def start(self, stage, u):
        for k in (2, 1, 3):
            self.hop(stage, u, k).start()
        self.own(stage, u).start()

    def wait(self, stage, u):
        for k in (1, 2, 3):
            self.hop(stage, u, k).wait_recv()
        self.own(stage, u).wait()

    def advance(self, stage, u):
        if stage > 0:
            self.wait(stage - 1, u)
        elif UNITS[u][1] == 1:
            self.core_copy(UNITS[u][0]).wait_recv()
        self.start(stage, u)

    def first_stage(self, units):
        for u in units:
            self.advance(0, u)

    def next_stage(self, stage):
        for u in range(8):
            self.wait(stage - 1, u)
            self.start(stage, u)

    def last_wait(self):
        for u in range(8):
            self.wait(2, u)

    def drain(self, *stages):
        for stage in stages:
            if stage == 0:
                for hs in range(4):
                    self.core_copy(hs).wait_send()
            for u in range(8):
                for k in (1, 2, 3):
                    self.hop(stage, u, k).wait_send()


def swap_sems():
    dma = pltpu.SemaphoreType.DMA
    return [dma((4,)), dma((4,)), dma((3, 8, 3)), dma((3, 8, 3)), dma((3, 8))]


def table_peer(stage, k):
    t, b, tiles, bands = place_in_mesh()
    x, y, z, core = spot(t, b)
    if stage == 0:
        return (t, lax.rem(b + k, 4))
    if stage == 1:
        return (t - x + lax.rem(x + k, 4), b)
    if stage == 2:
        return (t + 4 - 8 * lax.rem(lax.div(t, 4), 2), b)
    return (lax.rem(t + 8 * k, 32), b)


TABLE_PEERS = (3, 3, 1, 3)
TABLE_ROWS = (1, 4, 16, 32)


def table_copy(tab, ss, rs, stage, k):
    t, b, tiles, bands = place_in_mesh()
    n = TABLE_ROWS[stage]
    at = lax.div(t * 4 + b, n) * n
    rows = tab.at[pl.ds(at, n)]
    return pltpu.make_async_remote_copy(
        src_ref=rows, dst_ref=rows, send_sem=ss.at[stage, k - 1], recv_sem=rs.at[stage, k - 1],
        device_id=table_peer(stage, k), device_id_type=MESH,
    )


def table_start(tab, ss, rs, stage):
    for k in range(1, TABLE_PEERS[stage] + 1):
        table_copy(tab, ss, rs, stage, k).start()


def table_wait(tab, ss, rs, stage):
    for k in range(1, TABLE_PEERS[stage] + 1):
        table_copy(tab, ss, rs, stage, k).wait()


def greet_table():
    barrier = pltpu.get_barrier_semaphore()
    for stage in range(4):
        for k in range(1, TABLE_PEERS[stage] + 1):
            pl.semaphore_signal(barrier, inc=1, device_id=table_peer(stage, k), device_id_type=MESH)


def back_kernel(
    flip, tgt_ref, blk_ref, src_row, w_ref, g_ref, k1_ref, k2_ref, outgoing,
    hg_ref, k1t_ref, arrived, ids_ref, safe_ref, w_cells, ps_cells,
    tab, ext, send, recv, tmp, rim, trim, wide, k2t, b1, b2, b3, ss, rs, rss, rrs, tss, trs, *sems,
):
    d = 2
    swap = Swap((outgoing, b1, b2, b3, arrived), sems)
    greet_table()
    greet_axes()
    greet()
    t, b, tiles, bands = place_in_mesh()
    tab[t * 4 + b] = tgt_ref[...] * BLOCKS + blk_ref[...]
    me, before, after = flags(flip)
    ext[pl.ds(d, ROWS)] = g_ref[...]
    make_slab(ext, d, send, 0, me, tmp)
    clear_edges(ext, d)
    clear_groups(recv)
    greet_wait(sum(TABLE_PEERS) + AXIS_PEERS)
    table_start(tab, tss, trs, 0)
    start_sides(send, recv, ss, rs)
    start_rows(ext, d, rss, rrs)
    for hs in range(4):
        swap.core_start(hs)
    swap.first_stage(range(0, 4))
    table_wait(tab, tss, trs, 0)
    table_start(tab, tss, trs, 1)
    swap.first_stage(range(4, 8))
    for i in range(3):
        for j in range(3):
            k2t[i, j * CH : (j + 1) * CH, :] = k2_ref[2 - i, 2 - j].T
    wait_sides_recv(send, recv, ss, rs)
    wait_rows_recv(ext, d, rss, rrs)
    open_slab(recv, d, 0, me, rim)
    split_rim(rim, d, me, before, after, trim)
    table_wait(tab, tss, trs, 1)
    table_start(tab, tss, trs, 2)
    swap.next_stage(1)
    widen(ext, d, rim, wide)

    def block(n, carry):
        m = pl.multiple_of(n * STEP, STEP)
        hg_ref[pl.ds(m, STEP), :] = conv_block(wide, d, k2t, m, STEP)
        return carry

    lax.fori_loop(0, CELLS // STEP, block, 0)
    table_wait(tab, tss, trs, 2)
    table_start(tab, tss, trs, 3)
    swap.next_stage(2)
    turned_part(trim, d, k2t, hg_ref)
    for i in range(3):
        for j in range(3):
            k1t_ref[i, j * CH : (j + 1) * CH, :] = k1_ref[2 - i, 2 - j].T
    for n in range(SB):
        part = w_ref[n * 8 : (n + 1) * 8].reshape(128, BL).astype(F32)
        part = jnp.concatenate([part, part], axis=1).T
        w_cells[:, n * 128 : (n + 1) * 128] = part[0:BL].astype(BF16)
    spread = (
        lax.broadcasted_iota(jnp.int32, (PAIRS, PAIRS * BT), 1) // BT
        == lax.broadcasted_iota(jnp.int32, (PAIRS, PAIRS * BT), 0)
    ).astype(F32)
    own = jnp.broadcast_to(src_row[...], (8, PAIRS)).astype(F32)
    ps_cells[...] = jnp.dot(own.astype(BF16), spread.astype(BF16), preferred_element_type=F32)
    table_wait(tab, tss, trs, 3)
    table = tab[...].reshape(PAIRS, PAIRS).T
    order = lax.broadcasted_iota(jnp.int32, (PAIRS, PAIRS), 0)
    block_of = lax.bitwise_and(table, BLOCKS - 1)
    mine = lax.shift_right_logical(table, 6) == t * 4 + b
    first = jnp.min(jnp.where(mine, order, PAIRS), axis=0, keepdims=True)
    last = jnp.max(jnp.where(mine, order, -1), axis=0, keepdims=True)
    id_first = jnp.sum(jnp.where(order == first, block_of, 0), axis=0, keepdims=True)
    id_last = jnp.sum(jnp.where(order == last, block_of, 0), axis=0, keepdims=True)
    ids_ref[0:1, :] = jnp.where(first < PAIRS, id_first, BLOCKS)
    ids_ref[1:2, :] = jnp.where(last > first, id_last, BLOCKS)
    safe_ref[0:1, :] = id_first
    safe_ref[1:2, :] = id_last
    wait_sides_send(send, recv, ss, rs)
    wait_rows_send(ext, d, rss, rrs)
    swap.drain(0, 1)
    swap.last_wait()
    swap.drain(2)


def back(flip, target, block, source, weights, grad, k1, k2, outgoing):
    d = 2
    return pl.pallas_call(
        back_kernel,
        name="hidden_adjoint",
        out_shape=(
            jax.ShapeDtypeStruct((CELLS, CH), F32),
            jax.ShapeDtypeStruct((3, 3 * CH, CH), BF16),
            jax.ShapeDtypeStruct(WORLD, BF16),
            jax.ShapeDtypeStruct((2, PAIRS), jnp.int32),
            jax.ShapeDtypeStruct((2, PAIRS), jnp.int32),
            jax.ShapeDtypeStruct((BL, PAIRS * BT), BF16),
            jax.ShapeDtypeStruct((8, PAIRS * BT), F32),
        ),
        in_specs=[SM] + [VM] * 8,
        out_specs=(VM,) * 7,
        scratch_shapes=[
            pltpu.VMEM((PAIRS, 1, PAIRS), jnp.int32),
            pltpu.VMEM((ROWS + 2 * d, COLS, CH), BF16),
            pltpu.VMEM((2, 16, CH), BF16),
            pltpu.VMEM((2, 3, 16, CH), BF16),
            pltpu.VMEM((2, 16, CH), F32),
            pltpu.VMEM((2, d, 16, CH), F32),
            pltpu.VMEM((2, d, 16, CH), F32),
            pltpu.VMEM(((ROWS + 2 * d) * COLS, 3 * CH), BF16),
            pltpu.VMEM((3, 3 * CH, CH), BF16),
            pltpu.VMEM(WORLD, BF16),
            pltpu.VMEM(WORLD, BF16),
            pltpu.VMEM(WORLD, BF16),
            pltpu.SemaphoreType.DMA((2, 3)),
            pltpu.SemaphoreType.DMA((2, 3)),
            pltpu.SemaphoreType.DMA((2,)),
            pltpu.SemaphoreType.DMA((2,)),
            pltpu.SemaphoreType.DMA((4, 3)),
            pltpu.SemaphoreType.DMA((4, 3)),
            *swap_sems(),
        ],
        compiler_params=pltpu.CompilerParams(vmem_limit_bytes=18 * 2**20, collective_id=1, has_side_effects=True),
        cost_estimate=pl.CostEstimate(flops=6 * 2**30, bytes_accessed=8 * 2**20, transcendentals=0),
    )(flip, target, block, source, weights, grad, k1, k2, outgoing)


ORDER = (
    "a0123",
    "H",
    "K0",
    "a45",
    "K1",
    "20",
    "K2",
    "21",
    "a67",
    "22",
    "b012",
    "30",
    "b345",
    "M",
    "b67",
    "31",
    "32",
    "W",
    "c012",
    "4012",
    "c345",
    "5012",
    "c67",
    "6012",
    "x",
    "d01234567",
    "S",
    "7012",
    "y",
)


def mid_kernel(
    flip, ids, slot, x_ref, hg_ref, g_ref, k1_ref, k1t_ref, k2_ref, w_ref, ps_ref,
    mixed_ref, out_ref, source_ref,
    ext, exth, extp, send, recv, send2, recv2, tmp, rim, rim2, trim, wide1_ref, wide2_ref, widep, pg_ref, ing, rounded,
    b0, b1, b2, b3, b4, rows, wexp,
    acc, send1, recv1, sent2, got2, sent3, got3, got4,
    ss, rs, rss, rrs, ss2, rs2, rssh, rrsh, rssp, rrsp,
    s1, r1, s2, r2, s3, r3, s4, r4, s5, r5, s6, r6, s7, r7, *sems,
):
    swap = Swap((b0, b1, b2, b3, b4), sems)
    sums = Sums(out_ref, acc, send1, recv1, sent2, got2, sent3, got3, got4, (s1, r1, s2, r2, s3, r3, s4, r4, s5, r5, s6, r6, s7, r7))
    greet_axes()
    greet()
    me, before, after = flags(flip)
    ext[pl.ds(1, ROWS)] = x_ref[...]
    make_slab(ext, 1, send, 0, me, tmp)
    clear_edges(ext, 1)
    clear_edges(exth, 2)
    clear_edges(extp, 1)
    clear_groups(recv)
    clear_groups(recv2)
    greet_wait(AXIS_PEERS)
    start_sides(send, recv, ss, rs)
    start_rows(ext, 1, rss, rrs)
    widen_own(ext, wide1_ref, 1, ROWS)

    def inner_pre(n, carry):
        m = pl.multiple_of(COLS + n * STEP, COLS)
        ing[pl.ds(m, STEP), :] = conv_block(wide1_ref, 1, k1_ref, m, STEP)
        return carry

    lax.fori_loop(0, 3, inner_pre, 0)
    wait_sides_recv(send, recv, ss, rs)
    wait_rows_recv(ext, 1, rss, rrs)
    open_slab(recv, 1, 0, me, rim)
    for edge in (0, ROWS - 1):
        widen_own(ext, wide1_ref, 0 if edge == 0 else ROWS + 1, 1)
        ing[edge * COLS : (edge + 1) * COLS, :] = conv_block(wide1_ref, 1, k1_ref, edge * COLS, COLS)
    side_part(rim, None, k1_ref, ing)

    def act(n, carry):
        m = pl.multiple_of(n * STEP, STEP)
        pre = ing[pl.ds(m, STEP), :]
        s = jax.nn.sigmoid(pre)
        hid = (pre * s).astype(BF16)
        grad = (hg_ref[pl.ds(m, STEP), :] * s * (1.0 + pre * (1.0 - s))).astype(BF16)
        for q in range(STEP // COLS):
            row = n * (STEP // COLS) + q
            exth[2 + row] = hid[q * COLS : (q + 1) * COLS]
            extp[1 + row] = grad[q * COLS : (q + 1) * COLS]
        pg_ref[pl.ds(m, STEP), :] = grad
        return carry

    lax.fori_loop(0, CELLS // STEP, act, 0)
    make_slab(extp, 1, send2, 16, me, tmp)
    make_slab(exth, 2, send2, 0, me, tmp)
    start_sides(send2, recv2, ss2, rs2)
    start_rows(extp, 1, rssp, rrsp)
    start_rows(exth, 2, rssh, rrsh)
    widen_own(extp, widep, 1, ROWS)

    def inner_fold(n, carry):
        m = pl.multiple_of(COLS + n * STEP, COLS)
        ing[pl.ds(m, STEP), :] = g_ref[pl.ds(m, STEP), :].astype(F32) + conv_block(widep, 1, k1t_ref, m, STEP)
        return carry

    lax.fori_loop(0, 3, inner_fold, 0)
    patch_sides(wide1_ref, rim)
    wait_sides_recv(send2, recv2, ss2, rs2)
    wait_rows_recv(extp, 1, rssp, rrsp)
    open_slab(recv2, 1, 16, me, rim)
    split_rim(rim, 1, me, before, after, trim)
    for edge in (0, ROWS - 1):
        widen_own(extp, widep, 0 if edge == 0 else ROWS + 1, 1)
        ing[edge * COLS : (edge + 1) * COLS, :] = g_ref[edge * COLS : (edge + 1) * COLS, :].astype(F32) + conv_block(
            widep, 1, k1t_ref, edge * COLS, COLS
        )
    side_part(rim, trim, k1t_ref, ing)
    for q in range(4):
        part = ing[q * 256 : (q + 1) * 256, :].astype(BF16)
        rounded[q * 16 : (q + 1) * 16] = part.reshape(16, BT, CH)

    for half in (0, 1):

        def pick(q, carry):
            block = rounded[ids[half, q]]
            y, zh, x = lax.div(q, 32), lax.rem(lax.div(q, 16), 2), lax.rem(lax.div(q, 4), 4)
            zl, c = lax.rem(lax.div(q, 2), 2), lax.rem(q, 2)
            b0[half, y, zh, x, zl, c] = block[:, 0:128]
            b0[2 + half, y, zh, x, zl, c] = block[:, 128:256]
            return carry

        lax.fori_loop(0, PAIRS, pick, 0, unroll=4)
        swap.core_start(half)
        swap.core_start(2 + half)

    def hidden_rows():
        wait_rows_recv(exth, 2, rssh, rrsh)
        open_slab(recv2, 2, 0, me, rim2)
        widen(exth, 2, rim2, wide2_ref)

    def kernel_grads(o):
        acc[1, o] = lax.dot_general(
            wide2_ref[o * 2 * COLS : o * 2 * COLS + CELLS, :],
            g_ref[...],
            (((0,), (0,)), ((), ())),
            preferred_element_type=F32,
        )
        acc[0, o] = lax.dot_general(
            wide1_ref[o * COLS : o * COLS + CELLS, :],
            pg_ref[...],
            (((0,), (0,)), ((), ())),
            preferred_element_type=F32,
        )
        sums.start(o)

    def mixed():
        def block(n, carry):
            m = pl.multiple_of(n * STEP, STEP)
            mixed_ref[pl.ds(m, STEP), :] = (
                x_ref[pl.ds(m // COLS, STEP // COLS)].reshape(STEP, CH).astype(F32)
                + conv_block(wide2_ref, 2, k2_ref, m, STEP)
            ).astype(BF16)
            return carry

        lax.fori_loop(0, CELLS // STEP, block, 0)

    def spread_weights():
        w = w_ref[...]
        ps = ps_ref[0:1, :]
        for n in range(SB):
            wexp[n * BL : (n + 1) * BL, :] = w * (ps == n).astype(F32).astype(BF16)

    def source():
        def take(p, carry):
            q = slot[p]
            half, t = lax.div(q, PAIRS), lax.rem(q, PAIRS)
            y, zh, x = lax.div(t, 32), lax.rem(lax.div(t, 16), 2), lax.rem(lax.div(t, 4), 4)
            zl, c = lax.rem(lax.div(t, 2), 2), lax.rem(t, 2)
            at = pl.ds(pl.multiple_of(p * BT, BT), BT)
            rows[at, 0:128] = b4[half, y, zh, x, zl, c]
            rows[at, 128:256] = b4[2 + half, y, zh, x, zl, c]
            return carry

        lax.fori_loop(0, PAIRS, take, 0, unroll=4)
        for m in range(4):
            source_ref[m * 256 : (m + 1) * 256, :] = jnp.dot(
                wexp[m * 256 : (m + 1) * 256, :], rows[...], preferred_element_type=F32
            ).astype(BF16)

    def drained():
        wait_sides_send(send, recv, ss, rs)
        wait_rows_send(ext, 1, rss, rrs)
        wait_sides_send(send2, recv2, ss2, rs2)
        wait_rows_send(exth, 2, rssh, rrsh)
        wait_rows_send(extp, 1, rssp, rrsp)
        swap.drain(0, 1)

    steps = {
        "x": drained, "y": lambda: swap.drain(2),
        "H": hidden_rows, "K": kernel_grads, "M": mixed, "W": spread_weights, "S": source,
        "a": lambda u: swap.advance(0, u), "b": lambda u: swap.advance(1, u),
        "c": lambda u: swap.advance(2, u), "d": lambda u: swap.wait(2, u),
        "2": sums.to_second, "3": sums.to_third, "4": sums.to_fourth,
        "5": sums.to_fifth, "6": sums.to_sixth, "7": sums.to_seventh,
    }
    for word in ORDER:
        if len(word) == 1:
            steps[word]()
        for n in word[1:]:
            steps[word[0]](int(n))
    sums.finish()


def mid(flip, ids, slot, x, hidden_grad, grad, k1, k1t, k2, w_cells, ps_cells):
    dma = pltpu.SemaphoreType.DMA
    three, nine = [dma((3,))] * 2, [dma((3, 3))] * 2
    return pl.pallas_call(
        mid_kernel,
        name="middle",
        out_shape=(
            jax.ShapeDtypeStruct((CELLS, CH), BF16),
            jax.ShapeDtypeStruct((2, 3, PART, CH), BF16),
            jax.ShapeDtypeStruct((SB * BL, CH), BF16),
        ),
        in_specs=[SM, SM, SM] + [VM] * 8,
        out_specs=(VM, VM, VM),
        scratch_shapes=[
            pltpu.VMEM((ROWS + 2, COLS, CH), BF16),
            pltpu.VMEM((ROWS + 4, COLS, CH), BF16),
            pltpu.VMEM((ROWS + 2, COLS, CH), BF16),
            pltpu.VMEM((2, 16, CH), BF16),
            pltpu.VMEM((2, 3, 16, CH), BF16),
            pltpu.VMEM((2, 32, CH), BF16),
            pltpu.VMEM((2, 3, 32, CH), BF16),
            pltpu.VMEM((2, 16, CH), F32),
            pltpu.VMEM((2, 1, 16, CH), F32),
            pltpu.VMEM((2, 2, 16, CH), F32),
            pltpu.VMEM((2, 1, 16, CH), F32),
            pltpu.VMEM(((ROWS + 2) * COLS, 3 * CH), BF16),
            pltpu.VMEM(((ROWS + 4) * COLS, 3 * CH), BF16),
            pltpu.VMEM(((ROWS + 2) * COLS, 3 * CH), BF16),
            pltpu.VMEM((CELLS, CH), BF16),
            pltpu.VMEM((CELLS, CH), F32),
            pltpu.VMEM((BLOCKS, BT, CH), BF16),
            *[pltpu.VMEM(WORLD, BF16)] * 5,
            pltpu.VMEM((PAIRS * BT, CH), BF16),
            pltpu.VMEM((SB * BL, PAIRS * BT), BF16),
            pltpu.VMEM((2, 3, PART, CH), F32),
            pltpu.VMEM((3, PART, CH), BF16),
            pltpu.VMEM((3, PART, CH), BF16),
            pltpu.VMEM((3, PART, CH), BF16),
            pltpu.VMEM((3, 3, 192, CH), BF16),
            pltpu.VMEM((3, 192, CH), BF16),
            pltpu.VMEM((3, 3, 48, CH), BF16),
            pltpu.VMEM((3, 4, 48, CH), BF16),
            dma((2, 3)), dma((2, 3)), dma((2,)), dma((2,)),
            dma((2, 3)), dma((2, 3)), dma((2,)), dma((2,)), dma((2,)), dma((2,)),
            *three, *nine, *nine, *nine, *nine, *nine, *three,
            *swap_sems(),
        ],
        compiler_params=pltpu.CompilerParams(vmem_limit_bytes=42 * 2**20, collective_id=2, has_side_effects=True),
        cost_estimate=pl.CostEstimate(flops=6 * 2**30, bytes_accessed=12 * 2**20, transcendentals=2**18),
    )(flip, ids, slot, x, hidden_grad, grad, k1, k1t, k2, w_cells, ps_cells)


PART = 3 * CH


def axes_of(o):
    return o, (o + 1) % 3, (o + 2) % 3


class Sums:
    def __init__(self, out, acc, send1, recv1, sent2, got2, sent3, got3, got4, sems):
        self.out, self.acc, self.send1, self.recv1 = out, acc, send1, recv1
        self.sent2, self.got2, self.sent3, self.got3, self.got4, self.sems = sent2, got2, sent3, got3, got4, sems
        t, b, tiles, bands = place_in_mesh()
        self.place = spot(t, b)
        self.core = self.place[3]

    def first(self, o):
        s, r = self.sems[0:2]
        return remote(self.send1.at[o], self.recv1.at[o], s.at[o], r.at[o], twin())

    def second(self, o, k):
        s, r = self.sems[2:4]
        a = axes_of(o)[0]
        at = pl.ds(pl.multiple_of(lax.rem(self.place[a] + k, 4) * 192, 64), 192)
        return remote(self.sent2.at[o, at], self.got2.at[o, k - 1], s.at[o, k - 1], r.at[o, k - 1], axis_peer(a, k))

    def third(self, o, k):
        s, r = self.sems[4:6]
        a = axes_of(o)[1]
        at = pl.ds(pl.multiple_of(lax.rem(self.place[a] + k, 4) * 48, 16), 48)
        return remote(self.sent3.at[o, at], self.got3.at[o, k - 1], s.at[o, k - 1], r.at[o, k - 1], axis_peer(a, k))

    def fourth(self, o, k):
        s, r = self.sems[6:8]
        a = axes_of(o)[2]
        mine = self.got4.at[o, self.place[a]]
        return remote(mine, mine, s.at[o, k - 1], r.at[o, k - 1], axis_peer(a, k))

    def rows(self, o, wide):
        a, c, _ = axes_of(o)
        if wide:
            return pl.ds(pl.multiple_of(self.place[a] * 192, 64), 192)
        return pl.ds(pl.multiple_of(self.place[a] * 192 + self.place[c] * 48, 16), 48)

    def fifth(self, o, k):
        s, r = self.sems[8:10]
        rows = self.out.at[self.core, o, self.rows(o, False)]
        return remote(rows, rows, s.at[o, k - 1], r.at[o, k - 1], axis_peer(axes_of(o)[1], k))

    def sixth(self, o, k):
        s, r = self.sems[10:12]
        rows = self.out.at[self.core, o, self.rows(o, True)]
        return remote(rows, rows, s.at[o, k - 1], r.at[o, k - 1], axis_peer(axes_of(o)[0], k))

    def seventh(self, o):
        s, r = self.sems[12:14]
        whole = self.out.at[self.core, o]
        return remote(whole, whole, s.at[o], r.at[o], twin())

    def start(self, o):
        self.send1[o] = self.acc[1 - self.core, o].astype(BF16)
        self.first(o).start()

    def to_second(self, o):
        self.first(o).wait_recv()
        total = self.acc[self.core, o] + self.recv1[o].astype(F32)
        self.acc[self.core, o] = total
        self.sent2[o] = total.astype(BF16)
        for k in (2, 1, 3):
            self.second(o, k).start()

    def to_third(self, o):
        for k in (1, 2, 3):
            self.second(o, k).wait_recv()
        total = self.acc[self.core, o, self.rows(o, True), :]
        for k in (1, 2, 3):
            total = total + self.got2[o, k - 1].astype(F32)
        self.acc[self.core, o, 0:192, :] = total
        self.sent3[o] = total.astype(BF16)
        for k in (2, 1, 3):
            self.third(o, k).start()

    def to_fourth(self, o):
        a, c, e = axes_of(o)
        for k in (1, 2, 3):
            self.third(o, k).wait_recv()
        total = self.acc[self.core, o, pl.ds(pl.multiple_of(self.place[c] * 48, 16), 48), :]
        for k in (1, 2, 3):
            total = total + self.got3[o, k - 1].astype(F32)
        self.got4[o, self.place[e]] = total.astype(BF16)
        for k in (2, 1, 3):
            self.fourth(o, k).start()

    def to_fifth(self, o):
        for k in (1, 2, 3):
            self.fourth(o, k).wait_recv()
        v = [self.got4[o, q].astype(F32) for q in range(4)]
        self.out[self.core, o, self.rows(o, False), :] = (((v[0] + v[1]) + v[2]) + v[3]).astype(BF16)
        for k in (2, 1, 3):
            self.fifth(o, k).start()

    def to_sixth(self, o):
        for k in (1, 2, 3):
            self.fifth(o, k).wait_recv()
        for k in (2, 1, 3):
            self.sixth(o, k).start()

    def to_seventh(self, o):
        for k in (1, 2, 3):
            self.sixth(o, k).wait_recv()
        self.seventh(o).start()

    def finish(self):
        for o in range(3):
            self.first(o).wait_send()
            for k in (1, 2, 3):
                for step in (self.second, self.third, self.fourth, self.fifth, self.sixth):
                    step(o, k).wait_send()
        for o in range(3):
            self.seventh(o).wait()


def finish_kernel(sums, mixed, source, one, two, mixed_out, source_out, wide, sems):
    copies = [
        pltpu.make_async_copy(mixed, mixed_out, sems.at[6]),
        pltpu.make_async_copy(source, source_out, sems.at[7]),
    ]
    for copy in copies:
        copy.start()
    for n, out in ((0, one), (1, two)):
        for i in range(3):
            wide[n, i] = sums[n, i].astype(F32)
            copy = pltpu.make_async_copy(wide.at[n, i], out.at[i], sems.at[n * 3 + i])
            copy.start()
            copies.append(copy)
    for copy in copies:
        copy.wait()


def finish(sums, mixed, source):
    away = pl.BlockSpec(memory_space=pltpu.HBM)
    return pl.pallas_call(
        finish_kernel,
        name="finish",
        out_shape=(
            jax.ShapeDtypeStruct((3, PART, CH), F32),
            jax.ShapeDtypeStruct((3, PART, CH), F32),
            jax.ShapeDtypeStruct((CELLS, CH), BF16),
            jax.ShapeDtypeStruct((SB * BL, CH), BF16),
        ),
        in_specs=[VM] * 3,
        out_specs=(away,) * 4,
        scratch_shapes=[pltpu.VMEM((2, 3, PART, CH), F32), pltpu.SemaphoreType.DMA((8,))],
        compiler_params=params(),
        cost_estimate=pl.CostEstimate(flops=2**20, bytes_accessed=8 * 2**20, transcendentals=0),
    )(sums, mixed, source)


def local(
    source_cells, regrid_weights, pair_target, pair_block, pair_source, flip_codes, kernel_one, kernel_two, out_grad
):
    target = pair_target[:, 0]
    outgoing, slot = regrid(target, pair_source, regrid_weights, source_cells)
    upstream = out_grad[0]
    hidden_grad, k1_back, arrived, ids, safe_ids, w_cells, ps_cells = back(
        flip_codes,
        pair_target.reshape(1, PAIRS),
        pair_block.reshape(1, PAIRS),
        pair_source.reshape(1, PAIRS),
        regrid_weights,
        upstream,
        kernel_one,
        kernel_two,
        outgoing.reshape(WORLD),
    )
    regridded = gather_sum(ids, arrived.reshape(2, 2 * PAIRS, BT, 128))
    mixed, sums, source_grad = mid(
        flip_codes,
        safe_ids,
        slot,
        regridded.reshape(ROWS, COLS, CH),
        hidden_grad,
        upstream.reshape(CELLS, CH),
        kernel_one.reshape(3, PART, CH),
        k1_back,
        kernel_two.reshape(3, PART, CH),
        w_cells,
        ps_cells,
    )
    one, two, mixed, source_grad = finish(sums, mixed, source_grad)
    return (
        mixed.reshape(1, ROWS, COLS, CH),
        one.reshape(3, 3, CH, CH),
        two.reshape(3, 3, CH, CH),
        source_grad,
    )


def solution(mesh):
    placed = (
        P(("tile", "band"), None),
        P(("tile", "band"), None, None),
        P(("tile", "band"), None),
        P(("tile", "band")),
        P(("tile", "band")),
        P(),
        P(),
        P(),
        P("tile", "band", None, None),
    )
    return jax.shard_map(
        local,
        mesh=mesh,
        in_specs=placed,
        out_specs=(P("tile", "band", None, None), P(), P(), P(("tile", "band"), None)),
        check_vma=False,
    )
```

```python
import jax
import jax.numpy as jnp
from jax import lax
from jax.experimental import pallas as pl
from jax.experimental.pallas import tpu as pltpu
from jax.sharding import PartitionSpec as P

F32 = jnp.float32
BF16 = jnp.bfloat16
MESH = pl.DeviceIdType.MESH
VM = pl.BlockSpec(memory_space=pltpu.VMEM)
SM = pl.BlockSpec(memory_space=pltpu.SMEM)
FAR = pl.BlockSpec(memory_space=pltpu.HBM)
LIMIT = 16 * 2**20
ROWS, COLS, CH = 8, 128, 256
PAIRS, BT, BL, SB, BLOCKS = 128, 16, 64, 16, 64
CELLS = ROWS * COLS


def params(**more):
    return pltpu.CompilerParams(vmem_limit_bytes=LIMIT, **more)


def regrid_kernel(pair_far, w_ref, src_far, out_ref, slot_ref, cnt, masks, wexp, pair, src_ref, sems):
    copies = [
        pltpu.make_async_copy(pair_far, pair, sems.at[0]),
        pltpu.make_async_copy(src_far, src_ref, sems.at[1]),
    ]
    for copy in copies:
        copy.start()
    lane = lax.broadcasted_iota(jnp.int32, (BT, 128), 1)
    masks[0] = (lane < BL).astype(F32).astype(BF16)
    masks[1] = (lane >= BL).astype(F32).astype(BF16)
    wexp[...] = jnp.zeros_like(wexp)

    def clear(i, c):
        cnt[i] = 0
        return c

    lax.fori_loop(0, PAIRS, clear, 0, unroll=8)
    copies[0].wait()

    def place(p, c):
        named = pair[p]
        t = lax.shift_right_logical(named, 4)
        r = cnt[t]
        cnt[t] = r + 1
        slot_ref[p] = jnp.minimum(r, 1) * PAIRS + t
        s = lax.bitwise_and(named, SB - 1)
        w = w_ref[p]
        ww = jnp.concatenate([w, w], axis=1) * masks[lax.rem(s, 2)]
        row = pl.multiple_of(p * BT, BT)
        col = pl.multiple_of((s // 2) * 128, 128)
        wexp[pl.ds(row, BT), pl.ds(col, 128)] = ww
        return c

    lax.fori_loop(0, PAIRS, place, 0, unroll=8)
    copies[1].wait()
    for m in range(4):
        part = jnp.dot(wexp[m * 512 : (m + 1) * 512, :], src_ref[...], preferred_element_type=F32).astype(BF16)
        for q in range(32):
            at = slot_ref[m * 32 + q]
            for h in (0, 1):
                out_ref[h, at] = part[q * BT : (q + 1) * BT, h * 128 : (h + 1) * 128]


def regrid(named, weights, source):
    return pl.pallas_call(
        regrid_kernel,
        name="regrid",
        out_shape=(
            jax.ShapeDtypeStruct((2, 2 * PAIRS, BT, 128), BF16),
            jax.ShapeDtypeStruct((PAIRS,), jnp.int32),
        ),
        in_specs=[FAR, VM, FAR],
        out_specs=(VM, SM),
        scratch_shapes=[
            pltpu.SMEM((PAIRS,), jnp.int32),
            pltpu.VMEM((2, BT, 128), BF16),
            pltpu.VMEM((PAIRS * BT, SB * BL), BF16),
            pltpu.SMEM((PAIRS,), jnp.int32),
            pltpu.VMEM((SB * BL, CH), BF16),
            pltpu.SemaphoreType.DMA((2,)),
        ],
        compiler_params=params(),
        cost_estimate=pl.CostEstimate(flops=2 * 2048 * 1024 * 256, bytes_accessed=6 * 2**20, transcendentals=0),
    )(named, weights, source)


def gather_sum_kernel(ids, got_ref, out_ref, acc, more):
    acc[...] = jnp.zeros_like(acc)
    more[...] = jnp.zeros_like(more)

    def add(q, c):
        k, n = ids[0, q], ids[1, q]
        for h in (0, 1):
            acc[h, k] += got_ref[h, q].astype(F32)
            more[h, n] += got_ref[h, PAIRS + q].astype(F32)
        return c

    lax.fori_loop(0, PAIRS, add, 0, unroll=8)
    for h in (0, 1):
        out_ref[:, :, h * 128 : (h + 1) * 128] = (acc[h, 0:BLOCKS] + more[h, 0:BLOCKS]).astype(BF16)


def gather_sum(ids, arrived):
    return pl.pallas_call(
        gather_sum_kernel,
        name="gather_sum",
        out_shape=jax.ShapeDtypeStruct((BLOCKS, BT, CH), BF16),
        in_specs=[SM, VM],
        out_specs=VM,
        scratch_shapes=[pltpu.VMEM((2, BLOCKS + 1, BT, 128), F32)] * 2,
        compiler_params=params(),
        cost_estimate=pl.CostEstimate(flops=2**21, bytes_accessed=3 * 2**20, transcendentals=0),
    )(ids, arrived)


def place_in_mesh():
    return lax.axis_index("tile"), lax.axis_index("band"), lax.axis_size("tile"), lax.axis_size("band")


def greet():
    t, b, tiles, bands = place_in_mesh()
    barrier = pltpu.get_barrier_semaphore()
    for dt in (1, -1, 0):
        for db in (-1, 0, 1):
            if dt == 0 and db == 0:
                continue

            def say(dt=dt, db=db):
                pl.semaphore_signal(
                    barrier, inc=1, device_id=(lax.rem(t + dt + tiles, tiles), b + db), device_id_type=MESH
                )

            near_band(b, bands, db, say)


def greet_wait(others):
    b, bands = lax.axis_index("band"), lax.axis_size("band")
    near = 2 + jnp.where(b > 0, 3, 0) + jnp.where(b < bands - 1, 3, 0)
    pl.semaphore_wait(pltpu.get_barrier_semaphore(), near + others)


def near_band(b, bands, db, action):
    if db == 0:
        action()
    elif db < 0:
        pl.when(b > 0)(action)
    else:
        pl.when(b < bands - 1)(action)


def side_copy(send, recv, ss, rs, way, db, group):
    t, b, tiles, bands = place_in_mesh()
    to = lax.rem(t + (1 if way == 0 else tiles - 1), tiles)
    return pltpu.make_async_remote_copy(
        src_ref=send.at[way],
        dst_ref=recv.at[way, group],
        send_sem=ss.at[way, 1 + db],
        recv_sem=rs.at[way, group],
        device_id=(to, b + db),
        device_id_type=MESH,
    )


def row_copy(ext, d, ss, rs, db):
    t, b, tiles, bands = place_in_mesh()
    if db < 0:
        src, dst, k = ext.at[pl.ds(d, d)], ext.at[pl.ds(ROWS + d, d)], 0
    else:
        src, dst, k = ext.at[pl.ds(ROWS, d)], ext.at[pl.ds(0, d)], 1
    return pltpu.make_async_remote_copy(
        src_ref=src, dst_ref=dst, send_sem=ss.at[k], recv_sem=rs.at[k], device_id=(t, b + db), device_id_type=MESH
    )


def start_sides(send, recv, ss, rs):
    b, bands = lax.axis_index("band"), lax.axis_size("band")
    for way in (0, 1):
        for db in (0, -1, 1):
            near_band(b, bands, db, lambda way=way, db=db: side_copy(send, recv, ss, rs, way, db, 1 - db).start())


def start_rows(ext, d, ss, rs):
    b, bands = lax.axis_index("band"), lax.axis_size("band")
    for db in (-1, 1):
        near_band(b, bands, db, lambda db=db: row_copy(ext, d, ss, rs, db).start())


def wait_sides_recv(send, recv, ss, rs):
    b, bands = lax.axis_index("band"), lax.axis_size("band")
    for way in (0, 1):
        for db in (0, -1, 1):
            near_band(b, bands, db, lambda way=way, db=db: side_copy(send, recv, ss, rs, way, 0, 1 + db).wait_recv())


def wait_sides_send(send, recv, ss, rs):
    b, bands = lax.axis_index("band"), lax.axis_size("band")
    for way in (0, 1):
        for db in (0, -1, 1):
            near_band(b, bands, db, lambda way=way, db=db: side_copy(send, recv, ss, rs, way, db, 1 - db).wait_send())


def wait_rows_recv(ext, d, ss, rs):
    b, bands = lax.axis_index("band"), lax.axis_size("band")
    near_band(b, bands, -1, lambda: row_copy(ext, d, ss, rs, 1).wait_recv())
    near_band(b, bands, 1, lambda: row_copy(ext, d, ss, rs, -1).wait_recv())


def wait_rows_send(ext, d, ss, rs):
    b, bands = lax.axis_index("band"), lax.axis_size("band")
    for db in (-1, 1):
        near_band(b, bands, db, lambda db=db: row_copy(ext, d, ss, rs, db).wait_send())


def clear_edges(ext, d):
    b, bands = lax.axis_index("band"), lax.axis_size("band")

    @pl.when(b == 0)
    def _():
        ext[0:d] = jnp.zeros((d, COLS, CH), BF16)

    @pl.when(b == bands - 1)
    def _():
        ext[ROWS + d : ROWS + 2 * d] = jnp.zeros((d, COLS, CH), BF16)


def clear_groups(recv):
    b, bands = lax.axis_index("band"), lax.axis_size("band")
    for way in (0, 1):

        @pl.when(b == 0)
        def _():
            recv[way, 0] = jnp.zeros(recv.shape[2:], BF16)

        @pl.when(b == bands - 1)
        def _():
            recv[way, 2] = jnp.zeros(recv.shape[2:], BF16)


def flags(flip):
    t, b, tiles, bands = place_in_mesh()
    me = flip[t]
    before = flip[lax.rem(t + tiles - 1, tiles)]
    after = flip[lax.rem(t + 1, tiles)]
    return me, before, after


def make_slab(ext, d, send, base, flip_me, tmp):
    if d == 1:
        tmp[...] = jnp.zeros_like(tmp)
    for r in range(ROWS):
        first = ext[d + r, 0:16, :].astype(F32)
        last = ext[d + r, COLS - 16 : COLS, :].astype(F32)
        for k in range(d):
            tmp[0, k * 8 + r : k * 8 + r + 1, :] = first[k : k + 1]
            tmp[1, k * 8 + r : k * 8 + r + 1, :] = last[15 - k : 16 - k]
    turned = jnp.full((16, CH), flip_me, jnp.int32) == 1
    left, right = tmp[0], tmp[1]
    send[0, base : base + 16] = jnp.where(turned, left, right).astype(BF16)
    send[1, base : base + 16] = jnp.where(turned, right, left).astype(BF16)


def open_slab(recv, d, base, flip_me, rim):
    turned = jnp.full((16, CH), flip_me, jnp.int32) == 1
    for g in range(3):
        before = recv[0, g, base : base + 16].astype(F32)
        after = recv[1, g, base : base + 16].astype(F32)
        sides = (jnp.where(turned, after, before), jnp.where(turned, before, after))
        for side in (0, 1):
            for k in range(d):
                part = sides[side][k * 8 : k * 8 + 8]
                if g == 0:
                    rim[side, k, 0:d, :] = part[8 - d :]
                elif g == 1:
                    rim[side, k, d : d + 8, :] = part
                else:
                    rim[side, k, d + 8 : 2 * d + 8, :] = part[:d]


def split_rim(rim, d, flip_me, flip_before, flip_after, turned_rim):
    odd_before = (flip_before != flip_me).astype(jnp.int32)
    odd_after = (flip_after != flip_me).astype(jnp.int32)
    odd_left = jnp.where(flip_me == 0, odd_before, odd_after)
    odd_right = jnp.where(flip_me == 0, odd_after, odd_before)
    for side, odd in ((0, odd_left), (1, odd_right)):
        mask = jnp.full((16, CH), odd, jnp.int32) == 1
        for k in range(d):
            whole = rim[side, k]
            turned_rim[side, k] = jnp.where(mask, whole, 0.0)
            rim[side, k] = jnp.where(mask, 0.0, whole)


def widen(ext, d, rim, wide):
    col = lax.broadcasted_iota(jnp.int32, (COLS, CH), 0)

    def one(row, carry):
        mid = ext[row]
        x = mid.astype(F32)
        left = pltpu.roll(x, d, 0)
        right = pltpu.roll(x, COLS - d, 0)
        for k in range(d):
            near = jnp.broadcast_to(rim[0, k, pl.ds(row, 1), :], (COLS, CH))
            left = jnp.where(col == d - 1 - k, near, left)
            near = jnp.broadcast_to(rim[1, k, pl.ds(row, 1), :], (COLS, CH))
            right = jnp.where(col == COLS - d + k, near, right)
        at = pl.ds(pl.multiple_of(row * COLS, COLS), COLS)
        wide[at, 0:CH] = left.astype(BF16)
        wide[at, CH : 2 * CH] = mid
        wide[at, 2 * CH : 3 * CH] = right.astype(BF16)
        return carry

    lax.fori_loop(0, ROWS + 2 * d, one, 0)


def widen_own(ext, wide, first, count):
    col = lax.broadcasted_iota(jnp.int32, (COLS, CH), 0)

    def one(row, carry):
        mid = ext[row]
        x = mid.astype(F32)
        left = jnp.where(col == 0, 0.0, pltpu.roll(x, 1, 0))
        right = jnp.where(col == COLS - 1, 0.0, pltpu.roll(x, COLS - 1, 0))
        at = pl.ds(pl.multiple_of(row * COLS, COLS), COLS)
        wide[at, 0:CH] = left.astype(BF16)
        wide[at, CH : 2 * CH] = mid
        wide[at, 2 * CH : 3 * CH] = right.astype(BF16)
        return carry

    lax.fori_loop(first, first + count, one, 0)


def side_part(rim, turned_rim, taps, out):
    total = None
    none = jnp.zeros((ROWS, CH), F32)
    for i in range(3):
        near = [rim[side, 0, i : i + ROWS, :] for side in (0, 1)]
        turned = [none, none] if turned_rim is None else [turned_rim[side, 0, i : i + ROWS, :] for side in (0, 1)]
        lhs = jnp.concatenate(
            [
                jnp.concatenate([near[0], none, turned[0]], axis=1),
                jnp.concatenate([turned[1], none, near[1]], axis=1),
            ],
            axis=0,
        )
        part = jnp.dot(lhs.astype(BF16), taps[i], preferred_element_type=F32)
        total = part if total is None else total + part
    for r in range(ROWS):
        at = r * COLS
        out[at : at + 1, :] += total[r : r + 1]
        at = r * COLS + COLS - 1
        out[at : at + 1, :] += total[ROWS + r : ROWS + r + 1]


def patch_sides(wide, rim):
    row = lax.broadcasted_iota(jnp.int32, (16, CH), 0)
    for r in range(ROWS + 2):
        at = r * COLS
        tile = wide[at : at + 16, 0:CH].astype(F32)
        near = jnp.broadcast_to(rim[0, 0, r : r + 1, :], (16, CH))
        wide[at : at + 16, 0:CH] = jnp.where(row == 0, near, tile).astype(BF16)
        at = r * COLS + COLS - 16
        tile = wide[at : at + 16, 2 * CH : 3 * CH].astype(F32)
        near = jnp.broadcast_to(rim[1, 0, r : r + 1, :], (16, CH))
        wide[at : at + 16, 2 * CH : 3 * CH] = jnp.where(row == 15, near, tile).astype(BF16)


def conv_block(wide, d, taps, m, rows):
    total = None
    for i in range(3):
        lhs = wide[pl.ds(pl.multiple_of(m + i * d * COLS, COLS), rows), :]
        part = jnp.dot(lhs, taps[i], preferred_element_type=F32)
        total = part if total is None else total + part
    return total


def turned_part(turned_rim, d, taps, out):
    left, right = None, None
    for i in range(3):
        lhs_left = jnp.concatenate([turned_rim[0, d - 1 - c, i * d : i * d + 8, :] for c in range(d)], axis=0)
        lhs_right = jnp.concatenate([turned_rim[1, c, i * d : i * d + 8, :] for c in range(d)], axis=0)
        a = jnp.dot(lhs_left.astype(BF16), taps[i, 2 * CH : 3 * CH, :], preferred_element_type=F32)
        z = jnp.dot(lhs_right.astype(BF16), taps[i, 0:CH, :], preferred_element_type=F32)
        left = a if left is None else left + a
        right = z if right is None else right + z
    for c in range(d):
        for r in range(ROWS):
            at = r * COLS + c
            out[at : at + 1, :] += left[c * 8 + r : c * 8 + r + 1]
            at = r * COLS + COLS - d + c
            out[at : at + 1, :] += right[c * 8 + r : c * 8 + r + 1]


STEP = 256


def spot(t, b):
    x = lax.rem(t, 4)
    y = lax.div(t, 8)
    z = lax.rem(lax.div(t, 4), 2) * 2 + lax.div(b, 2)
    return x, y, z, lax.rem(b, 2)


def device_at(x, y, z, core):
    return (y * 8 + lax.div(z, 2) * 4 + x, lax.rem(z, 2) * 2 + core)


WORLD = (4, 4, 2, 4, 2, 2, BT, 128)
UNITS = [(hs, other) for other in (0, 1) for hs in range(4)]


def axis_peer(axis, k):
    t, b, tiles, bands = place_in_mesh()
    at = list(spot(t, b))
    at[axis] = lax.rem(at[axis] + k, 4)
    return device_at(*at)


def twin():
    t, b, tiles, bands = place_in_mesh()
    return (t, b + 1 - 2 * lax.rem(b, 2))


def greet_axes():
    barrier = pltpu.get_barrier_semaphore()
    pl.semaphore_signal(barrier, inc=1, device_id=twin(), device_id_type=MESH)
    for axis in range(3):
        for k in (1, 2, 3):
            pl.semaphore_signal(barrier, inc=1, device_id=axis_peer(axis, k), device_id_type=MESH)


AXIS_PEERS = 10


def along(ref, unit, axis, v):
    hs, other = UNITS[unit]
    c = lax.rem(lax.axis_index("band") + other, 2)
    if axis == 0:
        return ref.at[hs, :, :, v, :, c]
    if axis == 1:
        return ref.at[hs, v, :, :, :, c]
    return ref.at[hs, :, lax.div(v, 2), :, lax.rem(v, 2), c]


def remote(src, dst, ss, rs, to):
    return pltpu.make_async_remote_copy(
        src_ref=src, dst_ref=dst, send_sem=ss, recv_sem=rs, device_id=to, device_id_type=MESH
    )


class Swap:
    def __init__(self, bufs, sems):
        self.bufs, self.sems = bufs, sems
        t, b, tiles, bands = place_in_mesh()
        self.place = spot(t, b)

    def core_copy(self, hs):
        me = self.place[3]
        src, dst = self.bufs[0], self.bufs[1]
        ss, rs = self.sems[0], self.sems[1]
        return remote(
            src.at[hs, :, :, :, :, 1 - me], dst.at[hs, :, :, :, :, me], ss.at[hs], rs.at[hs], twin()
        )

    def core_start(self, hs):
        self.core_copy(hs).start()

    def source(self, stage, u):
        return self.bufs[0] if stage == 0 and UNITS[u][1] == 0 else self.bufs[1 + stage]

    def hop(self, stage, u, k):
        axis = (u + stage) % 3
        me = self.place[axis]
        src, dst = self.source(stage, u), self.bufs[2 + stage]
        return remote(
            along(src, u, axis, lax.rem(me + k, 4)), along(dst, u, axis, me),
            self.sems[2].at[stage, u, k - 1], self.sems[3].at[stage, u, k - 1], axis_peer(axis, k),
        )

    def own(self, stage, u):
        axis = (u + stage) % 3
        me = self.place[axis]
        src, dst = self.source(stage, u), self.bufs[2 + stage]
        return pltpu.make_async_copy(along(src, u, axis, me), along(dst, u, axis, me), self.sems[4].at[stage, u])

    def start(self, stage, u):
        for k in (2, 1, 3):
            self.hop(stage, u, k).start()
        self.own(stage, u).start()

    def wait(self, stage, u):
        for k in (1, 2, 3):
            self.hop(stage, u, k).wait_recv()
        self.own(stage, u).wait()

    def advance(self, stage, u):
        if stage > 0:
            self.wait(stage - 1, u)
        elif UNITS[u][1] == 1:
            self.core_copy(UNITS[u][0]).wait_recv()
        self.start(stage, u)

    def first_stage(self, units):
        for u in units:
            self.advance(0, u)

    def next_stage(self, stage):
        for u in range(8):
            self.wait(stage - 1, u)
            self.start(stage, u)

    def last_wait(self):
        for u in range(8):
            self.wait(2, u)

    def drain(self, *stages):
        for stage in stages:
            if stage == 0:
                for hs in range(4):
                    self.core_copy(hs).wait_send()
            for u in range(8):
                for k in (1, 2, 3):
                    self.hop(stage, u, k).wait_send()


def swap_sems():
    dma = pltpu.SemaphoreType.DMA
    return [dma((4,)), dma((4,)), dma((3, 8, 3)), dma((3, 8, 3)), dma((3, 8))]


def table_peer(stage, k):
    t, b, tiles, bands = place_in_mesh()
    x, y, z, core = spot(t, b)
    if stage == 0:
        return (t, lax.rem(b + k, 4))
    if stage == 1:
        return (t - x + lax.rem(x + k, 4), b)
    if stage == 2:
        return (t + 4 - 8 * lax.rem(lax.div(t, 4), 2), b)
    return (lax.rem(t + 8 * k, 32), b)


TABLE_PEERS = (3, 3, 1, 3)
TABLE_ROWS = (1, 4, 16, 32)


def table_copy(tab, ss, rs, stage, k):
    t, b, tiles, bands = place_in_mesh()
    n = TABLE_ROWS[stage]
    at = lax.div(t * 4 + b, n) * n
    rows = tab.at[pl.ds(at, n)]
    return pltpu.make_async_remote_copy(
        src_ref=rows, dst_ref=rows, send_sem=ss.at[stage, k - 1], recv_sem=rs.at[stage, k - 1],
        device_id=table_peer(stage, k), device_id_type=MESH,
    )


def table_start(tab, ss, rs, stage):
    for k in range(1, TABLE_PEERS[stage] + 1):
        table_copy(tab, ss, rs, stage, k).start()


def table_wait(tab, ss, rs, stage):
    for k in range(1, TABLE_PEERS[stage] + 1):
        table_copy(tab, ss, rs, stage, k).wait()


def greet_table():
    barrier = pltpu.get_barrier_semaphore()
    for stage in range(4):
        for k in range(1, TABLE_PEERS[stage] + 1):
            pl.semaphore_signal(barrier, inc=1, device_id=table_peer(stage, k), device_id_type=MESH)


def back_kernel(
    flip, tgt_ref, blk_ref, src_row, w_ref, g_ref, k1_ref, k2_ref, outgoing,
    hg_ref, k1t_ref, arrived, ids_ref, safe_ref, w_cells, ps_cells,
    tab, ext, send, recv, tmp, rim, trim, wide, k2t, b1, b2, b3, ss, rs, rss, rrs, tss, trs, *sems,
):
    d = 2
    swap = Swap((outgoing, b1, b2, b3, arrived), sems)
    greet_table()
    greet_axes()
    greet()
    t, b, tiles, bands = place_in_mesh()
    tab[t * 4 + b] = tgt_ref[...] * BLOCKS + blk_ref[...]
    me, before, after = flags(flip)
    ext[pl.ds(d, ROWS)] = g_ref[...]
    make_slab(ext, d, send, 0, me, tmp)
    clear_edges(ext, d)
    clear_groups(recv)
    greet_wait(sum(TABLE_PEERS) + AXIS_PEERS)
    table_start(tab, tss, trs, 0)
    start_sides(send, recv, ss, rs)
    start_rows(ext, d, rss, rrs)
    for hs in range(4):
        swap.core_start(hs)
    swap.first_stage(range(0, 4))
    table_wait(tab, tss, trs, 0)
    table_start(tab, tss, trs, 1)
    swap.first_stage(range(4, 8))
    for i in range(3):
        for j in range(3):
            k2t[i, j * CH : (j + 1) * CH, :] = k2_ref[2 - i, 2 - j].T
    wait_sides_recv(send, recv, ss, rs)
    wait_rows_recv(ext, d, rss, rrs)
    open_slab(recv, d, 0, me, rim)
    split_rim(rim, d, me, before, after, trim)
    table_wait(tab, tss, trs, 1)
    table_start(tab, tss, trs, 2)
    swap.next_stage(1)
    widen(ext, d, rim, wide)

    def block(n, carry):
        m = pl.multiple_of(n * STEP, STEP)
        hg_ref[pl.ds(m, STEP), :] = conv_block(wide, d, k2t, m, STEP)
        return carry

    lax.fori_loop(0, CELLS // STEP, block, 0)
    table_wait(tab, tss, trs, 2)
    table_start(tab, tss, trs, 3)
    swap.next_stage(2)
    turned_part(trim, d, k2t, hg_ref)
    for i in range(3):
        for j in range(3):
            k1t_ref[i, j * CH : (j + 1) * CH, :] = k1_ref[2 - i, 2 - j].T
    for n in range(SB):
        part = w_ref[n * 8 : (n + 1) * 8].reshape(128, BL).astype(F32)
        part = jnp.concatenate([part, part], axis=1).T
        w_cells[:, n * 128 : (n + 1) * 128] = part[0:BL].astype(BF16)
    spread = (
        lax.broadcasted_iota(jnp.int32, (PAIRS, PAIRS * BT), 1) // BT
        == lax.broadcasted_iota(jnp.int32, (PAIRS, PAIRS * BT), 0)
    ).astype(F32)
    own = jnp.broadcast_to(src_row[...], (8, PAIRS)).astype(F32)
    ps_cells[...] = jnp.dot(own.astype(BF16), spread.astype(BF16), preferred_element_type=F32)
    table_wait(tab, tss, trs, 3)
    table = tab[...].reshape(PAIRS, PAIRS).T
    order = lax.broadcasted_iota(jnp.int32, (PAIRS, PAIRS), 0)
    block_of = lax.bitwise_and(table, BLOCKS - 1)
    mine = lax.shift_right_logical(table, 6) == t * 4 + b
    first = jnp.min(jnp.where(mine, order, PAIRS), axis=0, keepdims=True)
    last = jnp.max(jnp.where(mine, order, -1), axis=0, keepdims=True)
    id_first = jnp.sum(jnp.where(order == first, block_of, 0), axis=0, keepdims=True)
    id_last = jnp.sum(jnp.where(order == last, block_of, 0), axis=0, keepdims=True)
    ids_ref[0:1, :] = jnp.where(first < PAIRS, id_first, BLOCKS)
    ids_ref[1:2, :] = jnp.where(last > first, id_last, BLOCKS)
    safe_ref[0:1, :] = id_first
    safe_ref[1:2, :] = id_last
    wait_sides_send(send, recv, ss, rs)
    wait_rows_send(ext, d, rss, rrs)
    swap.drain(0, 1)
    swap.last_wait()
    swap.drain(2)


def back(flip, target, block, source, weights, grad, k1, k2, outgoing):
    d = 2
    return pl.pallas_call(
        back_kernel,
        name="hidden_adjoint",
        out_shape=(
            jax.ShapeDtypeStruct((CELLS, CH), F32),
            jax.ShapeDtypeStruct((3, 3 * CH, CH), BF16),
            jax.ShapeDtypeStruct(WORLD, BF16),
            jax.ShapeDtypeStruct((2, PAIRS), jnp.int32),
            jax.ShapeDtypeStruct((2, PAIRS), jnp.int32),
            jax.ShapeDtypeStruct((BL, PAIRS * BT), BF16),
            jax.ShapeDtypeStruct((8, PAIRS * BT), F32),
        ),
        in_specs=[SM] + [VM] * 8,
        out_specs=(VM,) * 7,
        scratch_shapes=[
            pltpu.VMEM((PAIRS, 1, PAIRS), jnp.int32),
            pltpu.VMEM((ROWS + 2 * d, COLS, CH), BF16),
            pltpu.VMEM((2, 16, CH), BF16),
            pltpu.VMEM((2, 3, 16, CH), BF16),
            pltpu.VMEM((2, 16, CH), F32),
            pltpu.VMEM((2, d, 16, CH), F32),
            pltpu.VMEM((2, d, 16, CH), F32),
            pltpu.VMEM(((ROWS + 2 * d) * COLS, 3 * CH), BF16),
            pltpu.VMEM((3, 3 * CH, CH), BF16),
            pltpu.VMEM(WORLD, BF16),
            pltpu.VMEM(WORLD, BF16),
            pltpu.VMEM(WORLD, BF16),
            pltpu.SemaphoreType.DMA((2, 3)),
            pltpu.SemaphoreType.DMA((2, 3)),
            pltpu.SemaphoreType.DMA((2,)),
            pltpu.SemaphoreType.DMA((2,)),
            pltpu.SemaphoreType.DMA((4, 3)),
            pltpu.SemaphoreType.DMA((4, 3)),
            *swap_sems(),
        ],
        compiler_params=pltpu.CompilerParams(vmem_limit_bytes=18 * 2**20, collective_id=1, has_side_effects=True),
        cost_estimate=pl.CostEstimate(flops=6 * 2**30, bytes_accessed=8 * 2**20, transcendentals=0),
    )(flip, target, block, source, weights, grad, k1, k2, outgoing)


ORDER = (
    "a0123",
    "H",
    "K0",
    "a45",
    "K1",
    "20",
    "K2",
    "21",
    "a67",
    "22",
    "b012",
    "30",
    "b345",
    "M",
    "b67",
    "31",
    "32",
    "W",
    "c012",
    "4012",
    "c345",
    "5012",
    "c67",
    "6012",
    "x",
    "d01234567",
    "S",
    "7012",
    "y",
)


def mid_kernel(
    flip, ids, slot, x_ref, hg_ref, g_ref, k1_ref, k1t_ref, k2_ref, w_ref, ps_ref,
    mixed_ref, out_ref, source_ref,
    ext, exth, extp, send, recv, send2, recv2, tmp, rim, rim2, trim, wide1_ref, wide2_ref, widep, pg_ref, ing, rounded,
    b0, b1, b2, b3, b4, rows, wexp,
    acc, send1, recv1, sent2, got2, sent3, got3, got4,
    ss, rs, rss, rrs, ss2, rs2, rssh, rrsh, rssp, rrsp,
    s1, r1, s2, r2, s3, r3, s4, r4, s5, r5, s6, r6, s7, r7, *sems,
):
    swap = Swap((b0, b1, b2, b3, b4), sems)
    sums = Sums(out_ref, acc, send1, recv1, sent2, got2, sent3, got3, got4, (s1, r1, s2, r2, s3, r3, s4, r4, s5, r5, s6, r6, s7, r7))
    greet_axes()
    greet()
    me, before, after = flags(flip)
    ext[pl.ds(1, ROWS)] = x_ref[...]
    make_slab(ext, 1, send, 0, me, tmp)
    clear_edges(ext, 1)
    clear_edges(exth, 2)
    clear_edges(extp, 1)
    clear_groups(recv)
    clear_groups(recv2)
    greet_wait(AXIS_PEERS)
    start_sides(send, recv, ss, rs)
    start_rows(ext, 1, rss, rrs)
    widen_own(ext, wide1_ref, 1, ROWS)

    def inner_pre(n, carry):
        m = pl.multiple_of(COLS + n * STEP, COLS)
        ing[pl.ds(m, STEP), :] = conv_block(wide1_ref, 1, k1_ref, m, STEP)
        return carry

    lax.fori_loop(0, 3, inner_pre, 0)
    wait_sides_recv(send, recv, ss, rs)
    wait_rows_recv(ext, 1, rss, rrs)
    open_slab(recv, 1, 0, me, rim)
    for edge in (0, ROWS - 1):
        widen_own(ext, wide1_ref, 0 if edge == 0 else ROWS + 1, 1)
        ing[edge * COLS : (edge + 1) * COLS, :] = conv_block(wide1_ref, 1, k1_ref, edge * COLS, COLS)
    side_part(rim, None, k1_ref, ing)

    def act(n, carry):
        m = pl.multiple_of(n * STEP, STEP)
        pre = ing[pl.ds(m, STEP), :]
        s = jax.nn.sigmoid(pre)
        hid = (pre * s).astype(BF16)
        grad = (hg_ref[pl.ds(m, STEP), :] * s * (1.0 + pre * (1.0 - s))).astype(BF16)
        for q in range(STEP // COLS):
            row = n * (STEP // COLS) + q
            exth[2 + row] = hid[q * COLS : (q + 1) * COLS]
            extp[1 + row] = grad[q * COLS : (q + 1) * COLS]
        pg_ref[pl.ds(m, STEP), :] = grad
        return carry

    lax.fori_loop(0, CELLS // STEP, act, 0)
    make_slab(extp, 1, send2, 16, me, tmp)
    make_slab(exth, 2, send2, 0, me, tmp)
    start_sides(send2, recv2, ss2, rs2)
    start_rows(extp, 1, rssp, rrsp)
    start_rows(exth, 2, rssh, rrsh)
    widen_own(extp, widep, 1, ROWS)

    def inner_fold(n, carry):
        m = pl.multiple_of(COLS + n * STEP, COLS)
        ing[pl.ds(m, STEP), :] = g_ref[pl.ds(m, STEP), :].astype(F32) + conv_block(widep, 1, k1t_ref, m, STEP)
        return carry

    lax.fori_loop(0, 3, inner_fold, 0)
    patch_sides(wide1_ref, rim)
    wait_sides_recv(send2, recv2, ss2, rs2)
    wait_rows_recv(extp, 1, rssp, rrsp)
    open_slab(recv2, 1, 16, me, rim)
    split_rim(rim, 1, me, before, after, trim)
    for edge in (0, ROWS - 1):
        widen_own(extp, widep, 0 if edge == 0 else ROWS + 1, 1)
        ing[edge * COLS : (edge + 1) * COLS, :] = g_ref[edge * COLS : (edge + 1) * COLS, :].astype(F32) + conv_block(
            widep, 1, k1t_ref, edge * COLS, COLS
        )
    side_part(rim, trim, k1t_ref, ing)
    for q in range(4):
        part = ing[q * 256 : (q + 1) * 256, :].astype(BF16)
        rounded[q * 16 : (q + 1) * 16] = part.reshape(16, BT, CH)

    for half in (0, 1):

        def pick(q, carry):
            block = rounded[ids[half, q]]
            y, zh, x = lax.div(q, 32), lax.rem(lax.div(q, 16), 2), lax.rem(lax.div(q, 4), 4)
            zl, c = lax.rem(lax.div(q, 2), 2), lax.rem(q, 2)
            b0[half, y, zh, x, zl, c] = block[:, 0:128]
            b0[2 + half, y, zh, x, zl, c] = block[:, 128:256]
            return carry

        lax.fori_loop(0, PAIRS, pick, 0, unroll=4)
        swap.core_start(half)
        swap.core_start(2 + half)

    def hidden_rows():
        wait_rows_recv(exth, 2, rssh, rrsh)
        open_slab(recv2, 2, 0, me, rim2)
        widen(exth, 2, rim2, wide2_ref)

    def kernel_grads(o):
        acc[1, o] = lax.dot_general(
            wide2_ref[o * 2 * COLS : o * 2 * COLS + CELLS, :],
            g_ref[...],
            (((0,), (0,)), ((), ())),
            preferred_element_type=F32,
        )
        acc[0, o] = lax.dot_general(
            wide1_ref[o * COLS : o * COLS + CELLS, :],
            pg_ref[...],
            (((0,), (0,)), ((), ())),
            preferred_element_type=F32,
        )
        sums.start(o)

    def mixed():
        def block(n, carry):
            m = pl.multiple_of(n * STEP, STEP)
            mixed_ref[pl.ds(m, STEP), :] = (
                x_ref[pl.ds(m // COLS, STEP // COLS)].reshape(STEP, CH).astype(F32)
                + conv_block(wide2_ref, 2, k2_ref, m, STEP)
            ).astype(BF16)
            return carry

        lax.fori_loop(0, CELLS // STEP, block, 0)

    def spread_weights():
        w = w_ref[...]
        ps = ps_ref[0:1, :]
        for n in range(SB):
            wexp[n * BL : (n + 1) * BL, :] = w * (ps == n).astype(F32).astype(BF16)

    def source():
        def take(p, carry):
            q = slot[p]
            half, t = lax.div(q, PAIRS), lax.rem(q, PAIRS)
            y, zh, x = lax.div(t, 32), lax.rem(lax.div(t, 16), 2), lax.rem(lax.div(t, 4), 4)
            zl, c = lax.rem(lax.div(t, 2), 2), lax.rem(t, 2)
            at = pl.ds(pl.multiple_of(p * BT, BT), BT)
            rows[at, 0:128] = b4[half, y, zh, x, zl, c]
            rows[at, 128:256] = b4[2 + half, y, zh, x, zl, c]
            return carry

        lax.fori_loop(0, PAIRS, take, 0, unroll=4)
        for m in range(4):
            source_ref[m * 256 : (m + 1) * 256, :] = jnp.dot(
                wexp[m * 256 : (m + 1) * 256, :], rows[...], preferred_element_type=F32
            ).astype(BF16)

    def drained():
        wait_sides_send(send, recv, ss, rs)
        wait_rows_send(ext, 1, rss, rrs)
        wait_sides_send(send2, recv2, ss2, rs2)
        wait_rows_send(exth, 2, rssh, rrsh)
        wait_rows_send(extp, 1, rssp, rrsp)
        swap.drain(0, 1)

    steps = {
        "x": drained, "y": lambda: swap.drain(2),
        "H": hidden_rows, "K": kernel_grads, "M": mixed, "W": spread_weights, "S": source,
        "a": lambda u: swap.advance(0, u), "b": lambda u: swap.advance(1, u),
        "c": lambda u: swap.advance(2, u), "d": lambda u: swap.wait(2, u),
        "2": sums.to_second, "3": sums.to_third, "4": sums.to_fourth,
        "5": sums.to_fifth, "6": sums.to_sixth, "7": sums.to_seventh,
    }
    for word in ORDER:
        if len(word) == 1:
            steps[word]()
        for n in word[1:]:
            steps[word[0]](int(n))
    sums.finish()


def mid(flip, ids, slot, x, hidden_grad, grad, k1, k1t, k2, w_cells, ps_cells):
    dma = pltpu.SemaphoreType.DMA
    three, nine = [dma((3,))] * 2, [dma((3, 3))] * 2
    return pl.pallas_call(
        mid_kernel,
        name="middle",
        out_shape=(
            jax.ShapeDtypeStruct((CELLS, CH), BF16),
            jax.ShapeDtypeStruct((2, 3, PART, CH), BF16),
            jax.ShapeDtypeStruct((SB * BL, CH), BF16),
        ),
        in_specs=[SM, SM, SM] + [VM] * 8,
        out_specs=(VM, VM, VM),
        scratch_shapes=[
            pltpu.VMEM((ROWS + 2, COLS, CH), BF16),
            pltpu.VMEM((ROWS + 4, COLS, CH), BF16),
            pltpu.VMEM((ROWS + 2, COLS, CH), BF16),
            pltpu.VMEM((2, 16, CH), BF16),
            pltpu.VMEM((2, 3, 16, CH), BF16),
            pltpu.VMEM((2, 32, CH), BF16),
            pltpu.VMEM((2, 3, 32, CH), BF16),
            pltpu.VMEM((2, 16, CH), F32),
            pltpu.VMEM((2, 1, 16, CH), F32),
            pltpu.VMEM((2, 2, 16, CH), F32),
            pltpu.VMEM((2, 1, 16, CH), F32),
            pltpu.VMEM(((ROWS + 2) * COLS, 3 * CH), BF16),
            pltpu.VMEM(((ROWS + 4) * COLS, 3 * CH), BF16),
            pltpu.VMEM(((ROWS + 2) * COLS, 3 * CH), BF16),
            pltpu.VMEM((CELLS, CH), BF16),
            pltpu.VMEM((CELLS, CH), F32),
            pltpu.VMEM((BLOCKS, BT, CH), BF16),
            *[pltpu.VMEM(WORLD, BF16)] * 5,
            pltpu.VMEM((PAIRS * BT, CH), BF16),
            pltpu.VMEM((SB * BL, PAIRS * BT), BF16),
            pltpu.VMEM((2, 3, PART, CH), F32),
            pltpu.VMEM((3, PART, CH), BF16),
            pltpu.VMEM((3, PART, CH), BF16),
            pltpu.VMEM((3, PART, CH), BF16),
            pltpu.VMEM((3, 3, 192, CH), BF16),
            pltpu.VMEM((3, 192, CH), BF16),
            pltpu.VMEM((3, 3, 48, CH), BF16),
            pltpu.VMEM((3, 4, 48, CH), BF16),
            dma((2, 3)), dma((2, 3)), dma((2,)), dma((2,)),
            dma((2, 3)), dma((2, 3)), dma((2,)), dma((2,)), dma((2,)), dma((2,)),
            *three, *nine, *nine, *nine, *nine, *nine, *three,
            *swap_sems(),
        ],
        compiler_params=pltpu.CompilerParams(vmem_limit_bytes=42 * 2**20, collective_id=2, has_side_effects=True),
        cost_estimate=pl.CostEstimate(flops=6 * 2**30, bytes_accessed=12 * 2**20, transcendentals=2**18),
    )(flip, ids, slot, x, hidden_grad, grad, k1, k1t, k2, w_cells, ps_cells)


PART = 3 * CH


def axes_of(o):
    return o, (o + 1) % 3, (o + 2) % 3


class Sums:
    def __init__(self, out, acc, send1, recv1, sent2, got2, sent3, got3, got4, sems):
        self.out, self.acc, self.send1, self.recv1 = out, acc, send1, recv1
        self.sent2, self.got2, self.sent3, self.got3, self.got4, self.sems = sent2, got2, sent3, got3, got4, sems
        t, b, tiles, bands = place_in_mesh()
        self.place = spot(t, b)
        self.core = self.place[3]

    def first(self, o):
        s, r = self.sems[0:2]
        return remote(self.send1.at[o], self.recv1.at[o], s.at[o], r.at[o], twin())

    def second(self, o, k):
        s, r = self.sems[2:4]
        a = axes_of(o)[0]
        at = pl.ds(pl.multiple_of(lax.rem(self.place[a] + k, 4) * 192, 64), 192)
        return remote(self.sent2.at[o, at], self.got2.at[o, k - 1], s.at[o, k - 1], r.at[o, k - 1], axis_peer(a, k))

    def third(self, o, k):
        s, r = self.sems[4:6]
        a = axes_of(o)[1]
        at = pl.ds(pl.multiple_of(lax.rem(self.place[a] + k, 4) * 48, 16), 48)
        return remote(self.sent3.at[o, at], self.got3.at[o, k - 1], s.at[o, k - 1], r.at[o, k - 1], axis_peer(a, k))

    def fourth(self, o, k):
        s, r = self.sems[6:8]
        a = axes_of(o)[2]
        mine = self.got4.at[o, self.place[a]]
        return remote(mine, mine, s.at[o, k - 1], r.at[o, k - 1], axis_peer(a, k))

    def rows(self, o, wide):
        a, c, _ = axes_of(o)
        if wide:
            return pl.ds(pl.multiple_of(self.place[a] * 192, 64), 192)
        return pl.ds(pl.multiple_of(self.place[a] * 192 + self.place[c] * 48, 16), 48)

    def fifth(self, o, k):
        s, r = self.sems[8:10]
        rows = self.out.at[self.core, o, self.rows(o, False)]
        return remote(rows, rows, s.at[o, k - 1], r.at[o, k - 1], axis_peer(axes_of(o)[1], k))

    def sixth(self, o, k):
        s, r = self.sems[10:12]
        rows = self.out.at[self.core, o, self.rows(o, True)]
        return remote(rows, rows, s.at[o, k - 1], r.at[o, k - 1], axis_peer(axes_of(o)[0], k))

    def seventh(self, o):
        s, r = self.sems[12:14]
        whole = self.out.at[self.core, o]
        return remote(whole, whole, s.at[o], r.at[o], twin())

    def start(self, o):
        self.send1[o] = self.acc[1 - self.core, o].astype(BF16)
        self.first(o).start()

    def to_second(self, o):
        self.first(o).wait_recv()
        total = self.acc[self.core, o] + self.recv1[o].astype(F32)
        self.acc[self.core, o] = total
        self.sent2[o] = total.astype(BF16)
        for k in (2, 1, 3):
            self.second(o, k).start()

    def to_third(self, o):
        for k in (1, 2, 3):
            self.second(o, k).wait_recv()
        total = self.acc[self.core, o, self.rows(o, True), :]
        for k in (1, 2, 3):
            total = total + self.got2[o, k - 1].astype(F32)
        self.acc[self.core, o, 0:192, :] = total
        self.sent3[o] = total.astype(BF16)
        for k in (2, 1, 3):
            self.third(o, k).start()

    def to_fourth(self, o):
        a, c, e = axes_of(o)
        for k in (1, 2, 3):
            self.third(o, k).wait_recv()
        total = self.acc[self.core, o, pl.ds(pl.multiple_of(self.place[c] * 48, 16), 48), :]
        for k in (1, 2, 3):
            total = total + self.got3[o, k - 1].astype(F32)
        self.got4[o, self.place[e]] = total.astype(BF16)
        for k in (2, 1, 3):
            self.fourth(o, k).start()

    def to_fifth(self, o):
        for k in (1, 2, 3):
            self.fourth(o, k).wait_recv()
        v = [self.got4[o, q].astype(F32) for q in range(4)]
        self.out[self.core, o, self.rows(o, False), :] = (((v[0] + v[1]) + v[2]) + v[3]).astype(BF16)
        for k in (2, 1, 3):
            self.fifth(o, k).start()

    def to_sixth(self, o):
        for k in (1, 2, 3):
            self.fifth(o, k).wait_recv()
        for k in (2, 1, 3):
            self.sixth(o, k).start()

    def to_seventh(self, o):
        for k in (1, 2, 3):
            self.sixth(o, k).wait_recv()
        self.seventh(o).start()

    def finish(self):
        for o in range(3):
            self.first(o).wait_send()
            for k in (1, 2, 3):
                for step in (self.second, self.third, self.fourth, self.fifth, self.sixth):
                    step(o, k).wait_send()
        for o in range(3):
            self.seventh(o).wait()


def finish_kernel(sums, mixed, source, one, two, mixed_out, source_out, wide, sems):
    copies = [
        pltpu.make_async_copy(mixed, mixed_out, sems.at[6]),
        pltpu.make_async_copy(source, source_out, sems.at[7]),
    ]
    for copy in copies:
        copy.start()
    for n, out in ((0, one), (1, two)):
        for i in range(3):
            wide[n, i] = sums[n, i].astype(F32)
            copy = pltpu.make_async_copy(wide.at[n, i], out.at[i], sems.at[n * 3 + i])
            copy.start()
            copies.append(copy)
    for copy in copies:
        copy.wait()


def finish(sums, mixed, source):
    away = pl.BlockSpec(memory_space=pltpu.HBM)
    return pl.pallas_call(
        finish_kernel,
        name="finish",
        out_shape=(
            jax.ShapeDtypeStruct((3, PART, CH), F32),
            jax.ShapeDtypeStruct((3, PART, CH), F32),
            jax.ShapeDtypeStruct((CELLS, CH), BF16),
            jax.ShapeDtypeStruct((SB * BL, CH), BF16),
        ),
        in_specs=[VM] * 3,
        out_specs=(away,) * 4,
        scratch_shapes=[pltpu.VMEM((2, 3, PART, CH), F32), pltpu.SemaphoreType.DMA((8,))],
        compiler_params=params(),
        cost_estimate=pl.CostEstimate(flops=2**20, bytes_accessed=8 * 2**20, transcendentals=0),
    )(sums, mixed, source)


def local(
    source_cells, regrid_weights, pair_target, pair_block, pair_source, flip_codes, kernel_one, kernel_two, out_grad
):
    outgoing, slot = regrid(pair_target[:, 0] * SB + pair_source, regrid_weights, source_cells)
    upstream = out_grad[0]
    hidden_grad, k1_back, arrived, ids, safe_ids, w_cells, ps_cells = back(
        flip_codes,
        pair_target.reshape(1, PAIRS),
        pair_block.reshape(1, PAIRS),
        pair_source.reshape(1, PAIRS),
        regrid_weights,
        upstream,
        kernel_one,
        kernel_two,
        outgoing.reshape(WORLD),
    )
    regridded = gather_sum(ids, arrived.reshape(2, 2 * PAIRS, BT, 128))
    mixed, sums, source_grad = mid(
        flip_codes,
        safe_ids,
        slot,
        regridded.reshape(ROWS, COLS, CH),
        hidden_grad,
        upstream.reshape(CELLS, CH),
        kernel_one.reshape(3, PART, CH),
        k1_back,
        kernel_two.reshape(3, PART, CH),
        w_cells,
        ps_cells,
    )
    one, two, mixed, source_grad = finish(sums, mixed, source_grad)
    return (
        mixed.reshape(1, ROWS, COLS, CH),
        one.reshape(3, 3, CH, CH),
        two.reshape(3, 3, CH, CH),
        source_grad,
    )


def solution(mesh):
    placed = (
        P(("tile", "band"), None),
        P(("tile", "band"), None, None),
        P(("tile", "band"), None),
        P(("tile", "band")),
        P(("tile", "band")),
        P(),
        P(),
        P(),
        P("tile", "band", None, None),
    )
    return jax.shard_map(
        local,
        mesh=mesh,
        in_specs=placed,
        out_specs=(P("tile", "band", None, None), P(), P(), P(("tile", "band"), None)),
        check_vma=False,
    )
```

```python
import jax
import jax.numpy as jnp
from jax import lax
from jax.experimental import pallas as pl
from jax.experimental.pallas import tpu as pltpu
from jax.sharding import PartitionSpec as P

F32 = jnp.float32
BF16 = jnp.bfloat16
MESH = pl.DeviceIdType.MESH
VM = pl.BlockSpec(memory_space=pltpu.VMEM)
SM = pl.BlockSpec(memory_space=pltpu.SMEM)
FAR = pl.BlockSpec(memory_space=pltpu.HBM)
LIMIT = 16 * 2**20
ROWS, COLS, CH = 8, 128, 256
PAIRS, BT, BL, SB, BLOCKS = 128, 16, 64, 16, 64
CELLS = ROWS * COLS


def params(**more):
    return pltpu.CompilerParams(vmem_limit_bytes=LIMIT, **more)


def regrid_kernel(pair_far, w_ref, src_far, out_ref, slot_ref, cnt, masks, wexp, pair, src_ref, sems):
    copies = [
        pltpu.make_async_copy(pair_far, pair, sems.at[0]),
        pltpu.make_async_copy(src_far, src_ref, sems.at[1]),
    ]
    for copy in copies:
        copy.start()
    lane = lax.broadcasted_iota(jnp.int32, (BT, 128), 1)
    masks[0] = (lane < BL).astype(F32).astype(BF16)
    masks[1] = (lane >= BL).astype(F32).astype(BF16)
    wexp[...] = jnp.zeros_like(wexp)

    def clear(i, c):
        cnt[i] = 0
        return c

    lax.fori_loop(0, PAIRS, clear, 0, unroll=8)
    copies[0].wait()

    def place(p, c):
        named = pair[p]
        t = lax.shift_right_logical(named, 4)
        r = cnt[t]
        cnt[t] = r + 1
        slot_ref[p] = jnp.minimum(r, 1) * PAIRS + t
        s = lax.bitwise_and(named, SB - 1)
        w = w_ref[p]
        ww = jnp.concatenate([w, w], axis=1) * masks[lax.rem(s, 2)]
        row = pl.multiple_of(p * BT, BT)
        col = pl.multiple_of((s // 2) * 128, 128)
        wexp[pl.ds(row, BT), pl.ds(col, 128)] = ww
        return c

    lax.fori_loop(0, PAIRS, place, 0, unroll=8)
    copies[1].wait()
    for m in range(4):
        part = jnp.dot(wexp[m * 512 : (m + 1) * 512, :], src_ref[...], preferred_element_type=F32).astype(BF16)
        for q in range(32):
            at = slot_ref[m * 32 + q]
            for h in (0, 1):
                out_ref[h, at] = part[q * BT : (q + 1) * BT, h * 128 : (h + 1) * 128]


def regrid(named, weights, source):
    return pl.pallas_call(
        regrid_kernel,
        name="regrid",
        out_shape=(
            jax.ShapeDtypeStruct((2, 2 * PAIRS, BT, 128), BF16),
            jax.ShapeDtypeStruct((PAIRS,), jnp.int32),
        ),
        in_specs=[FAR, VM, FAR],
        out_specs=(VM, SM),
        scratch_shapes=[
            pltpu.SMEM((PAIRS,), jnp.int32),
            pltpu.VMEM((2, BT, 128), BF16),
            pltpu.VMEM((PAIRS * BT, SB * BL), BF16),
            pltpu.SMEM((PAIRS,), jnp.int32),
            pltpu.VMEM((SB * BL, CH), BF16),
            pltpu.SemaphoreType.DMA((2,)),
        ],
        compiler_params=params(),
        cost_estimate=pl.CostEstimate(flops=2 * 2048 * 1024 * 256, bytes_accessed=6 * 2**20, transcendentals=0),
    )(named, weights, source)


def gather_sum_kernel(ids, got_ref, out_ref, acc, more):
    acc[...] = jnp.zeros_like(acc)
    more[...] = jnp.zeros_like(more)

    def add(q, c):
        k, n = ids[0, q], ids[1, q]
        for h in (0, 1):
            acc[h, k] += got_ref[h, q].astype(F32)
            more[h, n] += got_ref[h, PAIRS + q].astype(F32)
        return c

    lax.fori_loop(0, PAIRS, add, 0, unroll=8)
    for h in (0, 1):
        out_ref[:, :, h * 128 : (h + 1) * 128] = (acc[h, 0:BLOCKS] + more[h, 0:BLOCKS]).astype(BF16)


def gather_sum(ids, arrived):
    return pl.pallas_call(
        gather_sum_kernel,
        name="gather_sum",
        out_shape=jax.ShapeDtypeStruct((BLOCKS, BT, CH), BF16),
        in_specs=[SM, VM],
        out_specs=VM,
        scratch_shapes=[pltpu.VMEM((2, BLOCKS + 1, BT, 128), F32)] * 2,
        compiler_params=params(),
        cost_estimate=pl.CostEstimate(flops=2**21, bytes_accessed=3 * 2**20, transcendentals=0),
    )(ids, arrived)


def place_in_mesh():
    return lax.axis_index("tile"), lax.axis_index("band"), lax.axis_size("tile"), lax.axis_size("band")


def greet():
    t, b, tiles, bands = place_in_mesh()
    barrier = pltpu.get_barrier_semaphore()
    for dt in (1, -1, 0):
        for db in (-1, 0, 1):
            if dt == 0 and db == 0:
                continue

            def say(dt=dt, db=db):
                pl.semaphore_signal(
                    barrier, inc=1, device_id=(lax.rem(t + dt + tiles, tiles), b + db), device_id_type=MESH
                )

            near_band(b, bands, db, say)


def greet_wait(others):
    b, bands = lax.axis_index("band"), lax.axis_size("band")
    near = 2 + jnp.where(b > 0, 3, 0) + jnp.where(b < bands - 1, 3, 0)
    pl.semaphore_wait(pltpu.get_barrier_semaphore(), near + others)


def near_band(b, bands, db, action):
    if db == 0:
        action()
    elif db < 0:
        pl.when(b > 0)(action)
    else:
        pl.when(b < bands - 1)(action)


def side_copy(send, recv, ss, rs, way, db, group):
    t, b, tiles, bands = place_in_mesh()
    to = lax.rem(t + (1 if way == 0 else tiles - 1), tiles)
    return pltpu.make_async_remote_copy(
        src_ref=send.at[way],
        dst_ref=recv.at[way, group],
        send_sem=ss.at[way, 1 + db],
        recv_sem=rs.at[way, group],
        device_id=(to, b + db),
        device_id_type=MESH,
    )


def row_copy(ext, d, ss, rs, db):
    t, b, tiles, bands = place_in_mesh()
    if db < 0:
        src, dst, k = ext.at[pl.ds(d, d)], ext.at[pl.ds(ROWS + d, d)], 0
    else:
        src, dst, k = ext.at[pl.ds(ROWS, d)], ext.at[pl.ds(0, d)], 1
    return pltpu.make_async_remote_copy(
        src_ref=src, dst_ref=dst, send_sem=ss.at[k], recv_sem=rs.at[k], device_id=(t, b + db), device_id_type=MESH
    )


def start_sides(send, recv, ss, rs):
    b, bands = lax.axis_index("band"), lax.axis_size("band")
    for way in (0, 1):
        for db in (0, -1, 1):
            near_band(b, bands, db, lambda way=way, db=db: side_copy(send, recv, ss, rs, way, db, 1 - db).start())


def start_rows(ext, d, ss, rs):
    b, bands = lax.axis_index("band"), lax.axis_size("band")
    for db in (-1, 1):
        near_band(b, bands, db, lambda db=db: row_copy(ext, d, ss, rs, db).start())


def wait_sides_recv(send, recv, ss, rs):
    b, bands = lax.axis_index("band"), lax.axis_size("band")
    for way in (0, 1):
        for db in (0, -1, 1):
            near_band(b, bands, db, lambda way=way, db=db: side_copy(send, recv, ss, rs, way, 0, 1 + db).wait_recv())


def wait_sides_send(send, recv, ss, rs):
    b, bands = lax.axis_index("band"), lax.axis_size("band")
    for way in (0, 1):
        for db in (0, -1, 1):
            near_band(b, bands, db, lambda way=way, db=db: side_copy(send, recv, ss, rs, way, db, 1 - db).wait_send())


def wait_rows_recv(ext, d, ss, rs):
    b, bands = lax.axis_index("band"), lax.axis_size("band")
    near_band(b, bands, -1, lambda: row_copy(ext, d, ss, rs, 1).wait_recv())
    near_band(b, bands, 1, lambda: row_copy(ext, d, ss, rs, -1).wait_recv())


def wait_rows_send(ext, d, ss, rs):
    b, bands = lax.axis_index("band"), lax.axis_size("band")
    for db in (-1, 1):
        near_band(b, bands, db, lambda db=db: row_copy(ext, d, ss, rs, db).wait_send())


def clear_edges(ext, d):
    b, bands = lax.axis_index("band"), lax.axis_size("band")

    @pl.when(b == 0)
    def _():
        ext[0:d] = jnp.zeros((d, COLS, CH), BF16)

    @pl.when(b == bands - 1)
    def _():
        ext[ROWS + d : ROWS + 2 * d] = jnp.zeros((d, COLS, CH), BF16)


def clear_groups(recv):
    b, bands = lax.axis_index("band"), lax.axis_size("band")
    for way in (0, 1):

        @pl.when(b == 0)
        def _():
            recv[way, 0] = jnp.zeros(recv.shape[2:], BF16)

        @pl.when(b == bands - 1)
        def _():
            recv[way, 2] = jnp.zeros(recv.shape[2:], BF16)


def flags(flip):
    t, b, tiles, bands = place_in_mesh()
    me = flip[t]
    before = flip[lax.rem(t + tiles - 1, tiles)]
    after = flip[lax.rem(t + 1, tiles)]
    return me, before, after


def make_slab(ext, d, send, base, flip_me, tmp):
    if d == 1:
        tmp[...] = jnp.zeros_like(tmp)
    for r in range(ROWS):
        first = ext[d + r, 0:16, :].astype(F32)
        last = ext[d + r, COLS - 16 : COLS, :].astype(F32)
        for k in range(d):
            tmp[0, k * 8 + r : k * 8 + r + 1, :] = first[k : k + 1]
            tmp[1, k * 8 + r : k * 8 + r + 1, :] = last[15 - k : 16 - k]
    turned = jnp.full((16, CH), flip_me, jnp.int32) == 1
    left, right = tmp[0], tmp[1]
    send[0, base : base + 16] = jnp.where(turned, left, right).astype(BF16)
    send[1, base : base + 16] = jnp.where(turned, right, left).astype(BF16)


def open_slab(recv, d, base, flip_me, rim):
    turned = jnp.full((16, CH), flip_me, jnp.int32) == 1
    for g in range(3):
        before = recv[0, g, base : base + 16].astype(F32)
        after = recv[1, g, base : base + 16].astype(F32)
        sides = (jnp.where(turned, after, before), jnp.where(turned, before, after))
        for side in (0, 1):
            for k in range(d):
                part = sides[side][k * 8 : k * 8 + 8]
                if g == 0:
                    rim[side, k, 0:d, :] = part[8 - d :]
                elif g == 1:
                    rim[side, k, d : d + 8, :] = part
                else:
                    rim[side, k, d + 8 : 2 * d + 8, :] = part[:d]


def split_rim(rim, d, flip_me, flip_before, flip_after, turned_rim):
    odd_before = (flip_before != flip_me).astype(jnp.int32)
    odd_after = (flip_after != flip_me).astype(jnp.int32)
    odd_left = jnp.where(flip_me == 0, odd_before, odd_after)
    odd_right = jnp.where(flip_me == 0, odd_after, odd_before)
    for side, odd in ((0, odd_left), (1, odd_right)):
        mask = jnp.full((16, CH), odd, jnp.int32) == 1
        for k in range(d):
            whole = rim[side, k]
            turned_rim[side, k] = jnp.where(mask, whole, 0.0)
            rim[side, k] = jnp.where(mask, 0.0, whole)


def widen(ext, d, rim, wide):
    col = lax.broadcasted_iota(jnp.int32, (COLS, CH), 0)

    def one(row, carry):
        mid = ext[row]
        x = mid.astype(F32)
        left = pltpu.roll(x, d, 0)
        right = pltpu.roll(x, COLS - d, 0)
        for k in range(d):
            near = jnp.broadcast_to(rim[0, k, pl.ds(row, 1), :], (COLS, CH))
            left = jnp.where(col == d - 1 - k, near, left)
            near = jnp.broadcast_to(rim[1, k, pl.ds(row, 1), :], (COLS, CH))
            right = jnp.where(col == COLS - d + k, near, right)
        at = pl.ds(pl.multiple_of(row * COLS, COLS), COLS)
        wide[at, 0:CH] = left.astype(BF16)
        wide[at, CH : 2 * CH] = mid
        wide[at, 2 * CH : 3 * CH] = right.astype(BF16)
        return carry

    lax.fori_loop(0, ROWS + 2 * d, one, 0)


def widen_own(ext, wide, first, count):
    col = lax.broadcasted_iota(jnp.int32, (COLS, CH), 0)

    def one(row, carry):
        mid = ext[row]
        x = mid.astype(F32)
        left = jnp.where(col == 0, 0.0, pltpu.roll(x, 1, 0))
        right = jnp.where(col == COLS - 1, 0.0, pltpu.roll(x, COLS - 1, 0))
        at = pl.ds(pl.multiple_of(row * COLS, COLS), COLS)
        wide[at, 0:CH] = left.astype(BF16)
        wide[at, CH : 2 * CH] = mid
        wide[at, 2 * CH : 3 * CH] = right.astype(BF16)
        return carry

    lax.fori_loop(first, first + count, one, 0)


def side_part(rim, turned_rim, taps, out):
    total = None
    none = jnp.zeros((ROWS, CH), F32)
    for i in range(3):
        near = [rim[side, 0, i : i + ROWS, :] for side in (0, 1)]
        turned = [none, none] if turned_rim is None else [turned_rim[side, 0, i : i + ROWS, :] for side in (0, 1)]
        lhs = jnp.concatenate(
            [
                jnp.concatenate([near[0], none, turned[0]], axis=1),
                jnp.concatenate([turned[1], none, near[1]], axis=1),
            ],
            axis=0,
        )
        part = jnp.dot(lhs.astype(BF16), taps[i], preferred_element_type=F32)
        total = part if total is None else total + part
    for r in range(ROWS):
        at = r * COLS
        out[at : at + 1, :] += total[r : r + 1]
        at = r * COLS + COLS - 1
        out[at : at + 1, :] += total[ROWS + r : ROWS + r + 1]


def patch_sides(wide, rim):
    row = lax.broadcasted_iota(jnp.int32, (16, CH), 0)
    for r in range(ROWS + 2):
        at = r * COLS
        tile = wide[at : at + 16, 0:CH].astype(F32)
        near = jnp.broadcast_to(rim[0, 0, r : r + 1, :], (16, CH))
        wide[at : at + 16, 0:CH] = jnp.where(row == 0, near, tile).astype(BF16)
        at = r * COLS + COLS - 16
        tile = wide[at : at + 16, 2 * CH : 3 * CH].astype(F32)
        near = jnp.broadcast_to(rim[1, 0, r : r + 1, :], (16, CH))
        wide[at : at + 16, 2 * CH : 3 * CH] = jnp.where(row == 15, near, tile).astype(BF16)


def conv_block(wide, d, taps, m, rows):
    total = None
    for i in range(3):
        lhs = wide[pl.ds(pl.multiple_of(m + i * d * COLS, COLS), rows), :]
        part = jnp.dot(lhs, taps[i], preferred_element_type=F32)
        total = part if total is None else total + part
    return total


def turned_part(turned_rim, d, taps, out):
    left, right = None, None
    for i in range(3):
        lhs_left = jnp.concatenate([turned_rim[0, d - 1 - c, i * d : i * d + 8, :] for c in range(d)], axis=0)
        lhs_right = jnp.concatenate([turned_rim[1, c, i * d : i * d + 8, :] for c in range(d)], axis=0)
        a = jnp.dot(lhs_left.astype(BF16), taps[i, 2 * CH : 3 * CH, :], preferred_element_type=F32)
        z = jnp.dot(lhs_right.astype(BF16), taps[i, 0:CH, :], preferred_element_type=F32)
        left = a if left is None else left + a
        right = z if right is None else right + z
    for c in range(d):
        for r in range(ROWS):
            at = r * COLS + c
            out[at : at + 1, :] += left[c * 8 + r : c * 8 + r + 1]
            at = r * COLS + COLS - d + c
            out[at : at + 1, :] += right[c * 8 + r : c * 8 + r + 1]


STEP = 256


def spot(t, b):
    x = lax.rem(t, 4)
    y = lax.div(t, 8)
    z = lax.rem(lax.div(t, 4), 2) * 2 + lax.div(b, 2)
    return x, y, z, lax.rem(b, 2)


def device_at(x, y, z, core):
    return (y * 8 + lax.div(z, 2) * 4 + x, lax.rem(z, 2) * 2 + core)


WORLD = (4, 4, 2, 4, 2, 2, BT, 128)
UNITS = [(hs, other) for other in (0, 1) for hs in range(4)]


def axis_peer(axis, k):
    t, b, tiles, bands = place_in_mesh()
    at = list(spot(t, b))
    at[axis] = lax.rem(at[axis] + k, 4)
    return device_at(*at)


def twin():
    t, b, tiles, bands = place_in_mesh()
    return (t, b + 1 - 2 * lax.rem(b, 2))


def greet_axes():
    barrier = pltpu.get_barrier_semaphore()
    pl.semaphore_signal(barrier, inc=1, device_id=twin(), device_id_type=MESH)
    for axis in range(3):
        for k in (1, 2, 3):
            pl.semaphore_signal(barrier, inc=1, device_id=axis_peer(axis, k), device_id_type=MESH)


AXIS_PEERS = 10


def along(ref, unit, axis, v):
    hs, other = UNITS[unit]
    c = lax.rem(lax.axis_index("band") + other, 2)
    if axis == 0:
        return ref.at[hs, :, :, v, :, c]
    if axis == 1:
        return ref.at[hs, v, :, :, :, c]
    return ref.at[hs, :, lax.div(v, 2), :, lax.rem(v, 2), c]


def remote(src, dst, ss, rs, to):
    return pltpu.make_async_remote_copy(
        src_ref=src, dst_ref=dst, send_sem=ss, recv_sem=rs, device_id=to, device_id_type=MESH
    )


class Swap:
    def __init__(self, bufs, sems):
        self.bufs, self.sems = bufs, sems
        t, b, tiles, bands = place_in_mesh()
        self.place = spot(t, b)

    def core_copy(self, hs):
        me = self.place[3]
        src, dst = self.bufs[0], self.bufs[1]
        ss, rs = self.sems[0], self.sems[1]
        return remote(
            src.at[hs, :, :, :, :, 1 - me], dst.at[hs, :, :, :, :, me], ss.at[hs], rs.at[hs], twin()
        )

    def core_start(self, hs):
        self.core_copy(hs).start()

    def source(self, stage, u):
        return self.bufs[0] if stage == 0 and UNITS[u][1] == 0 else self.bufs[1 + stage]

    def hop(self, stage, u, k):
        axis = (u + stage) % 3
        me = self.place[axis]
        src, dst = self.source(stage, u), self.bufs[2 + stage]
        return remote(
            along(src, u, axis, lax.rem(me + k, 4)), along(dst, u, axis, me),
            self.sems[2].at[stage, u, k - 1], self.sems[3].at[stage, u, k - 1], axis_peer(axis, k),
        )

    def own(self, stage, u):
        axis = (u + stage) % 3
        me = self.place[axis]
        src, dst = self.source(stage, u), self.bufs[2 + stage]
        return pltpu.make_async_copy(along(src, u, axis, me), along(dst, u, axis, me), self.sems[4].at[stage, u])

    def start(self, stage, u):
        for k in (2, 1, 3):
            self.hop(stage, u, k).start()
        self.own(stage, u).start()

    def wait(self, stage, u):
        for k in (1, 2, 3):
            self.hop(stage, u, k).wait_recv()
        self.own(stage, u).wait()

    def advance(self, stage, u):
        if stage > 0:
            self.wait(stage - 1, u)
        elif UNITS[u][1] == 1:
            self.core_copy(UNITS[u][0]).wait_recv()
        self.start(stage, u)

    def first_stage(self, units):
        for u in units:
            self.advance(0, u)

    def next_stage(self, stage):
        for u in range(8):
            self.wait(stage - 1, u)
            self.start(stage, u)

    def last_wait(self):
        for u in range(8):
            self.wait(2, u)

    def drain(self, *stages):
        for stage in stages:
            if stage == 0:
                for hs in range(4):
                    self.core_copy(hs).wait_send()
            for u in range(8):
                for k in (1, 2, 3):
                    self.hop(stage, u, k).wait_send()


def swap_sems():
    dma = pltpu.SemaphoreType.DMA
    return [dma((4,)), dma((4,)), dma((3, 8, 3)), dma((3, 8, 3)), dma((3, 8))]


def table_peer(stage, k):
    t, b, tiles, bands = place_in_mesh()
    x, y, z, core = spot(t, b)
    if stage == 0:
        return (t, lax.rem(b + k, 4))
    if stage == 1:
        return (t - x + lax.rem(x + k, 4), b)
    if stage == 2:
        return (t + 4 - 8 * lax.rem(lax.div(t, 4), 2), b)
    return (lax.rem(t + 8 * k, 32), b)


TABLE_PEERS = (3, 3, 1, 3)
TABLE_ROWS = (1, 4, 16, 32)


def table_copy(tab, ss, rs, stage, k):
    t, b, tiles, bands = place_in_mesh()
    n = TABLE_ROWS[stage]
    at = lax.div(t * 4 + b, n) * n
    rows = tab.at[pl.ds(at, n)]
    return pltpu.make_async_remote_copy(
        src_ref=rows, dst_ref=rows, send_sem=ss.at[stage, k - 1], recv_sem=rs.at[stage, k - 1],
        device_id=table_peer(stage, k), device_id_type=MESH,
    )


def table_start(tab, ss, rs, stage):
    for k in range(1, TABLE_PEERS[stage] + 1):
        table_copy(tab, ss, rs, stage, k).start()


def table_wait(tab, ss, rs, stage):
    for k in range(1, TABLE_PEERS[stage] + 1):
        table_copy(tab, ss, rs, stage, k).wait()


def greet_table():
    barrier = pltpu.get_barrier_semaphore()
    for stage in range(4):
        for k in range(1, TABLE_PEERS[stage] + 1):
            pl.semaphore_signal(barrier, inc=1, device_id=table_peer(stage, k), device_id_type=MESH)


def back_kernel(
    flip, tgt_ref, blk_ref, src_row, w_ref, g_ref, k1_ref, k2_ref, outgoing,
    hg_ref, k1t_ref, arrived, ids_ref, safe_ref, w_cells, ps_cells,
    tab, ext, send, recv, tmp, rim, trim, wide, k2t, b1, b2, b3, ss, rs, rss, rrs, tss, trs, *sems,
):
    d = 2
    swap = Swap((outgoing, b1, b2, b3, arrived), sems)
    greet_table()
    greet_axes()
    greet()
    t, b, tiles, bands = place_in_mesh()
    tab[t * 4 + b] = tgt_ref[...] * BLOCKS + blk_ref[...]
    me, before, after = flags(flip)
    ext[pl.ds(d, ROWS)] = g_ref[...]
    make_slab(ext, d, send, 0, me, tmp)
    clear_edges(ext, d)
    clear_groups(recv)
    greet_wait(sum(TABLE_PEERS) + AXIS_PEERS)
    table_start(tab, tss, trs, 0)
    start_sides(send, recv, ss, rs)
    start_rows(ext, d, rss, rrs)
    for hs in range(4):
        swap.core_start(hs)
    swap.first_stage(range(0, 4))
    table_wait(tab, tss, trs, 0)
    table_start(tab, tss, trs, 1)
    swap.first_stage(range(4, 8))
    for i in range(3):
        for j in range(3):
            k2t[i, j * CH : (j + 1) * CH, :] = k2_ref[2 - i, 2 - j].T
    wait_sides_recv(send, recv, ss, rs)
    wait_rows_recv(ext, d, rss, rrs)
    open_slab(recv, d, 0, me, rim)
    split_rim(rim, d, me, before, after, trim)
    table_wait(tab, tss, trs, 1)
    table_start(tab, tss, trs, 2)
    swap.next_stage(1)
    widen(ext, d, rim, wide)

    def block(n, carry):
        m = pl.multiple_of(n * STEP, STEP)
        hg_ref[pl.ds(m, STEP), :] = conv_block(wide, d, k2t, m, STEP)
        return carry

    lax.fori_loop(0, CELLS // STEP, block, 0)
    table_wait(tab, tss, trs, 2)
    table_start(tab, tss, trs, 3)
    swap.next_stage(2)
    turned_part(trim, d, k2t, hg_ref)
    for i in range(3):
        for j in range(3):
            k1t_ref[i, j * CH : (j + 1) * CH, :] = k1_ref[2 - i, 2 - j].T
    for n in range(SB):
        part = w_ref[n * 8 : (n + 1) * 8].reshape(128, BL).astype(F32)
        part = jnp.concatenate([part, part], axis=1).T
        w_cells[:, n * 128 : (n + 1) * 128] = part[0:BL].astype(BF16)
    spread = (
        lax.broadcasted_iota(jnp.int32, (PAIRS, PAIRS * BT), 1) // BT
        == lax.broadcasted_iota(jnp.int32, (PAIRS, PAIRS * BT), 0)
    ).astype(F32)
    own = jnp.broadcast_to(src_row[...], (8, PAIRS)).astype(F32)
    ps_cells[...] = jnp.dot(own.astype(BF16), spread.astype(BF16), preferred_element_type=F32)
    table_wait(tab, tss, trs, 3)
    table = tab[...].reshape(PAIRS, PAIRS).T
    order = lax.broadcasted_iota(jnp.int32, (PAIRS, PAIRS), 0)
    block_of = lax.bitwise_and(table, BLOCKS - 1)
    mine = lax.shift_right_logical(table, 6) == t * 4 + b
    first = jnp.min(jnp.where(mine, order, PAIRS), axis=0, keepdims=True)
    last = jnp.max(jnp.where(mine, order, -1), axis=0, keepdims=True)
    id_first = jnp.sum(jnp.where(order == first, block_of, 0), axis=0, keepdims=True)
    id_last = jnp.sum(jnp.where(order == last, block_of, 0), axis=0, keepdims=True)
    ids_ref[0:1, :] = jnp.where(first < PAIRS, id_first, BLOCKS)
    ids_ref[1:2, :] = jnp.where(last > first, id_last, BLOCKS)
    safe_ref[0:1, :] = id_first
    safe_ref[1:2, :] = id_last
    wait_sides_send(send, recv, ss, rs)
    wait_rows_send(ext, d, rss, rrs)
    swap.drain(0, 1)
    swap.last_wait()
    swap.drain(2)


def back(flip, target, block, source, weights, grad, k1, k2, outgoing):
    d = 2
    return pl.pallas_call(
        back_kernel,
        name="hidden_adjoint",
        out_shape=(
            jax.ShapeDtypeStruct((CELLS, CH), F32),
            jax.ShapeDtypeStruct((3, 3 * CH, CH), BF16),
            jax.ShapeDtypeStruct(WORLD, BF16),
            jax.ShapeDtypeStruct((2, PAIRS), jnp.int32),
            jax.ShapeDtypeStruct((2, PAIRS), jnp.int32),
            jax.ShapeDtypeStruct((BL, PAIRS * BT), BF16),
            jax.ShapeDtypeStruct((8, PAIRS * BT), F32),
        ),
        in_specs=[SM] + [VM] * 8,
        out_specs=(VM,) * 7,
        scratch_shapes=[
            pltpu.VMEM((PAIRS, 1, PAIRS), jnp.int32),
            pltpu.VMEM((ROWS + 2 * d, COLS, CH), BF16),
            pltpu.VMEM((2, 16, CH), BF16),
            pltpu.VMEM((2, 3, 16, CH), BF16),
            pltpu.VMEM((2, 16, CH), F32),
            pltpu.VMEM((2, d, 16, CH), F32),
            pltpu.VMEM((2, d, 16, CH), F32),
            pltpu.VMEM(((ROWS + 2 * d) * COLS, 3 * CH), BF16),
            pltpu.VMEM((3, 3 * CH, CH), BF16),
            pltpu.VMEM(WORLD, BF16),
            pltpu.VMEM(WORLD, BF16),
            pltpu.VMEM(WORLD, BF16),
            pltpu.SemaphoreType.DMA((2, 3)),
            pltpu.SemaphoreType.DMA((2, 3)),
            pltpu.SemaphoreType.DMA((2,)),
            pltpu.SemaphoreType.DMA((2,)),
            pltpu.SemaphoreType.DMA((4, 3)),
            pltpu.SemaphoreType.DMA((4, 3)),
            *swap_sems(),
        ],
        compiler_params=pltpu.CompilerParams(vmem_limit_bytes=18 * 2**20, collective_id=1, has_side_effects=True),
        cost_estimate=pl.CostEstimate(flops=6 * 2**30, bytes_accessed=8 * 2**20, transcendentals=0),
    )(flip, target, block, source, weights, grad, k1, k2, outgoing)


ORDER = (
    "a0123",
    "H",
    "K0",
    "a45",
    "K1",
    "20",
    "K2",
    "21",
    "a67",
    "22",
    "b012",
    "30",
    "b345",
    "M",
    "b67",
    "31",
    "32",
    "W",
    "c012",
    "4012",
    "c345",
    "5012",
    "c67",
    "6012",
    "x",
    "d01234567",
    "S",
    "7012",
    "y",
)


def mid_kernel(
    flip, ids, slot, x_ref, hg_ref, g_ref, k1_ref, k1t_ref, k2_ref, w_ref, ps_ref,
    mixed_ref, out_ref, source_ref,
    ext, exth, extp, send, recv, send2, recv2, tmp, rim, rim2, trim, wide1_ref, wide2_ref, widep, pg_ref, ing, rounded,
    b0, b1, b2, b3, b4, rows, wexp,
    acc, send1, recv1, sent2, got2, sent3, got3, got4,
    ss, rs, rss, rrs, ss2, rs2, rssh, rrsh, rssp, rrsp,
    s1, r1, s2, r2, s3, r3, s4, r4, s5, r5, s6, r6, s7, r7, *sems,
):
    swap = Swap((b0, b1, b2, b3, b4), sems)
    sums = Sums(out_ref, acc, send1, recv1, sent2, got2, sent3, got3, got4, (s1, r1, s2, r2, s3, r3, s4, r4, s5, r5, s6, r6, s7, r7))
    greet_axes()
    greet()
    me, before, after = flags(flip)
    ext[pl.ds(1, ROWS)] = x_ref[...]
    make_slab(ext, 1, send, 0, me, tmp)
    clear_edges(ext, 1)
    clear_edges(exth, 2)
    clear_edges(extp, 1)
    clear_groups(recv)
    clear_groups(recv2)
    greet_wait(AXIS_PEERS)
    start_sides(send, recv, ss, rs)
    start_rows(ext, 1, rss, rrs)
    widen_own(ext, wide1_ref, 1, ROWS)

    def inner_pre(n, carry):
        m = pl.multiple_of(COLS + n * STEP, COLS)
        ing[pl.ds(m, STEP), :] = conv_block(wide1_ref, 1, k1_ref, m, STEP)
        return carry

    lax.fori_loop(0, 3, inner_pre, 0)
    wait_sides_recv(send, recv, ss, rs)
    wait_rows_recv(ext, 1, rss, rrs)
    open_slab(recv, 1, 0, me, rim)
    for edge in (0, ROWS - 1):
        widen_own(ext, wide1_ref, 0 if edge == 0 else ROWS + 1, 1)
        ing[edge * COLS : (edge + 1) * COLS, :] = conv_block(wide1_ref, 1, k1_ref, edge * COLS, COLS)
    side_part(rim, None, k1_ref, ing)

    def act(n, carry):
        m = pl.multiple_of(n * STEP, STEP)
        pre = ing[pl.ds(m, STEP), :]
        s = jax.nn.sigmoid(pre)
        hid = (pre * s).astype(BF16)
        grad = (hg_ref[pl.ds(m, STEP), :] * s * (1.0 + pre * (1.0 - s))).astype(BF16)
        for q in range(STEP // COLS):
            row = n * (STEP // COLS) + q
            exth[2 + row] = hid[q * COLS : (q + 1) * COLS]
            extp[1 + row] = grad[q * COLS : (q + 1) * COLS]
        pg_ref[pl.ds(m, STEP), :] = grad
        return carry

    lax.fori_loop(0, CELLS // STEP, act, 0)
    make_slab(extp, 1, send2, 16, me, tmp)
    make_slab(exth, 2, send2, 0, me, tmp)
    start_sides(send2, recv2, ss2, rs2)
    start_rows(extp, 1, rssp, rrsp)
    start_rows(exth, 2, rssh, rrsh)
    widen_own(extp, widep, 1, ROWS)

    def inner_fold(n, carry):
        m = pl.multiple_of(COLS + n * STEP, COLS)
        ing[pl.ds(m, STEP), :] = g_ref[pl.ds(m, STEP), :].astype(F32) + conv_block(widep, 1, k1t_ref, m, STEP)
        return carry

    lax.fori_loop(0, 3, inner_fold, 0)
    patch_sides(wide1_ref, rim)
    wait_sides_recv(send2, recv2, ss2, rs2)
    wait_rows_recv(extp, 1, rssp, rrsp)
    open_slab(recv2, 1, 16, me, rim)
    split_rim(rim, 1, me, before, after, trim)
    for edge in (0, ROWS - 1):
        widen_own(extp, widep, 0 if edge == 0 else ROWS + 1, 1)
        ing[edge * COLS : (edge + 1) * COLS, :] = g_ref[edge * COLS : (edge + 1) * COLS, :].astype(F32) + conv_block(
            widep, 1, k1t_ref, edge * COLS, COLS
        )
    side_part(rim, trim, k1t_ref, ing)
    for q in range(4):
        part = ing[q * 256 : (q + 1) * 256, :].astype(BF16)
        rounded[q * 16 : (q + 1) * 16] = part.reshape(16, BT, CH)

    for half in (0, 1):

        def pick(q, carry):
            block = rounded[ids[half, q]]
            y, zh, x = lax.div(q, 32), lax.rem(lax.div(q, 16), 2), lax.rem(lax.div(q, 4), 4)
            zl, c = lax.rem(lax.div(q, 2), 2), lax.rem(q, 2)
            b0[half, y, zh, x, zl, c] = block[:, 0:128]
            b0[2 + half, y, zh, x, zl, c] = block[:, 128:256]
            return carry

        lax.fori_loop(0, PAIRS, pick, 0, unroll=16)
        swap.core_start(half)
        swap.core_start(2 + half)

    def hidden_rows():
        wait_rows_recv(exth, 2, rssh, rrsh)
        open_slab(recv2, 2, 0, me, rim2)
        widen(exth, 2, rim2, wide2_ref)

    def kernel_grads(o):
        acc[1, o] = lax.dot_general(
            wide2_ref[o * 2 * COLS : o * 2 * COLS + CELLS, :],
            g_ref[...],
            (((0,), (0,)), ((), ())),
            preferred_element_type=F32,
        )
        acc[0, o] = lax.dot_general(
            wide1_ref[o * COLS : o * COLS + CELLS, :],
            pg_ref[...],
            (((0,), (0,)), ((), ())),
            preferred_element_type=F32,
        )
        sums.start(o)

    def mixed():
        def block(n, carry):
            m = pl.multiple_of(n * STEP, STEP)
            mixed_ref[pl.ds(m, STEP), :] = (
                x_ref[pl.ds(m // COLS, STEP // COLS)].reshape(STEP, CH).astype(F32)
                + conv_block(wide2_ref, 2, k2_ref, m, STEP)
            ).astype(BF16)
            return carry

        lax.fori_loop(0, CELLS // STEP, block, 0)

    def spread_weights():
        w = w_ref[...]
        ps = ps_ref[0:1, :]
        for n in range(SB):
            wexp[n * BL : (n + 1) * BL, :] = w * (ps == n).astype(F32).astype(BF16)

    def source():
        def take(p, carry):
            q = slot[p]
            half, t = lax.div(q, PAIRS), lax.rem(q, PAIRS)
            y, zh, x = lax.div(t, 32), lax.rem(lax.div(t, 16), 2), lax.rem(lax.div(t, 4), 4)
            zl, c = lax.rem(lax.div(t, 2), 2), lax.rem(t, 2)
            at = pl.ds(pl.multiple_of(p * BT, BT), BT)
            rows[at, 0:128] = b4[half, y, zh, x, zl, c]
            rows[at, 128:256] = b4[2 + half, y, zh, x, zl, c]
            return carry

        lax.fori_loop(0, PAIRS, take, 0, unroll=16)
        for m in range(4):
            source_ref[m * 256 : (m + 1) * 256, :] = jnp.dot(
                wexp[m * 256 : (m + 1) * 256, :], rows[...], preferred_element_type=F32
            ).astype(BF16)

    def drained():
        wait_sides_send(send, recv, ss, rs)
        wait_rows_send(ext, 1, rss, rrs)
        wait_sides_send(send2, recv2, ss2, rs2)
        wait_rows_send(exth, 2, rssh, rrsh)
        wait_rows_send(extp, 1, rssp, rrsp)
        swap.drain(0, 1)

    steps = {
        "x": drained, "y": lambda: swap.drain(2),
        "H": hidden_rows, "K": kernel_grads, "M": mixed, "W": spread_weights, "S": source,
        "a": lambda u: swap.advance(0, u), "b": lambda u: swap.advance(1, u),
        "c": lambda u: swap.advance(2, u), "d": lambda u: swap.wait(2, u),
        "2": sums.to_second, "3": sums.to_third, "4": sums.to_fourth,
        "5": sums.to_fifth, "6": sums.to_sixth, "7": sums.to_seventh,
    }
    for word in ORDER:
        if len(word) == 1:
            steps[word]()
        for n in word[1:]:
            steps[word[0]](int(n))
    sums.finish()


def mid(flip, ids, slot, x, hidden_grad, grad, k1, k1t, k2, w_cells, ps_cells):
    dma = pltpu.SemaphoreType.DMA
    three, nine = [dma((3,))] * 2, [dma((3, 3))] * 2
    return pl.pallas_call(
        mid_kernel,
        name="middle",
        out_shape=(
            jax.ShapeDtypeStruct((CELLS, CH), BF16),
            jax.ShapeDtypeStruct((2, 3, PART, CH), BF16),
            jax.ShapeDtypeStruct((SB * BL, CH), BF16),
        ),
        in_specs=[SM, SM, SM] + [VM] * 8,
        out_specs=(VM, VM, VM),
        scratch_shapes=[
            pltpu.VMEM((ROWS + 2, COLS, CH), BF16),
            pltpu.VMEM((ROWS + 4, COLS, CH), BF16),
            pltpu.VMEM((ROWS + 2, COLS, CH), BF16),
            pltpu.VMEM((2, 16, CH), BF16),
            pltpu.VMEM((2, 3, 16, CH), BF16),
            pltpu.VMEM((2, 32, CH), BF16),
            pltpu.VMEM((2, 3, 32, CH), BF16),
            pltpu.VMEM((2, 16, CH), F32),
            pltpu.VMEM((2, 1, 16, CH), F32),
            pltpu.VMEM((2, 2, 16, CH), F32),
            pltpu.VMEM((2, 1, 16, CH), F32),
            pltpu.VMEM(((ROWS + 2) * COLS, 3 * CH), BF16),
            pltpu.VMEM(((ROWS + 4) * COLS, 3 * CH), BF16),
            pltpu.VMEM(((ROWS + 2) * COLS, 3 * CH), BF16),
            pltpu.VMEM((CELLS, CH), BF16),
            pltpu.VMEM((CELLS, CH), F32),
            pltpu.VMEM((BLOCKS, BT, CH), BF16),
            *[pltpu.VMEM(WORLD, BF16)] * 5,
            pltpu.VMEM((PAIRS * BT, CH), BF16),
            pltpu.VMEM((SB * BL, PAIRS * BT), BF16),
            pltpu.VMEM((2, 3, PART, CH), F32),
            pltpu.VMEM((3, PART, CH), BF16),
            pltpu.VMEM((3, PART, CH), BF16),
            pltpu.VMEM((3, PART, CH), BF16),
            pltpu.VMEM((3, 3, 192, CH), BF16),
            pltpu.VMEM((3, 192, CH), BF16),
            pltpu.VMEM((3, 3, 48, CH), BF16),
            pltpu.VMEM((3, 4, 48, CH), BF16),
            dma((2, 3)), dma((2, 3)), dma((2,)), dma((2,)),
            dma((2, 3)), dma((2, 3)), dma((2,)), dma((2,)), dma((2,)), dma((2,)),
            *three, *nine, *nine, *nine, *nine, *nine, *three,
            *swap_sems(),
        ],
        compiler_params=pltpu.CompilerParams(vmem_limit_bytes=42 * 2**20, collective_id=2, has_side_effects=True),
        cost_estimate=pl.CostEstimate(flops=6 * 2**30, bytes_accessed=12 * 2**20, transcendentals=2**18),
    )(flip, ids, slot, x, hidden_grad, grad, k1, k1t, k2, w_cells, ps_cells)


PART = 3 * CH


def axes_of(o):
    return o, (o + 1) % 3, (o + 2) % 3


class Sums:
    def __init__(self, out, acc, send1, recv1, sent2, got2, sent3, got3, got4, sems):
        self.out, self.acc, self.send1, self.recv1 = out, acc, send1, recv1
        self.sent2, self.got2, self.sent3, self.got3, self.got4, self.sems = sent2, got2, sent3, got3, got4, sems
        t, b, tiles, bands = place_in_mesh()
        self.place = spot(t, b)
        self.core = self.place[3]

    def first(self, o):
        s, r = self.sems[0:2]
        return remote(self.send1.at[o], self.recv1.at[o], s.at[o], r.at[o], twin())

    def second(self, o, k):
        s, r = self.sems[2:4]
        a = axes_of(o)[0]
        at = pl.ds(pl.multiple_of(lax.rem(self.place[a] + k, 4) * 192, 64), 192)
        return remote(self.sent2.at[o, at], self.got2.at[o, k - 1], s.at[o, k - 1], r.at[o, k - 1], axis_peer(a, k))

    def third(self, o, k):
        s, r = self.sems[4:6]
        a = axes_of(o)[1]
        at = pl.ds(pl.multiple_of(lax.rem(self.place[a] + k, 4) * 48, 16), 48)
        return remote(self.sent3.at[o, at], self.got3.at[o, k - 1], s.at[o, k - 1], r.at[o, k - 1], axis_peer(a, k))

    def fourth(self, o, k):
        s, r = self.sems[6:8]
        a = axes_of(o)[2]
        mine = self.got4.at[o, self.place[a]]
        return remote(mine, mine, s.at[o, k - 1], r.at[o, k - 1], axis_peer(a, k))

    def rows(self, o, wide):
        a, c, _ = axes_of(o)
        if wide:
            return pl.ds(pl.multiple_of(self.place[a] * 192, 64), 192)
        return pl.ds(pl.multiple_of(self.place[a] * 192 + self.place[c] * 48, 16), 48)

    def fifth(self, o, k):
        s, r = self.sems[8:10]
        rows = self.out.at[self.core, o, self.rows(o, False)]
        return remote(rows, rows, s.at[o, k - 1], r.at[o, k - 1], axis_peer(axes_of(o)[1], k))

    def sixth(self, o, k):
        s, r = self.sems[10:12]
        rows = self.out.at[self.core, o, self.rows(o, True)]
        return remote(rows, rows, s.at[o, k - 1], r.at[o, k - 1], axis_peer(axes_of(o)[0], k))

    def seventh(self, o):
        s, r = self.sems[12:14]
        whole = self.out.at[self.core, o]
        return remote(whole, whole, s.at[o], r.at[o], twin())

    def start(self, o):
        self.send1[o] = self.acc[1 - self.core, o].astype(BF16)
        self.first(o).start()

    def to_second(self, o):
        self.first(o).wait_recv()
        total = self.acc[self.core, o] + self.recv1[o].astype(F32)
        self.acc[self.core, o] = total
        self.sent2[o] = total.astype(BF16)
        for k in (2, 1, 3):
            self.second(o, k).start()

    def to_third(self, o):
        for k in (1, 2, 3):
            self.second(o, k).wait_recv()
        total = self.acc[self.core, o, self.rows(o, True), :]
        for k in (1, 2, 3):
            total = total + self.got2[o, k - 1].astype(F32)
        self.acc[self.core, o, 0:192, :] = total
        self.sent3[o] = total.astype(BF16)
        for k in (2, 1, 3):
            self.third(o, k).start()

    def to_fourth(self, o):
        a, c, e = axes_of(o)
        for k in (1, 2, 3):
            self.third(o, k).wait_recv()
        total = self.acc[self.core, o, pl.ds(pl.multiple_of(self.place[c] * 48, 16), 48), :]
        for k in (1, 2, 3):
            total = total + self.got3[o, k - 1].astype(F32)
        self.got4[o, self.place[e]] = total.astype(BF16)
        for k in (2, 1, 3):
            self.fourth(o, k).start()

    def to_fifth(self, o):
        for k in (1, 2, 3):
            self.fourth(o, k).wait_recv()
        v = [self.got4[o, q].astype(F32) for q in range(4)]
        self.out[self.core, o, self.rows(o, False), :] = (((v[0] + v[1]) + v[2]) + v[3]).astype(BF16)
        for k in (2, 1, 3):
            self.fifth(o, k).start()

    def to_sixth(self, o):
        for k in (1, 2, 3):
            self.fifth(o, k).wait_recv()
        for k in (2, 1, 3):
            self.sixth(o, k).start()

    def to_seventh(self, o):
        for k in (1, 2, 3):
            self.sixth(o, k).wait_recv()
        self.seventh(o).start()

    def finish(self):
        for o in range(3):
            self.first(o).wait_send()
            for k in (1, 2, 3):
                for step in (self.second, self.third, self.fourth, self.fifth, self.sixth):
                    step(o, k).wait_send()
        for o in range(3):
            self.seventh(o).wait()


def finish_kernel(sums, mixed, source, one, two, mixed_out, source_out, wide, sems):
    copies = [
        pltpu.make_async_copy(mixed, mixed_out, sems.at[6]),
        pltpu.make_async_copy(source, source_out, sems.at[7]),
    ]
    for copy in copies:
        copy.start()
    for n, out in ((0, one), (1, two)):
        for i in range(3):
            wide[n, i] = sums[n, i].astype(F32)
            copy = pltpu.make_async_copy(wide.at[n, i], out.at[i], sems.at[n * 3 + i])
            copy.start()
            copies.append(copy)
    for copy in copies:
        copy.wait()


def finish(sums, mixed, source):
    away = pl.BlockSpec(memory_space=pltpu.HBM)
    return pl.pallas_call(
        finish_kernel,
        name="finish",
        out_shape=(
            jax.ShapeDtypeStruct((3, PART, CH), F32),
            jax.ShapeDtypeStruct((3, PART, CH), F32),
            jax.ShapeDtypeStruct((CELLS, CH), BF16),
            jax.ShapeDtypeStruct((SB * BL, CH), BF16),
        ),
        in_specs=[VM] * 3,
        out_specs=(away,) * 4,
        scratch_shapes=[pltpu.VMEM((2, 3, PART, CH), F32), pltpu.SemaphoreType.DMA((8,))],
        compiler_params=params(),
        cost_estimate=pl.CostEstimate(flops=2**20, bytes_accessed=8 * 2**20, transcendentals=0),
    )(sums, mixed, source)


def local(
    source_cells, regrid_weights, pair_target, pair_block, pair_source, flip_codes, kernel_one, kernel_two, out_grad
):
    outgoing, slot = regrid(pair_target[:, 0] * SB + pair_source, regrid_weights, source_cells)
    upstream = out_grad[0]
    hidden_grad, k1_back, arrived, ids, safe_ids, w_cells, ps_cells = back(
        flip_codes,
        pair_target.reshape(1, PAIRS),
        pair_block.reshape(1, PAIRS),
        pair_source.reshape(1, PAIRS),
        regrid_weights,
        upstream,
        kernel_one,
        kernel_two,
        outgoing.reshape(WORLD),
    )
    regridded = gather_sum(ids, arrived.reshape(2, 2 * PAIRS, BT, 128))
    mixed, sums, source_grad = mid(
        flip_codes,
        safe_ids,
        slot,
        regridded.reshape(ROWS, COLS, CH),
        hidden_grad,
        upstream.reshape(CELLS, CH),
        kernel_one.reshape(3, PART, CH),
        k1_back,
        kernel_two.reshape(3, PART, CH),
        w_cells,
        ps_cells,
    )
    one, two, mixed, source_grad = finish(sums, mixed, source_grad)
    return (
        mixed.reshape(1, ROWS, COLS, CH),
        one.reshape(3, 3, CH, CH),
        two.reshape(3, 3, CH, CH),
        source_grad,
    )


def solution(mesh):
    placed = (
        P(("tile", "band"), None),
        P(("tile", "band"), None, None),
        P(("tile", "band"), None),
        P(("tile", "band")),
        P(("tile", "band")),
        P(),
        P(),
        P(),
        P("tile", "band", None, None),
    )
    return jax.shard_map(
        local,
        mesh=mesh,
        in_specs=placed,
        out_specs=(P("tile", "band", None, None), P(), P(), P(("tile", "band"), None)),
        check_vma=False,
    )
```
